32 devices in a mesh: wl: 4 (over y, x), cell: 8 (over z, core).
Axes of the slice: x: 2, y: 2, z: 4, core: 2. Of those that a mesh axis runs over, the one named last changes fastest.
Arguments:
- interfaces: float32 [8, 3, 2, 128, 128], replicated, may hold values from -0.10606602 to 1.006066
- cell_profile: int32 [64], P('cell'), may hold values from 0 to 3
- cell_section: int32 [64], P('cell'), may hold values from 0 to 7
- mode_loss: float32 [4, 128], replicated, may hold values from 0.985 to 1
- phase: float32 [4, 4, 128], P(None, 'wl'), may hold values from -3.140625 to 3.140625
- mode_field: float32 [4, 128, 4096], P(None, None, 'wl'), may hold values from -0.5 to 0.5
- target: float32 [4, 2, 128, 128], P('wl'), may hold values from -0.5 to 0.5
Outputs:
- reflection: float32 [4, 2, 128, 128], P('wl', None, 'cell')
- gradient: float32 [64, 4096], P('cell', 'wl')
The draws below stay inside these ranges and needn't reach their ends.
All inputs are finite; a program needn't handle non-finite values.
Results may differ from the reference program's by a relative error of at most 0.0003.
Values sent between devices are 32-bit elements; how exact they have to be, the bound alone decides.
No kernel may reach another device: no remote copies, remote signals or barrier semaphores. Data moves between devices by JAX's collectives and lax.ppermute only.
A program may use at most 128 MiB of HBM per device.

```python
import math
import jax
import jax.numpy as jnp
from jax import lax

MODES = 128
PIXELS = 4096
PROFILES = 4
SECTIONS = 8
CELLS = 64
WAVES = 4


def draw_interfaces(key, part):
    full_shape = (SECTIONS, 3, 2, MODES, MODES)
    unit_matrix = jnp.eye(MODES, dtype=jnp.float32)
    random_part = jnp.clip(jax.random.normal(key, full_shape, jnp.float32), -4.0, 4.0)
    spread_value = 0.3
    center = 0.9
    kind_scale = jnp.array([0.7, 1.0, 1.0], jnp.float32) * (spread_value / MODES ** 0.5)
    values = random_part * kind_scale[None, :, None, None, None]
    kind_mask = jnp.array([0.0, 1.0, 1.0], jnp.float32)[None, :, None, None, None]
    part_mask = jnp.array([1.0, 0.0], jnp.float32)[None, None, :, None, None]
    return values + kind_mask * part_mask * center * unit_matrix


def plant(drawn, own_key, smallest, top_value):
    longest = drawn.shape.index(max(drawn.shape))
    spots = []
    for shift in (0, 1):
        where = [jax.random.randint(jax.random.fold_in(own_key, axis), (), 0, length) for axis, length in enumerate(drawn.shape)]
        where[longest] = (where[longest] + shift) % drawn.shape[longest]
        spots.append(tuple(where))
    return drawn.at[spots[0]].set(smallest).at[spots[1]].set(top_value)


def block_scale(key, shape, shards, low, top_value):
    def one(axis_at, blocks):
        heights = jax.random.uniform(jax.random.fold_in(jax.random.fold_in(key, 6), axis_at), (blocks,), jnp.float32, low / len(shards), top_value / len(shards))
        return jnp.repeat(jnp.exp(heights), shape[axis_at] // blocks).reshape((-1,) + (1,) * (len(shape) - axis_at - 1))

    level = one(*shards[0])
    for cut in shards[1:]:
        level = level * one(*cut)
    return level


def normal_values(rng, dims, width, reach, shards=(), kind=jnp.bfloat16):
    entries = width * jax.random.normal(rng, dims, jnp.float32)
    if shards:
        entries = entries * block_scale(rng, dims, shards, -0.22, 0.18)
    return jnp.clip(entries, -reach, reach).astype(kind)


def setup_inputs(seed: int = 0) -> dict:
    streams_of = jax.random.split(jax.random.key(seed), 8)
    return {
        "interfaces": draw_interfaces(jax.random.fold_in(streams_of[7], 71), 0),
        "cell_profile": plant(jax.random.randint(streams_of[1], (CELLS,), 0, PROFILES), jax.random.fold_in(streams_of[1], 1), 0, PROFILES - 1).astype(jnp.int32),
        "cell_section": plant(jax.random.randint(streams_of[2], (CELLS,), 0, SECTIONS), jax.random.fold_in(streams_of[2], 1), 0, SECTIONS - 1).astype(jnp.int32),
        "mode_loss": jnp.clip(jnp.exp(jax.random.uniform(streams_of[3], (PROFILES, MODES), jnp.float32, math.log(0.985), math.log(1.0))), 0.985, 1.0),
        "phase": jnp.clip(jax.random.uniform(streams_of[4], (PROFILES, WAVES, MODES), jnp.float32, -3.140625, 3.140625), -3.140625, 3.140625),
        "mode_field": normal_values(streams_of[5], (PROFILES, MODES, PIXELS), MODES ** -0.5, 0.5, ((2, 4),), jnp.float32),
        "target": normal_values(streams_of[6], (WAVES, 2, MODES, MODES), MODES ** -0.5, 0.5, ((0, 4),), jnp.float32),
    }


def matmul_highest(first, second):
    return jnp.matmul(first, second, precision=lax.Precision.HIGHEST)


def complex_product(left_matrix, right_matrix):
    left_real = left_matrix[..., 0, :, :]
    left_imag = left_matrix[..., 1, :, :]
    right_real = right_matrix[..., 0, :, :]
    right_imag = right_matrix[..., 1, :, :]
    real_part = matmul_highest(left_real, right_real) - matmul_highest(left_imag, right_imag)
    imag_part = matmul_highest(left_real, right_imag) + matmul_highest(left_imag, right_real)
    return jnp.stack([real_part, imag_part], axis=-3)


def star_product(former, latter):
    refl_former, trans_former, back_former = former
    refl_latter, trans_latter, back_latter = latter
    reflect = refl_former + complex_product(complex_product(back_former, refl_latter), trans_former)
    return (reflect, complex_product(trans_latter, trans_former), complex_product(back_former, back_latter))


def transpose_complex(matrix):
    return jnp.swapaxes(matrix, -1, -2)


def build_cells(selected, prop_real, prop_imag):
    forward = selected[..., 1, :, :, :]
    backward = selected[..., 2, :, :, :]
    row_real = prop_real[..., :, None]
    row_imag = prop_imag[..., :, None]
    trans = jnp.stack([row_real * forward[..., 0, :, :] - row_imag * forward[..., 1, :, :],
                       row_real * forward[..., 1, :, :] + row_imag * forward[..., 0, :, :]], axis=-3)
    col_real = prop_real[..., None, :]
    col_imag = prop_imag[..., None, :]
    back = jnp.stack([backward[..., 0, :, :] * col_real - backward[..., 1, :, :] * col_imag,
                      backward[..., 0, :, :] * col_imag + backward[..., 1, :, :] * col_real], axis=-3)
    reflect = jnp.broadcast_to(selected[..., 0, :, :, :], trans.shape)
    return (reflect, trans, back)


def reference(interfaces, cell_profile, cell_section, mode_loss, phase, mode_field, target):
    cell_count = cell_profile.shape[0]
    mode_count = mode_loss.shape[1]
    wave_count = phase.shape[1]
    group_size = math.gcd(wave_count, 8)
    selected = interfaces[cell_section]
    amplitude = mode_loss[cell_profile]
    unit_matrix = jnp.stack([jnp.eye(mode_count, dtype=jnp.float32),
                             jnp.zeros((mode_count, mode_count), jnp.float32)])
    identity = jnp.broadcast_to(unit_matrix, (group_size, 2, mode_count, mode_count))
    zero_block = jnp.zeros_like(identity)
    phase_groups = jnp.moveaxis(phase, 1, 0).reshape(wave_count // group_size, group_size, phase.shape[0], mode_count)
    target_groups = target.reshape(wave_count // group_size, group_size, 2, mode_count, mode_count)

    def one_group(coupling, inputs):
        group_phase, group_target = inputs
        angle = jnp.moveaxis(group_phase[:, cell_profile], 1, 0)
        cells = build_cells(selected[:, None], amplitude[:, None, :] * jnp.cos(angle),
                            amplitude[:, None, :] * jnp.sin(angle))

        def forward_step(carry, trans):
            return complex_product(trans, carry), carry

        final_carry, prefix = lax.scan(forward_step, identity, cells[1])

        def backward_step(carry, cell):
            joined = star_product(cell, carry)
            return joined, joined

        last_carry, suffix = lax.scan(backward_step, (zero_block, identity, identity), cells, reverse=True)
        mismatch = suffix[1][0] - group_target
        fields = prefix + complex_product(suffix[0], prefix)
        adjoint = complex_product(transpose_complex(suffix[1]), mismatch)
        real_term = jnp.einsum("cwij,cwkj->cik", fields[:, :, 0], adjoint[:, :, 0], precision=lax.Precision.HIGHEST)
        imag_term = jnp.einsum("cwij,cwkj->cik", fields[:, :, 1], adjoint[:, :, 1], precision=lax.Precision.HIGHEST)
        return coupling + (real_term - imag_term), suffix[0][0]

    coupling, reflection = lax.scan(one_group, jnp.zeros((cell_count, mode_count, mode_count), jnp.float32),
                                    (phase_groups, target_groups))
    reflection = reflection.reshape(wave_count, 2, mode_count, mode_count)

    def project(inputs):
        cell_coupling, profile_index = inputs
        profile_field = mode_field[profile_index]
        return jnp.sum(profile_field * matmul_highest(cell_coupling, profile_field), axis=0)

    gradient = lax.map(project, (coupling, cell_profile))
    return reflection, gradient
```

```python
import functools
import jax
import jax.numpy as jnp
from jax import lax
from jax.experimental import pallas as pl
from jax.experimental.pallas import tpu as pltpu
from jax.sharding import PartitionSpec as P

F32 = jnp.float32
BF16 = jnp.bfloat16
VMEM_LIMIT = 56 * 1024 * 1024


def split(x):
    hi = x.astype(BF16)
    lo = (x - hi.astype(F32)).astype(BF16)
    return hi, lo


def expand(h):
    m = h.shape[0]
    return jnp.concatenate([h, jnp.concatenate([-h[:, m:], h[:, :m]], axis=1)], axis=0)


def right(pair):
    return expand(pair[0]), expand(pair[1])


def dot(a, b):
    return jnp.dot(a, b, preferred_element_type=F32)


def mul(left, weights):
    hi, lo = left
    m = hi.shape[0]
    both = dot(jnp.concatenate([hi, lo], axis=0), weights[0])
    return both[:m] + both[m:] + dot(hi, weights[1])


def get(ref, *at):
    return ref[(*at, 0)], ref[(*at, 1)]


def put(ref, value, *at):
    hi, lo = split(value)
    ref[(*at, 0)] = hi
    ref[(*at, 1)] = lo


def whole(pair):
    return pair[0].astype(F32) + pair[1].astype(F32)


def unit(m):
    row = lax.broadcasted_iota(jnp.int32, (m, 2 * m), 0)
    col = lax.broadcasted_iota(jnp.int32, (m, 2 * m), 1)
    return jnp.where(row == col, 1.0, 0.0).astype(F32)


def propagation(loss_ref, phase_ref, row_ref, col_ref):
    m = loss_ref.shape[1]
    amp = loss_ref[...]
    angle = phase_ref[...]
    for part, values in enumerate((amp * jnp.cos(angle), amp * jnp.sin(angle))):
        for q in range(loss_ref.shape[0]):
            wide = jnp.broadcast_to(values[q : q + 1], (m, m))
            row_ref[q, part] = wide[:8]
            col_ref[q, part] = wide.T


def trans_leaf(lib_ref, col_ref, q, s):
    re, im = lib_ref[s, 1, 0], lib_ref[s, 1, 1]
    cr, ci = col_ref[q, 0], col_ref[q, 1]
    return jnp.concatenate([cr * re - ci * im, cr * im + ci * re], axis=1)


def back_leaf(lib_ref, row_ref, q, s):
    re, im = lib_ref[s, 2, 0], lib_ref[s, 2, 1]
    rr, ri = row_ref[q, 0][:1], row_ref[q, 1][:1]
    return jnp.concatenate([re * rr - im * ri, re * ri + im * rr], axis=1)


def refl_leaf(lib_ref, s):
    return jnp.concatenate([lib_ref[s, 0, 0], lib_ref[s, 0, 1]], axis=1)


def own_kernel(
    prof_ref, sect_ref, lib_ref, loss_ref, phase_ref,
    grown_ref, back_ref, trans_ref, refl0_ref,
    row_ref, col_ref, tleaf_ref, bleaf_ref, pre_ref, refl_ref,
):
    cells = prof_ref.shape[0]
    m = loss_ref.shape[1]
    last = cells - 1
    propagation(loss_ref, phase_ref, row_ref, col_ref)

    def leaf(i, _):
        q, s = prof_ref[i], sect_ref[i]
        put(tleaf_ref, trans_leaf(lib_ref, col_ref, q, s), i)
        put(bleaf_ref, back_leaf(lib_ref, row_ref, q, s), i)
        return 0

    lax.fori_loop(0, cells, leaf, 0)
    put(pre_ref, unit(m), 0)
    pre_ref[1] = tleaf_ref[0]
    trans_ref[last] = tleaf_ref[last]
    back_ref[last] = bleaf_ref[last]
    put(refl_ref, refl_leaf(lib_ref, sect_ref[last]), last)

    def step(k, _):
        i = last - 1 - k
        b = get(bleaf_ref, i)
        t = right(get(tleaf_ref, i))
        z = mul(b, right(get(refl_ref, i + 1)))
        put(back_ref, mul(b, right(get(back_ref, i + 1))), i)
        put(trans_ref, mul(get(trans_ref, i + 1), t), i)
        put(pre_ref, mul(get(tleaf_ref, k + 1), right(get(pre_ref, k + 1))), k + 2)
        put(refl_ref, refl_leaf(lib_ref, sect_ref[i]) + mul(split(z), t), i)
        return 0

    lax.fori_loop(0, last, step, 0)
    refl0_ref[...] = whole(get(refl_ref, 0))
    for i in range(cells):
        pre = get(pre_ref, i)
        put(grown_ref, whole(pre) + mul(get(refl_ref, i), right(pre)), i)


def merge(former, latter):
    r1, t1, b1 = former
    r2, t2, b2 = latter
    t1w = right(t1)
    z = mul(b1, right(r2))
    back = mul(b1, right(b2))
    trans = mul(t2, t1w)
    refl = whole(r1) + mul(split(z), t1w)
    return refl, trans, back


def main_kernel(
    me_ref, prof_ref, sect_ref, lib_ref, loss_ref, phase_ref, target_ref,
    grown_ref, back_ref, trans_ref, refl0_ref,
    coupling_ref, reflection_ref,
    row_ref, col_ref, pairs_ref, quad_ref, s_ref, q_ref, p_ref, held_ref,
):
    cells = grown_ref.shape[0]
    m = loss_ref.shape[1]
    blocks = prof_ref.shape[0] // cells
    me = me_ref[0]
    propagation(loss_ref, phase_ref, row_ref, col_ref)
    eye = unit(m)

    def cell(c):
        q, s = prof_ref[c], sect_ref[c]
        return (
            split(refl_leaf(lib_ref, s)),
            split(trans_leaf(lib_ref, col_ref, q, s)),
            split(back_leaf(lib_ref, row_ref, q, s)),
        )

    def triple(ref, *at):
        return get(ref, *at, 0), get(ref, *at, 1), get(ref, *at, 2)

    def put_triple(ref, values, *at):
        for kind in range(3):
            put(ref, values[kind], *at, kind)

    put(p_ref, eye)
    put(q_ref, eye)
    put(s_ref, jnp.zeros_like(eye))
    put(held_ref, eye)
    for half in range(2):
        put_triple(quad_ref, (jnp.zeros_like(eye), eye, eye), half)

    def left_step(k, _):
        held = get(held_ref)
        advanced = mul(held, right(get(p_ref)))

        def leaf(c):
            return split(trans_leaf(lib_ref, col_ref, prof_ref[c], sect_ref[c]))

        level = [leaf(k * cells + i) for i in range(cells)]
        while len(level) > 1:
            level = [
                split(mul(level[i + 1], right(level[i]))) for i in range(0, len(level), 2)
            ]
        put(p_ref, advanced)
        held_ref[0], held_ref[1] = level[0]
        return 0

    lax.fori_loop(0, me, left_step, 0)
    put(p_ref, mul(get(held_ref), right(get(p_ref))))

    def pair_step(k, _):
        for j in range(cells // 2):
            c = k * cells + 2 * j
            put_triple(pairs_ref, merge(cell(c), cell(c + 1)), k, j)
        return 0

    lax.fori_loop(me + 1, blocks, pair_step, 0)

    def chain():
        s, q = get(s_ref), get(q_ref)
        for half in (1, 0):
            r, t, b = triple(quad_ref, half)
            tw = right(t)
            z = mul(b, right(s))
            q = split(mul(q, tw))
            s = split(whole(r) + mul(split(z), tw))
        return s, q

    def keep(pair, ref):
        ref[0], ref[1] = pair

    def right_step(i, _):
        k = blocks - 1 - i
        fours = [
            merge(triple(pairs_ref, k, 2 * half), triple(pairs_ref, k, 2 * half + 1))
            for half in range(2)
        ]
        s, q = chain()
        keep(s, s_ref)
        keep(q, q_ref)
        for half in range(2):
            put_triple(quad_ref, fours[half], half)
        return 0

    lax.fori_loop(0, blocks - 1 - me, right_step, 0)
    s, q = chain()
    p = get(p_ref)
    block = right(get(trans_ref, 0))
    q_block = split(mul(q, block))
    s_block = split(mul(s, block))
    total = mul(q_block, right(p))
    reflection_ref[...] = refl0_ref[...] + mul(get(back_ref, 0), right(s_block))
    miss_re = (total[:, :m] - target_ref[0]).T
    miss_im = (total[:, m:] - target_ref[1]).T
    miss = split(jnp.concatenate([miss_re, miss_im], axis=1))
    ahead = split(mul(miss, right(q)))
    x1 = right(split(mul(p, right(ahead))))
    x2 = right(split(mul(s_block, x1)))
    for i in range(cells):
        y = mul(get(grown_ref, i), x1) + mul(get(back_ref, i), x2)
        yh, yl = split(jnp.concatenate([y[:, :m], -y[:, m:]], axis=1))
        th, tl = get(trans_ref, i)
        th = jnp.concatenate([th[:, :m], th[:, m:]], axis=0)
        tl = jnp.concatenate([tl[:, :m], tl[:, m:]], axis=0)
        coupling_ref[i] = mul((yh, yl), (th, tl))


def project_kernel(prof_ref, field_ref, first_ref, second_ref, out_ref, hi_ref, lo_ref):
    for q in range(field_ref.shape[0]):
        hi_ref[q], lo_ref[q] = split(field_ref[q])
    for i in range(first_ref.shape[0]):
        q = prof_ref[i]
        ch, cl = split(first_ref[i] + second_ref[i])
        fh = hi_ref[q]
        w = dot(jnp.concatenate([ch, cl], axis=1), jnp.concatenate([fh, fh], axis=0))
        w = w + dot(ch, lo_ref[q])
        out_ref[i : i + 1] = jnp.sum(field_ref[q] * w, axis=0, keepdims=True)


def specs(kinds):
    return [
        pl.BlockSpec(memory_space=pltpu.SMEM if kind == "s" else pltpu.VMEM) for kind in kinds
    ]


def body(interfaces, cell_profile, cell_section, mode_loss, phase, mode_field, target):
    cells = cell_profile.shape[0]
    profiles, m = mode_loss.shape
    blocks = lax.axis_size("cell")
    waves = lax.axis_size("wl")
    pixels = mode_field.shape[2]
    params = pltpu.CompilerParams(vmem_limit_bytes=VMEM_LIMIT)
    angle = phase.reshape(profiles, m)
    wanted = target.reshape(2, m, m)

    ids = lax.all_gather(jnp.concatenate([cell_profile, cell_section]), "cell")
    prof_all = ids[:, :cells].reshape(-1)
    sect_all = ids[:, cells:].reshape(-1)
    me = lax.axis_index("cell").astype(jnp.int32).reshape(1)

    def pairs(*lead):
        return (*lead, 2, m, 2 * m)

    props = [pltpu.VMEM((profiles, 2, 8, m), F32), pltpu.VMEM((profiles, 2, m, m), F32)]
    grown, back, trans, refl0 = pl.pallas_call(
        own_kernel,
        out_shape=[jax.ShapeDtypeStruct(pairs(cells), BF16)] * 3
        + [jax.ShapeDtypeStruct((m, 2 * m), F32)],
        in_specs=specs("ssvvv"),
        out_specs=specs("vvvv"),
        scratch_shapes=props
        + [pltpu.VMEM(pairs(cells), BF16)] * 2
        + [pltpu.VMEM(pairs(cells + 1), BF16), pltpu.VMEM(pairs(cells), BF16)],
        compiler_params=params,
        name="own_block",
    )(cell_profile, cell_section, interfaces, mode_loss, angle)

    coupling, reflection = pl.pallas_call(
        main_kernel,
        out_shape=[
            jax.ShapeDtypeStruct((cells, m, m), F32),
            jax.ShapeDtypeStruct((m, 2 * m), F32),
        ],
        in_specs=specs("sssvvvvvvvv"),
        out_specs=specs("vv"),
        scratch_shapes=props
        + [
            pltpu.VMEM(pairs(blocks, cells // 2, 3), BF16),
            pltpu.VMEM(pairs(2, 3), BF16),
        ]
        + [pltpu.VMEM(pairs(), BF16)] * 4,
        compiler_params=params,
        name="couplings",
    )(me, prof_all, sect_all, interfaces, mode_loss, angle, wanted, grown, back, trans, refl0)

    rows = m // blocks
    sent = lax.all_to_all(reflection.reshape(blocks, rows, 2 * m), "cell", 0, 0)
    mine = sent[0].reshape(rows, 2, m).transpose(1, 0, 2)[None]

    half = cells // 2
    steps = []
    bit = 1
    while bit < waves:
        steps.append(bit)
        bit *= 2
    parts = [coupling[:half], coupling[half:]]
    other = [jnp.zeros_like(part) for part in parts]
    for number in range(len(steps)):
        if number:
            parts = [a + b for a, b in zip(parts, other)]
        other = [
            lax.ppermute(parts[h], "wl", [(i, i ^ order[number]) for i in range(waves)])
            for h, order in enumerate((steps, steps[::-1]))
        ]
    gradient = pl.pallas_call(
        project_kernel,
        out_shape=jax.ShapeDtypeStruct((cells, pixels), F32),
        in_specs=specs("svvv"),
        out_specs=specs("v")[0],
        scratch_shapes=[pltpu.VMEM((profiles, m, pixels), BF16)] * 2,
        compiler_params=params,
        name="project",
    )(cell_profile, mode_field, jnp.concatenate(parts), jnp.concatenate(other))
    return mine, gradient


def solution(mesh):
    in_specs = (
        P(),
        P("cell"),
        P("cell"),
        P(),
        P(None, "wl", None),
        P(None, None, "wl"),
        P("wl", None, None, None),
    )
    out_specs = (P("wl", None, "cell", None), P("cell", "wl"))
    return jax.shard_map(body, mesh=mesh, in_specs=in_specs, out_specs=out_specs, check_vma=False)
```

```python
import jax
import jax.numpy as jnp
from jax import lax
from jax.experimental import pallas as pl
from jax.experimental.pallas import tpu as pltpu
from jax.sharding import PartitionSpec as P

F32 = jnp.float32
BF16 = jnp.bfloat16
MIB = 1024 * 1024
SHIFT = 8
REFL, TRANS, BACK = 0, 1, 2


def split(x):
    hi = x.astype(BF16)
    lo = (x - hi.astype(F32)).astype(BF16)
    return hi, lo


def whole(pair):
    return pair[0].astype(F32) + pair[1].astype(F32)


def expand(h):
    m = h.shape[0]
    return jnp.concatenate([h, jnp.concatenate([-h[:, m:], h[:, :m]], axis=1)], axis=0)


def right(pair):
    return expand(pair[0]), expand(pair[1])


def dot(a, b):
    return jnp.dot(a, b, preferred_element_type=F32)


def mul(left, weights):
    hi, lo = left
    m = hi.shape[0]
    both = dot(jnp.concatenate([hi, lo], axis=0), weights[0])
    return both[:m] + both[m:] + dot(hi, weights[1])


def get(ref, *at):
    return ref[(*at, 0)], ref[(*at, 1)]


def keep(ref, pair, *at):
    ref[(*at, 0)], ref[(*at, 1)] = pair


def unit(m):
    row = lax.broadcasted_iota(jnp.int32, (m, 2 * m), 0)
    col = lax.broadcasted_iota(jnp.int32, (m, 2 * m), 1)
    return jnp.where(row == col, 1.0, 0.0).astype(F32)


def merge(former, latter):
    r1, t1, b1 = former
    r2, t2, b2 = latter
    t1w = right(t1)
    z = mul(b1, right(r2))
    back = mul(b1, right(b2))
    trans = mul(t2, t1w)
    refl = whole(r1) + mul(split(z), t1w)
    return split(refl), split(trans), split(back)


def merge_end(former, latter):
    r1, t1, b1 = former
    t1w = right(t1)
    z = mul(b1, right(latter[0]))
    trans = mul(latter[1], t1w)
    return split(whole(r1) + mul(split(z), t1w)), split(trans)


def triple(ref, *at):
    return tuple(get(ref, *at, kind) for kind in range(3))


def keep_triple(ref, values, *at):
    for kind in range(3):
        keep(ref, values[kind], *at, kind)


def split_triple(ref, *at):
    return tuple(split(ref[(*at, kind)]) for kind in range(3))


def propagation(loss_ref, phase_ref, row_ref, col_ref):
    m = loss_ref.shape[1]
    amp = loss_ref[...]
    angle = phase_ref[...]
    for part, values in enumerate((amp * jnp.cos(angle), amp * jnp.sin(angle))):
        for q in range(loss_ref.shape[0]):
            wide = jnp.broadcast_to(values[q : q + 1], (m, m))
            row_ref[q, part] = wide[:8]
            col_ref[q, part] = wide.T


def trans_leaf(lib_ref, col_ref, code):
    q, s = code >> SHIFT, code & ((1 << SHIFT) - 1)
    re, im = lib_ref[s, TRANS, 0], lib_ref[s, TRANS, 1]
    cr, ci = col_ref[q, 0], col_ref[q, 1]
    return split(jnp.concatenate([cr * re - ci * im, cr * im + ci * re], axis=1))


def back_leaf(lib_ref, row_ref, code):
    q, s = code >> SHIFT, code & ((1 << SHIFT) - 1)
    re, im = lib_ref[s, BACK, 0], lib_ref[s, BACK, 1]
    rr, ri = row_ref[q, 0][:1], row_ref[q, 1][:1]
    return split(jnp.concatenate([re * rr - im * ri, re * ri + im * rr], axis=1))


def refl_leaf(lib_ref, code):
    s = code & ((1 << SHIFT) - 1)
    return split(jnp.concatenate([lib_ref[s, REFL, 0], lib_ref[s, REFL, 1]], axis=1))


def leaf(lib_ref, row_ref, col_ref, code):
    return (
        refl_leaf(lib_ref, code),
        trans_leaf(lib_ref, col_ref, code),
        back_leaf(lib_ref, row_ref, code),
    )


def own_kernel(code_ref, lib_ref, loss_ref, phase_ref, nodes_ref, own_ref, row_ref, col_ref):
    cells = code_ref.shape[0]
    propagation(loss_ref, phase_ref, row_ref, col_ref)
    pairs = []
    for j in range(cells // 2):
        pairs.append(
            merge(
                leaf(lib_ref, row_ref, col_ref, code_ref[2 * j]),
                leaf(lib_ref, row_ref, col_ref, code_ref[2 * j + 1]),
            )
        )
        keep_triple(nodes_ref, pairs[j], j)
    fours = []
    for j in range(cells // 4):
        fours.append(merge(pairs[2 * j], pairs[2 * j + 1]))
        keep_triple(nodes_ref, fours[j], cells // 2 + j)
    top = merge(*fours)
    for kind in range(3):
        own_ref[kind] = whole(top[kind])


def scan_kernel(
    code_ref, lib_ref, loss_ref, phase_ref, nodes_ref, own_ref,
    grown_ref, back_ref, trans_ref,
    row_ref, col_ref,
):
    cells = code_ref.shape[0]
    m = loss_ref.shape[1]
    propagation(loss_ref, phase_ref, row_ref, col_ref)

    def cell(i):
        return leaf(lib_ref, row_ref, col_ref, code_ref[i])

    def put(i, values):
        keep(trans_ref, values[TRANS], i)
        keep(back_ref, values[BACK], i)
        return values

    def grow(i, refl, before):
        keep(grown_ref, split(whole(before) + mul(refl, right(before))), i)

    def trans_of(i):
        return trans_leaf(lib_ref, col_ref, code_ref[i])

    suffix4 = put(4, triple(nodes_ref, 5))
    before2 = get(nodes_ref, 0, TRANS)
    before4 = get(nodes_ref, 4, TRANS)
    suffix2 = put(2, merge(triple(nodes_ref, 1), suffix4))
    suffix3 = put(3, merge(cell(3), suffix4))
    before3 = split(mul(trans_of(2), right(before2)))
    grow(3, suffix3[REFL], before3)
    grow(2, suffix2[REFL], before2)
    grow(4, suffix4[REFL], before4)
    suffix1 = put(1, merge(cell(1), suffix2))
    before6 = split(mul(get(nodes_ref, 2, TRANS), right(before4)))
    suffix6 = put(6, triple(nodes_ref, 3))
    suffix5 = put(5, merge(cell(5), suffix6))
    grow(6, suffix6[REFL], before6)
    before5 = split(mul(trans_of(4), right(before4)))
    before7 = split(mul(trans_of(6), right(before6)))
    grow(5, suffix5[REFL], before5)
    suffix7 = put(7, cell(7))
    grow(7, suffix7[REFL], before7)
    grow(1, suffix1[REFL], trans_of(0))
    keep(grown_ref, split(unit(m) + own_ref[REFL]), 0)
    keep(trans_ref, split(own_ref[TRANS]), 0)
    keep(back_ref, split(own_ref[BACK]), 0)


def far_kernel(
    me_ref, code_ref, lib_ref, loss_ref, phase_ref, own_ref, out_ref,
    row_ref, col_ref, pairs_ref, fours_ref, acc_ref,
):
    blocks, cells = code_ref.shape
    m = loss_ref.shape[1]
    chips = blocks // 2
    chip = me_ref[0] >> 1
    core = me_ref[0] & 1
    right_count = chips - 1 - chip
    right_end = 2 * chip + 2 + (core + 1) * right_count
    left_end = (core + 1) * chip
    out_ref[0:3] = own_ref[...]
    propagation(loss_ref, phase_ref, row_ref, col_ref)
    eye = split(unit(m))
    none = (jnp.zeros_like(eye[0]), jnp.zeros_like(eye[0]))
    for side in range(2):
        keep_triple(acc_ref, (none, eye, eye), side)

    def place(i):
        on_right = i < right_count
        return jnp.where(on_right, right_end - 1 - i, left_end - 1 - (i - right_count)), on_right

    def pair_step(i, _):
        k, _ = place(i)
        for j in range(cells // 2):
            keep_triple(
                pairs_ref,
                merge(
                    leaf(lib_ref, row_ref, col_ref, code_ref[k, 2 * j]),
                    leaf(lib_ref, row_ref, col_ref, code_ref[k, 2 * j + 1]),
                ),
                i,
                j,
            )
        return 0

    lax.fori_loop(0, chips - 1, pair_step, 0)
    for i in range(chips - 1):
        for j in range(cells // 4):
            keep_triple(
                fours_ref, merge(triple(pairs_ref, i, 2 * j), triple(pairs_ref, i, 2 * j + 1)), i, j
            )
    for i in range(chips - 1):
        keep_triple(pairs_ref, merge(triple(fours_ref, i, 0), triple(fours_ref, i, 1)), i, 0)
    for i in range(chips - 1):
        side = jnp.where(i < right_count, 1, 0)
        first = (i == 0) | (i == right_count)

        @pl.when(first)
        def _():
            acc_ref[side] = pairs_ref[i, 0]

        @pl.when(jnp.logical_not(first))
        def _():
            keep_triple(acc_ref, merge(triple(pairs_ref, i, 0), triple(acc_ref, side)), side)

    for side in range(2):
        for kind in range(3):
            out_ref[3 + 3 * side + kind] = whole(get(acc_ref, side, kind))


OWN, LEFT, RIGHT = 0, 3, 6


def last_kernel(
    me_ref, target_ref, mine_ref, theirs_ref, grown_ref, back_ref, trans_ref,
    first_ref, second_ref, reflection_ref,
    s_ref, q_ref, left_ref,
):
    cells = grown_ref.shape[0]
    m = target_ref.shape[1]
    h = m // 2
    core = me_ref[0] & 1

    def part(ref, start):
        return tuple(split(ref[start + kind]) for kind in range(3))

    def join(zero_ref, one_ref):
        far = merge(part(zero_ref, LEFT), part(one_ref, LEFT))
        end = merge_end(part(zero_ref, RIGHT), part(one_ref, RIGHT))
        return far, end

    @pl.when(core == 0)
    def _():
        far, end = join(mine_ref, theirs_ref)
        s, q = merge_end(part(theirs_ref, OWN), end)
        keep(s_ref, s)
        keep(q_ref, q)
        for kind in range(3):
            left_ref[kind] = whole(far[kind])

    @pl.when(core == 1)
    def _():
        far, end = join(theirs_ref, mine_ref)
        far = merge(far, part(theirs_ref, OWN))
        keep(s_ref, end[0])
        keep(q_ref, end[1])
        for kind in range(3):
            left_ref[kind] = whole(far[kind])

    s, q = get(s_ref), get(q_ref)
    p = split(left_ref[TRANS])
    pw = right(p)
    block = right(get(trans_ref, 0))
    q_block = split(mul(q, block))
    s_block = split(mul(s, block))
    total = mul(q_block, pw)
    here = right(split(mine_ref[OWN + REFL] + mul(get(back_ref, 0), right(s_block))))
    rows = reflection_ref.shape[1]
    at = pl.ds(pl.multiple_of(me_ref[0] * rows, rows), rows)
    mine = mul(split(mul(split(left_ref[BACK, at, :]), here)), pw) + left_ref[REFL, at, :]
    reflection_ref[0] = mine[:, :m]
    reflection_ref[1] = mine[:, m:]
    miss = jnp.concatenate(
        [(total[:, :m] - target_ref[0]).T, (total[:, m:] - target_ref[1]).T], axis=1
    )
    ahead = split(mul(split(miss), right(q)))
    x1 = right(split(mul(p, right(ahead))))
    x2 = right(split(mul(s_block, x1)))
    row = lax.broadcasted_iota(jnp.int32, (h, m), 0)
    lane = lax.broadcasted_iota(jnp.int32, (h, m), 1)
    use_top = (lane >= h) | (row > lane)
    eye = lax.broadcasted_iota(jnp.int32, (m, m), 0) == lax.broadcasted_iota(jnp.int32, (m, m), 1)
    group = cells // 2
    for half, ref in enumerate((first_ref, second_ref)):
        ref[group * h :] = jnp.zeros_like(ref[group * h :])
        for j in range(group):
            i = half * group + j
            y = mul(get(grown_ref, i), x1) + mul(get(back_ref, i), x2)
            ys = split(jnp.concatenate([y[:, :m], -y[:, m:]], axis=1))
            th, tl = get(trans_ref, i)
            th = jnp.concatenate([th[:, :m], th[:, m:]], axis=0)
            tl = jnp.concatenate([tl[:, :m], tl[:, m:]], axis=0)
            c = mul(ys, (th, tl))
            both = c + c.T
            low = pltpu.roll(both[h:], h, 1)
            ref[j * h : (j + 1) * h] = jnp.where(use_top, both[:h], low)
            ref[group * h + j : group * h + j + 1] = jnp.sum(
                jnp.where(eye, c, 0.0), axis=0, keepdims=True
            )


def field_kernel(field_ref, hi_ref, lo_ref):
    for q in range(field_ref.shape[0]):
        hi_ref[q], lo_ref[q] = split(field_ref[q])


def project_kernel(prof_ref, hi_ref, lo_ref, a0_ref, a1_ref, b0_ref, b1_ref, out_ref):
    m = hi_ref.shape[1]
    h = m // 2
    group = prof_ref.shape[0] // 2
    row = lax.broadcasted_iota(jnp.int32, (h, m), 0)
    lane = lax.broadcasted_iota(jnp.int32, (h, m), 1)
    eye = lax.broadcasted_iota(jnp.int32, (m, m), 0) == lax.broadcasted_iota(jnp.int32, (m, m), 1)
    for half, (mine_ref, theirs_ref) in enumerate(((a0_ref, a1_ref), (b0_ref, b1_ref))):
        for j in range(group):
            i = half * group + j
            at = slice(j * h, (j + 1) * h)
            packed = mine_ref[at] + theirs_ref[at]
            at = slice(group * h + j, group * h + j + 1)
            diag = mine_ref[at] + theirs_ref[at]
            top = jnp.where((lane >= h) | (row > lane), packed, 0.0)
            low = pltpu.roll(jnp.where((lane < h) & (row < lane), packed, 0.0), h, 1)
            c = jnp.concatenate([top, low], axis=0) + jnp.where(eye, diag, 0.0)
            ch, cl = split(c)
            q = prof_ref[i]
            fh, fl = hi_ref[q], lo_ref[q]
            w = dot(jnp.concatenate([ch, cl], axis=1), jnp.concatenate([fh, fh], axis=0))
            w = w + dot(ch, fl)
            out_ref[i : i + 1] = jnp.sum(
                (fh.astype(F32) + fl.astype(F32)) * w, axis=0, keepdims=True
            )


def call(kernel, name, kinds, outs, scratch, limit, products, *args):
    def spec(kind):
        return pl.BlockSpec(memory_space=pltpu.SMEM if kind == "s" else pltpu.VMEM)

    several = isinstance(outs, list)
    return pl.pallas_call(
        kernel,
        out_shape=outs,
        in_specs=[spec(kind) for kind in kinds],
        out_specs=[spec("v")] * len(outs) if several else spec("v"),
        scratch_shapes=scratch,
        compiler_params=pltpu.CompilerParams(vmem_limit_bytes=limit * MIB),
        cost_estimate=pl.CostEstimate(
            flops=products * 6 * 8 * 128**3, bytes_accessed=4 * MIB, transcendentals=0
        ),
        name=name,
    )(*args)


def body(interfaces, cell_profile, cell_section, mode_loss, phase, mode_field, target):
    cells = cell_profile.shape[0]
    profiles, m = mode_loss.shape
    blocks = lax.axis_size("cell")
    waves = lax.axis_size("wl")
    pixels = mode_field.shape[2]
    chips = blocks // 2
    angle = phase.reshape(profiles, m)
    wanted = target.reshape(2, m, m)
    me = lax.axis_index("cell").astype(jnp.int32).reshape(1)

    def pairs(*lead):
        return (*lead, 2, m, 2 * m)

    def f32(*shape):
        return jax.ShapeDtypeStruct(shape, F32)

    def bf16(*shape):
        return jax.ShapeDtypeStruct(shape, BF16)

    props = [pltpu.VMEM((profiles, 2, 8, m), F32), pltpu.VMEM((profiles, 2, m, m), F32)]
    codes = (cell_profile << SHIFT) | cell_section
    all_codes = lax.all_to_all(jnp.broadcast_to(codes[None], (blocks, cells)), "cell", 0, 0)
    nodes, own = call(
        own_kernel, "own_tree", "svvv", [bf16(*pairs(6, 3)), f32(3, m, 2 * m)], props, 16, 28,
        codes, interfaces, mode_loss, angle,
    )
    mine = call(
        far_kernel, "far_trees", "ssvvvv", f32(9, m, 2 * m),
        props
        + [
            pltpu.VMEM(pairs(chips - 1, cells // 2, 3), BF16),
            pltpu.VMEM(pairs(chips - 1, cells // 4, 3), BF16),
            pltpu.VMEM(pairs(2, 3), BF16),
        ],
        8 + 3 * blocks, 32 * (chips - 1),
        me, all_codes, interfaces, mode_loss, angle, own,
    )
    theirs = lax.ppermute(mine, "cell", [(i, i ^ 1) for i in range(blocks)])
    grown, back, trans = call(
        scan_kernel, "own_scan", "svvvvv", [bf16(*pairs(cells))] * 3, props, 20, 27,
        codes, interfaces, mode_loss, angle, nodes, own,
    )
    half = f32(cells // 2 * (m // 2) + 8, m)
    first, second, reflection = call(
        last_kernel, "couplings", "svvvvvv", [half, half, f32(2, m // blocks, m)],
        [pltpu.VMEM(pairs(), BF16)] * 2 + [pltpu.VMEM((3, m, 2 * m), F32)], 24, 40,
        me, wanted, mine, theirs, grown, back, trans,
    )

    steps = []
    bit = 1
    while bit < waves:
        steps.append(bit)
        bit *= 2
    parts = [first, second]
    other = [jnp.zeros_like(part) for part in parts]
    for number in range(len(steps)):
        if number:
            parts = [a + b for a, b in zip(parts, other)]
        other = [
            lax.ppermute(part, "wl", [(i, i ^ order[number]) for i in range(waves)])
            for part, order in zip(parts, (steps, steps[::-1]))
        ]
    field = bf16(profiles, m, pixels)
    fields = call(field_kernel, "field_parts", "v", [field, field], [], 12, 1, mode_field)
    gradient = call(
        project_kernel, "project", "svvvvvv", f32(cells, pixels), [], 16, 8,
        cell_profile, *fields, parts[0], other[0], parts[1], other[1],
    )
    return reflection[None], gradient


def solution(mesh):
    in_specs = (
        P(),
        P("cell"),
        P("cell"),
        P(),
        P(None, "wl", None),
        P(None, None, "wl"),
        P("wl", None, None, None),
    )
    out_specs = (P("wl", None, "cell", None), P("cell", "wl"))
    return jax.shard_map(body, mesh=mesh, in_specs=in_specs, out_specs=out_specs, check_vma=False)
```

```python
import functools
import jax
import jax.numpy as jnp
from jax import lax
from jax.experimental import pallas as pl
from jax.experimental.pallas import tpu as pltpu
from jax.sharding import PartitionSpec as P

F32 = jnp.float32
BF16 = jnp.bfloat16
MIB = 1024 * 1024
SHIFT = 8
REFL, TRANS, BACK = 0, 1, 2


def split(x):
    hi = x.astype(BF16)
    lo = (x - hi.astype(F32)).astype(BF16)
    return hi, lo


def whole(pair):
    return pair[0].astype(F32) + pair[1].astype(F32)


def expand(h):
    m = h.shape[0]
    return jnp.concatenate([h, jnp.concatenate([-h[:, m:], h[:, :m]], axis=1)], axis=0)


def right(pair):
    return expand(pair[0]), expand(pair[1])


def dot(a, b):
    return jnp.dot(a, b, preferred_element_type=F32)


def mul(left, weights):
    hi, lo = left
    m = hi.shape[0]
    both = dot(jnp.concatenate([hi, lo], axis=0), weights[0])
    return both[:m] + both[m:] + dot(hi, weights[1])


def get(ref, *at):
    return ref[(*at, 0)], ref[(*at, 1)]


def keep(ref, pair, *at):
    ref[(*at, 0)], ref[(*at, 1)] = pair


def unit(m):
    row = lax.broadcasted_iota(jnp.int32, (m, 2 * m), 0)
    col = lax.broadcasted_iota(jnp.int32, (m, 2 * m), 1)
    return jnp.where(row == col, 1.0, 0.0).astype(F32)


def merge(former, latter):
    r1, t1, b1 = former
    r2, t2, b2 = latter
    t1w = right(t1)
    z = mul(b1, right(r2))
    back = mul(b1, right(b2))
    trans = mul(t2, t1w)
    refl = whole(r1) + mul(split(z), t1w)
    return split(refl), split(trans), split(back)


def triple(ref, *at):
    return tuple(get(ref, *at, kind) for kind in range(3))


def keep_triple(ref, values, *at):
    for kind in range(3):
        keep(ref, values[kind], *at, kind)


def propagation(loss_ref, phase_ref, row_ref, col_ref):
    m = loss_ref.shape[1]
    amp = loss_ref[...]
    angle = phase_ref[...]
    for part, values in enumerate((amp * jnp.cos(angle), amp * jnp.sin(angle))):
        for q in range(loss_ref.shape[0]):
            wide = jnp.broadcast_to(values[q : q + 1], (m, m))
            row_ref[q, part] = wide[:8]
            col_ref[q, part] = wide.T


def trans_leaf(lib_ref, col_ref, code):
    q, s = code >> SHIFT, code & ((1 << SHIFT) - 1)
    re, im = lib_ref[s, TRANS, 0], lib_ref[s, TRANS, 1]
    cr, ci = col_ref[q, 0], col_ref[q, 1]
    return split(jnp.concatenate([cr * re - ci * im, cr * im + ci * re], axis=1))


def back_leaf(lib_ref, row_ref, code):
    q, s = code >> SHIFT, code & ((1 << SHIFT) - 1)
    re, im = lib_ref[s, BACK, 0], lib_ref[s, BACK, 1]
    rr, ri = row_ref[q, 0][:1], row_ref[q, 1][:1]
    return split(jnp.concatenate([re * rr - im * ri, re * ri + im * rr], axis=1))


def refl_leaf(lib_ref, code):
    s = code & ((1 << SHIFT) - 1)
    return split(jnp.concatenate([lib_ref[s, REFL, 0], lib_ref[s, REFL, 1]], axis=1))


def leaf(lib_ref, row_ref, col_ref, code):
    return (
        refl_leaf(lib_ref, code),
        trans_leaf(lib_ref, col_ref, code),
        back_leaf(lib_ref, row_ref, code),
    )


def own_kernel(code_ref, lib_ref, loss_ref, phase_ref, nodes_ref, own_ref, row_ref, col_ref):
    cells = code_ref.shape[0]
    propagation(loss_ref, phase_ref, row_ref, col_ref)
    pairs = []
    for j in range(cells // 2):
        pairs.append(
            merge(
                leaf(lib_ref, row_ref, col_ref, code_ref[2 * j]),
                leaf(lib_ref, row_ref, col_ref, code_ref[2 * j + 1]),
            )
        )
        keep_triple(nodes_ref, pairs[j], j)
    fours = []
    for j in range(cells // 4):
        fours.append(merge(pairs[2 * j], pairs[2 * j + 1]))
        keep_triple(nodes_ref, fours[j], cells // 2 + j)
    top = merge(*fours)
    for kind in range(3):
        own_ref[kind] = whole(top[kind])


def scan_kernel(
    code_ref, lib_ref, row_ref, col_ref, nodes_ref, own_ref, grown_ref, back_ref, trans_ref
):
    m = own_ref.shape[1]

    def cell(i):
        return leaf(lib_ref, row_ref, col_ref, code_ref[i])

    def store(ref, i, pair):
        ref[0, i], ref[1, i] = pair

    def put(i, values):
        store(trans_ref, i, values[TRANS])
        store(back_ref, i, values[BACK])
        return values

    def grow(i, refl, before):
        store(grown_ref, i, split(whole(before) + mul(refl, right(before))))

    def trans_of(i):
        return trans_leaf(lib_ref, col_ref, code_ref[i])

    suffix4 = put(4, triple(nodes_ref, 5))
    before2 = get(nodes_ref, 0, TRANS)
    before4 = get(nodes_ref, 4, TRANS)
    suffix2 = put(2, merge(triple(nodes_ref, 1), suffix4))
    suffix3 = put(3, merge(cell(3), suffix4))
    before3 = split(mul(trans_of(2), right(before2)))
    grow(3, suffix3[REFL], before3)
    grow(2, suffix2[REFL], before2)
    grow(4, suffix4[REFL], before4)
    suffix1 = put(1, merge(cell(1), suffix2))
    before6 = split(mul(get(nodes_ref, 2, TRANS), right(before4)))
    suffix6 = put(6, triple(nodes_ref, 3))
    suffix5 = put(5, merge(cell(5), suffix6))
    grow(6, suffix6[REFL], before6)
    before5 = split(mul(trans_of(4), right(before4)))
    before7 = split(mul(trans_of(6), right(before6)))
    grow(5, suffix5[REFL], before5)
    suffix7 = put(7, cell(7))
    grow(7, suffix7[REFL], before7)
    grow(1, suffix1[REFL], trans_of(0))
    store(grown_ref, 0, split(unit(m) + own_ref[REFL]))
    store(trans_ref, 0, split(own_ref[TRANS]))
    store(back_ref, 0, split(own_ref[BACK]))


def far_kernel(*refs):
    me_ref, *code_refs = refs[:-9]
    lib_ref, row_ref, col_ref, own_ref, out_ref, code_ref, pairs_ref, fours_ref, acc_ref = refs[-9:]
    blocks, cells = code_ref.shape
    m = own_ref.shape[1]
    chips = blocks // 2
    me = me_ref[0]
    chip = me >> 1
    core = me & 1
    right_count = chips - 1 - chip
    right_end = 2 * chip + 2 + (core + 1) * right_count
    left_end = (core + 1) * chip
    out_ref[0:3] = own_ref[...]
    for r, ref in enumerate(code_refs):
        k = lax.rem(me + 1 + r, blocks)
        for i in range(cells):
            code_ref[k, i] = ref[i]
    eye = split(unit(m))
    none = (jnp.zeros_like(eye[0]), jnp.zeros_like(eye[0]))
    for side in range(2):
        keep_triple(acc_ref, (none, eye, eye), side)

    def place(i):
        on_right = i < right_count
        return jnp.where(on_right, right_end - 1 - i, left_end - 1 - (i - right_count))

    def pair_step(i, _):
        k = place(i)
        for j in range(cells // 2):
            keep_triple(
                pairs_ref,
                merge(
                    leaf(lib_ref, row_ref, col_ref, code_ref[k, 2 * j]),
                    leaf(lib_ref, row_ref, col_ref, code_ref[k, 2 * j + 1]),
                ),
                i,
                j,
            )
        return 0

    lax.fori_loop(0, chips - 1, pair_step, 0)
    for i in range(chips - 1):
        for j in range(cells // 4):
            keep_triple(
                fours_ref, merge(triple(pairs_ref, i, 2 * j), triple(pairs_ref, i, 2 * j + 1)), i, j
            )
    for i in range(chips - 1):
        keep_triple(pairs_ref, merge(triple(fours_ref, i, 0), triple(fours_ref, i, 1)), i, 0)
    for i in range(chips - 1):
        side = jnp.where(i < right_count, 1, 0)
        first = (i == 0) | (i == right_count)

        @pl.when(first)
        def _():
            acc_ref[side] = pairs_ref[i, 0]

        @pl.when(jnp.logical_not(first))
        def _():
            keep_triple(acc_ref, merge(triple(pairs_ref, i, 0), triple(acc_ref, side)), side)

    for side in range(2):
        for kind in range(3):
            out_ref[3 + 3 * side + kind] = whole(get(acc_ref, side, kind))


OWN, LEFT, RIGHT = 0, 3, 6


def sides(me_ref, mine_ref, theirs_ref):
    on_first = (me_ref[0] & 1) == 0

    def first(index):
        return jnp.where(on_first, mine_ref[index], theirs_ref[index])

    def second(index):
        return jnp.where(on_first, theirs_ref[index], mine_ref[index])

    return on_first, first, second


def chain_kernel(me_ref, target_ref, mine_ref, theirs_ref, x_ref):
    m = target_ref.shape[1]
    on_first, first, second = sides(me_ref, mine_ref, theirs_ref)
    own0_t = split(first(OWN + TRANS))
    own1_t = split(second(OWN + TRANS))
    own1_tw = right(own1_t)
    far0_tw = right(split(first(RIGHT + TRANS)))
    p_far = mul(split(second(LEFT + TRANS)), right(split(first(LEFT + TRANS))))
    q_far = mul(split(second(RIGHT + TRANS)), far0_tw)
    p_fars, q_fars = split(p_far), split(q_far)
    z = mul(split(first(RIGHT + BACK)), right(split(second(RIGHT + REFL))))
    p_here = mul(own0_t, right(p_fars))
    q_here = mul(q_fars, own1_tw)
    s_far = first(RIGHT + REFL) + mul(split(z), far0_tw)
    total = mul(split(q_here), right(split(p_here)))
    z = mul(split(second(OWN + BACK)), right(split(s_far)))
    miss = jnp.concatenate(
        [(total[:, :m] - target_ref[0]).T, (total[:, m:] - target_ref[1]).T], axis=1
    )
    s_here = second(OWN + REFL) + mul(split(z), own1_tw)
    p = split(jnp.where(on_first, p_far, p_here))
    q = split(jnp.where(on_first, q_here, q_far))
    s = split(jnp.where(on_first, s_here, s_far))
    ahead = mul(split(miss), right(q))
    s_block = mul(s, right(split(mine_ref[OWN + TRANS])))
    x1 = right(split(mul(p, right(split(ahead)))))
    x_ref[0, 0], x_ref[0, 1] = x1
    x_ref[1, 0], x_ref[1, 1] = right(split(mul(split(s_block), x1)))


def reflect_kernel(me_ref, mine_ref, theirs_ref, out_ref, left_ref):
    rows, m = out_ref.shape[1:]
    _, first, second = sides(me_ref, mine_ref, theirs_ref)

    def extend(former, refl):
        z = mul(split(former(BACK)), right(split(refl)))
        return former(REFL) + mul(split(z), right(split(former(TRANS))))

    refl = extend(lambda kind: first(RIGHT + kind), second(RIGHT + REFL))
    refl = extend(lambda kind: second(OWN + kind), refl)
    refl = extend(lambda kind: first(OWN + kind), refl)
    refl = extend(lambda kind: second(LEFT + kind), refl)
    left_ref[0] = first(LEFT + REFL)
    left_ref[1] = first(LEFT + BACK)
    at = pl.ds(pl.multiple_of(me_ref[0] * rows, rows), rows)
    z = mul(split(left_ref[1, at, :]), right(split(refl)))
    mine = left_ref[0, at, :] + mul(split(z), right(split(first(LEFT + TRANS))))
    out_ref[0] = mine[:, :m]
    out_ref[1] = mine[:, m:]


def coupling_kernel(half, x_ref, grown_ref, back_ref, trans_ref, out_ref):
    group = grown_ref.shape[1] // 2
    m = grown_ref.shape[2]
    h = m // 2
    cells = slice(half * group, (half + 1) * group)

    def stack(ref):
        return tuple(ref[part, cells].reshape(group * m, 2 * m) for part in range(2))

    row = lax.broadcasted_iota(jnp.int32, (h, m), 0)
    lane = lax.broadcasted_iota(jnp.int32, (h, m), 1)
    use_top = (lane >= h) | (row > lane)
    eye = lax.broadcasted_iota(jnp.int32, (m, m), 0) == lax.broadcasted_iota(jnp.int32, (m, m), 1)
    all_y = mul(stack(grown_ref), (x_ref[0, 0], x_ref[0, 1]))
    all_y = all_y + mul(stack(back_ref), (x_ref[1, 0], x_ref[1, 1]))
    out_ref[group * h :] = jnp.zeros_like(out_ref[group * h :])
    for j in range(group):
        y = all_y[j * m : (j + 1) * m]
        ys = split(jnp.concatenate([y[:, :m], -y[:, m:]], axis=1))
        t = [trans_ref[part, half * group + j] for part in range(2)]
        c = mul(ys, [jnp.concatenate([a[:, :m], a[:, m:]], axis=0) for a in t])
        both = c + c.T
        low = pltpu.roll(both[h:], h, 1)
        out_ref[j * h : (j + 1) * h] = jnp.where(use_top, both[:h], low)
        out_ref[group * h + j : group * h + j + 1] = jnp.sum(
            jnp.where(eye, c, 0.0), axis=0, keepdims=True
        )


def field_kernel(field_ref, hi_ref, lo_ref):
    for q in range(field_ref.shape[0]):
        hi_ref[q], lo_ref[q] = split(field_ref[q])


def project_kernel(half, prof_ref, hi_ref, lo_ref, mine_ref, theirs_ref, *rest):
    out_ref = rest[-1]
    m = hi_ref.shape[1]
    h = m // 2
    group = prof_ref.shape[0] // 2
    if half:
        out_ref[:group] = rest[0][...]
    row = lax.broadcasted_iota(jnp.int32, (h, m), 0)
    lane = lax.broadcasted_iota(jnp.int32, (h, m), 1)
    eye = lax.broadcasted_iota(jnp.int32, (m, m), 0) == lax.broadcasted_iota(jnp.int32, (m, m), 1)
    for j in range(group):
        at = slice(j * h, (j + 1) * h)
        packed = mine_ref[at] + theirs_ref[at]
        at = slice(group * h + j, group * h + j + 1)
        diag = mine_ref[at] + theirs_ref[at]
        top = jnp.where((lane >= h) | (row > lane), packed, 0.0)
        low = pltpu.roll(jnp.where((lane < h) & (row < lane), packed, 0.0), h, 1)
        c = jnp.concatenate([top, low], axis=0) + jnp.where(eye, diag, 0.0)
        ch, cl = split(c)
        q = prof_ref[half * group + j]
        fh, fl = hi_ref[q], lo_ref[q]
        w = dot(jnp.concatenate([ch, cl], axis=1), jnp.concatenate([fh, fh], axis=0))
        w = w + dot(ch, fl)
        i = half * group + j
        out_ref[i : i + 1] = jnp.sum(
            (fh.astype(F32) + fl.astype(F32)) * w, axis=0, keepdims=True
        )


def call(kernel, name, kinds, outs, scratch, limit, products, *args):
    def spec(kind):
        return pl.BlockSpec(memory_space=pltpu.SMEM if kind == "s" else pltpu.VMEM)

    several = isinstance(outs, list)
    return pl.pallas_call(
        kernel,
        out_shape=outs,
        in_specs=[spec(kind) for kind in kinds],
        out_specs=[spec("v")] * len(outs) if several else spec("v"),
        scratch_shapes=scratch,
        compiler_params=pltpu.CompilerParams(vmem_limit_bytes=limit * MIB),
        cost_estimate=pl.CostEstimate(
            flops=products * 6 * 8 * 128**3, bytes_accessed=4 * MIB, transcendentals=0
        ),
        name=name,
    )(*args)


def body(interfaces, cell_profile, cell_section, mode_loss, phase, mode_field, target):
    cells = cell_profile.shape[0]
    profiles, m = mode_loss.shape
    blocks = lax.axis_size("cell")
    waves = lax.axis_size("wl")
    pixels = mode_field.shape[2]
    chips = blocks // 2
    angle = phase.reshape(profiles, m)
    wanted = target.reshape(2, m, m)
    me = lax.axis_index("cell").astype(jnp.int32).reshape(1)

    def pairs(*lead):
        return (*lead, 2, m, 2 * m)

    def f32(*shape):
        return jax.ShapeDtypeStruct(shape, F32)

    def bf16(*shape):
        return jax.ShapeDtypeStruct(shape, BF16)

    tables = [f32(profiles, 2, 8, m), f32(profiles, 2, m, m)]
    codes = (cell_profile << SHIFT) | cell_section
    others = [
        lax.ppermute(codes, "cell", [((i + r) % blocks, i) for i in range(blocks)])
        for r in range(1, blocks)
    ]
    nodes, own, row_table, col_table = call(
        own_kernel, "own_tree", "svvv", [bf16(*pairs(6, 3)), f32(3, m, 2 * m), *tables], [], 16, 28,
        codes, interfaces, mode_loss, angle,
    )
    mine = call(
        far_kernel, "far_trees", "s" * blocks + "vvvv", f32(9, m, 2 * m),
        [
            pltpu.SMEM((blocks, cells), jnp.int32),
            pltpu.VMEM(pairs(chips - 1, cells // 2, 3), BF16),
            pltpu.VMEM(pairs(chips - 1, cells // 4, 3), BF16),
            pltpu.VMEM(pairs(2, 3), BF16),
        ],
        8 + 3 * blocks, 32 * (chips - 1),
        me, *others, interfaces, row_table, col_table, own,
    )
    theirs = lax.ppermute(mine, "cell", [(i, i ^ 1) for i in range(blocks)])
    parts_shape = bf16(2, cells, m, 2 * m)
    grown, back, trans = call(
        scan_kernel, "own_scan", "svvvvv", [parts_shape] * 3, [], 20, 27,
        codes, interfaces, row_table, col_table, nodes, own,
    )
    x = call(
        chain_kernel, "chain", "svvv", bf16(2, 2, 2 * m, 2 * m), [], 16, 20,
        me, wanted, mine, theirs,
    )
    parts = [
        call(
            functools.partial(coupling_kernel, half), "couplings", "vvvv",
            f32(cells // 2 * (m // 2) + 8, m), [], 16, 10,
            x, grown, back, trans,
        )
        for half in range(2)
    ]
    reflection = call(
        reflect_kernel, "reflection", "svv", f32(2, m // blocks, m),
        [pltpu.VMEM((2, m, 2 * m), F32)], 16, 10,
        me, mine, theirs,
    )

    steps = []
    bit = 1
    while bit < waves:
        steps.append(bit)
        bit *= 2
    other = [jnp.zeros_like(part) for part in parts]
    for number in range(len(steps)):
        if number:
            parts = [a + b for a, b in zip(parts, other)]
        other = [
            lax.ppermute(part, "wl", [(i, i ^ order[number]) for i in range(waves)])
            for part, order in zip(parts, (steps, steps[::-1]))
        ]
    field = bf16(profiles, m, pixels)
    fields = call(field_kernel, "field_parts", "v", [field, field], [], 12, 1, mode_field)
    gradient = call(
        functools.partial(project_kernel, 0), "project", "svvvv", f32(cells // 2, pixels), [], 16, 4,
        cell_profile, *fields, parts[0], other[0],
    )
    gradient = call(
        functools.partial(project_kernel, 1), "project", "svvvvv", f32(cells, pixels), [], 16, 4,
        cell_profile, *fields, parts[1], other[1], gradient,
    )
    return reflection[None], gradient


def solution(mesh):
    in_specs = (
        P(),
        P("cell"),
        P("cell"),
        P(),
        P(None, "wl", None),
        P(None, None, "wl"),
        P("wl", None, None, None),
    )
    out_specs = (P("wl", None, "cell", None), P("cell", "wl"))
    return jax.shard_map(body, mesh=mesh, in_specs=in_specs, out_specs=out_specs, check_vma=False)
```

```python
import functools
import jax
import jax.numpy as jnp
from jax import lax
from jax.experimental import pallas as pl
from jax.experimental.pallas import tpu as pltpu
from jax.sharding import PartitionSpec as P

F32 = jnp.float32
BF16 = jnp.bfloat16
MIB = 1024 * 1024
SHIFT = 8
LOW = (1 << SHIFT) - 1
REFL, TRANS, BACK = 0, 1, 2
FEWER = 3


def split(x):
    hi = x.astype(BF16)
    lo = (x - hi.astype(F32)).astype(BF16)
    return hi, lo


def whole(pair):
    return pair[0].astype(F32) + pair[1].astype(F32)


def expand(h):
    m = h.shape[0]
    return jnp.concatenate([h, jnp.concatenate([-h[:, m:], h[:, :m]], axis=1)], axis=0)


def right(pair):
    return expand(pair[0]), expand(pair[1])


def dot(a, b):
    return jnp.dot(a, b, preferred_element_type=F32)


def mul(left, weights):
    hi, lo = left
    m = hi.shape[0]
    both = dot(jnp.concatenate([hi, lo], axis=0), weights[0])
    return both[:m] + both[m:] + dot(hi, weights[1])


def get(ref, *at):
    return ref[(*at, 0)], ref[(*at, 1)]


def keep(ref, pair, *at):
    ref[(*at, 0)], ref[(*at, 1)] = pair


def unit(m):
    row = lax.broadcasted_iota(jnp.int32, (m, 2 * m), 0)
    col = lax.broadcasted_iota(jnp.int32, (m, 2 * m), 1)
    return jnp.where(row == col, 1.0, 0.0).astype(F32)


def merge(former, latter):
    r1, t1, b1 = former
    r2, t2, b2 = latter
    t1w = right(t1)
    z = mul(b1, right(r2))
    back = mul(b1, right(b2))
    trans = mul(t2, t1w)
    refl = whole(r1) + mul(split(z), t1w)
    return split(refl), split(trans), split(back)


def triple(ref, *at):
    return tuple(get(ref, *at, kind) for kind in range(3))


def keep_triple(ref, values, *at):
    for kind in range(3):
        keep(ref, values[kind], *at, kind)


def spread(factor_refs, row_ref, col_ref):
    for part, ref in enumerate(factor_refs):
        profiles, m = ref.shape
        for q in range(profiles):
            wide = jnp.broadcast_to(ref[q : q + 1], (m, m))
            row_ref[q, part] = wide[:8]
            col_ref[q, part] = wide.T


def trans_leaf(lib_ref, col_ref, code):
    q, s = code >> SHIFT, code & LOW
    re, im = lib_ref[s, TRANS, 0], lib_ref[s, TRANS, 1]
    cr, ci = col_ref[q, 0], col_ref[q, 1]
    return split(jnp.concatenate([cr * re - ci * im, cr * im + ci * re], axis=1))


def back_leaf(lib_ref, row_ref, code):
    q, s = code >> SHIFT, code & LOW
    re, im = lib_ref[s, BACK, 0], lib_ref[s, BACK, 1]
    rr, ri = row_ref[q, 0][:1], row_ref[q, 1][:1]
    return split(jnp.concatenate([re * rr - im * ri, re * ri + im * rr], axis=1))


def refl_leaf(lib_ref, code):
    s = code & LOW
    return split(jnp.concatenate([lib_ref[s, REFL, 0], lib_ref[s, REFL, 1]], axis=1))


def leaf(lib_ref, row_ref, col_ref, code):
    return (
        refl_leaf(lib_ref, code),
        trans_leaf(lib_ref, col_ref, code),
        back_leaf(lib_ref, row_ref, code),
    )


def own_kernel(
    me_ref, code_ref, lib_ref, real_ref, imag_ref, nodes_ref, own_ref, row_ref, col_ref
):
    cells = code_ref.shape[1]
    spread((real_ref, imag_ref), row_ref, col_ref)

    def cell(i):
        return leaf(lib_ref, row_ref, col_ref, code_ref[me_ref[0], i])

    pairs = []
    for j in range(cells // 2):
        pairs.append(merge(cell(2 * j), cell(2 * j + 1)))
        keep_triple(nodes_ref, pairs[j], j)
    fours = []
    for j in range(cells // 4):
        fours.append(merge(pairs[2 * j], pairs[2 * j + 1]))
        keep_triple(nodes_ref, fours[j], cells // 2 + j)
    top = merge(*fours)
    for kind in range(3):
        own_ref[kind] = whole(top[kind])


def scan_kernel(
    me_ref, code_ref, lib_ref, row_ref, col_ref, nodes_ref, own_ref,
    grown_ref, back_ref, trans_ref,
):
    m = own_ref.shape[1]

    def code(i):
        return code_ref[me_ref[0], i]

    def cell(i):
        return leaf(lib_ref, row_ref, col_ref, code(i))

    def store(ref, i, pair):
        ref[0, i], ref[1, i] = pair

    def put(i, values):
        store(trans_ref, i, values[TRANS])
        store(back_ref, i, values[BACK])
        return values

    def grow(i, refl, before):
        store(grown_ref, i, split(whole(before) + mul(refl, right(before))))

    def trans_of(i):
        return trans_leaf(lib_ref, col_ref, code(i))

    suffix4 = put(4, triple(nodes_ref, 5))
    before2 = get(nodes_ref, 0, TRANS)
    before4 = get(nodes_ref, 4, TRANS)
    suffix2 = put(2, merge(triple(nodes_ref, 1), suffix4))
    suffix3 = put(3, merge(cell(3), suffix4))
    before3 = split(mul(trans_of(2), right(before2)))
    grow(3, suffix3[REFL], before3)
    grow(2, suffix2[REFL], before2)
    grow(4, suffix4[REFL], before4)
    suffix1 = put(1, merge(cell(1), suffix2))
    before6 = split(mul(get(nodes_ref, 2, TRANS), right(before4)))
    suffix6 = put(6, triple(nodes_ref, 3))
    suffix5 = put(5, merge(cell(5), suffix6))
    grow(6, suffix6[REFL], before6)
    before5 = split(mul(trans_of(4), right(before4)))
    before7 = split(mul(trans_of(6), right(before6)))
    grow(5, suffix5[REFL], before5)
    suffix7 = put(7, cell(7))
    grow(7, suffix7[REFL], before7)
    grow(1, suffix1[REFL], trans_of(0))
    store(grown_ref, 0, split(unit(m) + own_ref[REFL]))
    store(trans_ref, 0, split(own_ref[TRANS]))
    store(back_ref, 0, split(own_ref[BACK]))


def far_kernel(
    me_ref, code_ref, lib_ref, row_ref, col_ref, own_ref, out_ref, pairs_ref, fours_ref, acc_ref
):
    blocks, cells = code_ref.shape
    m = own_ref.shape[1]
    chips = blocks // 2
    chip = me_ref[0] >> 1
    core = me_ref[0] & 1
    right_count = chips - 1 - chip
    right_end = 2 * chip + 2 + (core + 1) * right_count
    left_end = (core + 1) * chip
    out_ref[0:3] = own_ref[...]
    eye = split(unit(m))
    none = (jnp.zeros_like(eye[0]), jnp.zeros_like(eye[0]))
    for side in range(2):
        keep_triple(acc_ref, (none, eye, eye), side)

    def place(i):
        on_right = i < right_count
        return jnp.where(on_right, right_end - 1 - i, left_end - 1 - (i - right_count))

    def pair_step(i, _):
        k = place(i)
        for j in range(cells // 2):
            keep_triple(
                pairs_ref,
                merge(
                    leaf(lib_ref, row_ref, col_ref, code_ref[k, 2 * j]),
                    leaf(lib_ref, row_ref, col_ref, code_ref[k, 2 * j + 1]),
                ),
                i,
                j,
            )
        return 0

    lax.fori_loop(0, chips - 1, pair_step, 0)
    for i in range(chips - 1):
        for j in range(cells // 4):
            keep_triple(
                fours_ref, merge(triple(pairs_ref, i, 2 * j), triple(pairs_ref, i, 2 * j + 1)), i, j
            )
    for i in range(chips - 1):
        keep_triple(pairs_ref, merge(triple(fours_ref, i, 0), triple(fours_ref, i, 1)), i, 0)
    for i in range(chips - 1):
        side = jnp.where(i < right_count, 1, 0)
        first = (i == 0) | (i == right_count)

        @pl.when(first)
        def _():
            acc_ref[side] = pairs_ref[i, 0]

        @pl.when(jnp.logical_not(first))
        def _():
            keep_triple(acc_ref, merge(triple(pairs_ref, i, 0), triple(acc_ref, side)), side)

    for side in range(2):
        for kind in range(3):
            out_ref[3 + 3 * side + kind] = whole(get(acc_ref, side, kind))


OWN, LEFT, RIGHT = 0, 3, 6


def sides(me_ref, mine_ref, theirs_ref):
    on_first = (me_ref[0] & 1) == 0

    def first(index):
        return jnp.where(on_first, mine_ref[index], theirs_ref[index])

    def second(index):
        return jnp.where(on_first, theirs_ref[index], mine_ref[index])

    return on_first, first, second


def chain_kernel(me_ref, target_ref, mine_ref, theirs_ref, x_ref, part_ref):
    m = target_ref.shape[1]
    on_first, first, second = sides(me_ref, mine_ref, theirs_ref)
    own0_t = split(first(OWN + TRANS))
    own1_t = split(second(OWN + TRANS))
    own1_tw = right(own1_t)
    far0_tw = right(split(first(RIGHT + TRANS)))
    p_far = mul(split(second(LEFT + TRANS)), right(split(first(LEFT + TRANS))))
    q_far = mul(split(second(RIGHT + TRANS)), far0_tw)
    p_fars, q_fars = split(p_far), split(q_far)
    z = mul(split(first(RIGHT + BACK)), right(split(second(RIGHT + REFL))))
    p_here = mul(own0_t, right(p_fars))
    q_here = mul(q_fars, own1_tw)
    s_far = first(RIGHT + REFL) + mul(split(z), far0_tw)
    total = mul(split(q_here), right(split(p_here)))
    z = mul(split(second(OWN + BACK)), right(split(s_far)))
    miss = jnp.concatenate(
        [(total[:, :m] - target_ref[0]).T, (total[:, m:] - target_ref[1]).T], axis=1
    )
    s_here = second(OWN + REFL) + mul(split(z), own1_tw)
    part_ref[0] = s_here
    part_ref[1] = p_far
    p = split(jnp.where(on_first, p_far, p_here))
    q = split(jnp.where(on_first, q_here, q_far))
    s = split(jnp.where(on_first, s_here, s_far))
    ahead = mul(split(miss), right(q))
    s_block = mul(s, right(split(mine_ref[OWN + TRANS])))
    x1 = right(split(mul(p, right(split(ahead)))))
    x_ref[0, 0], x_ref[0, 1] = x1
    x_ref[1, 0], x_ref[1, 1] = right(split(mul(split(s_block), x1)))


def reflect_kernel(me_ref, mine_ref, theirs_ref, part_ref, out_ref, left_ref):
    rows, m = out_ref.shape[1:]
    _, first, second = sides(me_ref, mine_ref, theirs_ref)
    left_ref[0] = first(LEFT + REFL)
    left_ref[1] = first(LEFT + BACK)
    at = pl.ds(pl.multiple_of(me_ref[0] * rows, rows), rows)
    back = split(left_ref[1, at, :])
    z = mul(split(first(OWN + BACK)), right(split(part_ref[0])))
    refl = first(OWN + REFL) + mul(split(z), right(split(first(OWN + TRANS))))
    z = mul(back, right(split(second(LEFT + REFL))))
    left = left_ref[0, at, :] + mul(split(z), right(split(first(LEFT + TRANS))))
    back = mul(back, right(split(second(LEFT + BACK))))
    z = mul(split(back), right(split(refl)))
    mine = left + mul(split(z), right(split(part_ref[1])))
    out_ref[0] = mine[:, :m]
    out_ref[1] = mine[:, m:]


def coupling_kernel(start, group, x_ref, grown_ref, back_ref, trans_ref, out_ref):
    m = grown_ref.shape[2]
    h = m // 2
    cells = slice(start, start + group)

    def stack(ref):
        return tuple(ref[part, cells].reshape(group * m, 2 * m) for part in range(2))

    row = lax.broadcasted_iota(jnp.int32, (h, m), 0)
    lane = lax.broadcasted_iota(jnp.int32, (h, m), 1)
    use_top = (lane >= h) | (row > lane)
    eye = lax.broadcasted_iota(jnp.int32, (m, m), 0) == lax.broadcasted_iota(jnp.int32, (m, m), 1)
    all_y = mul(stack(grown_ref), (x_ref[0, 0], x_ref[0, 1]))
    all_y = all_y + mul(stack(back_ref), (x_ref[1, 0], x_ref[1, 1]))
    out_ref[group * h :] = jnp.zeros_like(out_ref[group * h :])
    for j in range(group):
        y = all_y[j * m : (j + 1) * m]
        ys = split(jnp.concatenate([y[:, :m], -y[:, m:]], axis=1))
        t = [trans_ref[part, start + j] for part in range(2)]
        c = mul(ys, [jnp.concatenate([a[:, :m], a[:, m:]], axis=0) for a in t])
        both = c + c.T
        low = pltpu.roll(both[h:], h, 1)
        out_ref[j * h : (j + 1) * h] = jnp.where(use_top, both[:h], low)
        out_ref[group * h + j : group * h + j + 1] = jnp.sum(
            jnp.where(eye, c, 0.0), axis=0, keepdims=True
        )


def field_kernel(field_ref, hi_ref, lo_ref):
    for q in range(field_ref.shape[0]):
        hi_ref[q], lo_ref[q] = split(field_ref[q])


def project_kernel(start, group, prof_ref, hi_ref, lo_ref, mine_ref, theirs_ref, *rest):
    out_ref = rest[-1]
    m = hi_ref.shape[1]
    h = m // 2
    if start:
        out_ref[:start] = rest[0][...]
    row = lax.broadcasted_iota(jnp.int32, (h, m), 0)
    lane = lax.broadcasted_iota(jnp.int32, (h, m), 1)
    eye = lax.broadcasted_iota(jnp.int32, (m, m), 0) == lax.broadcasted_iota(jnp.int32, (m, m), 1)
    for j in range(group):
        at = slice(j * h, (j + 1) * h)
        packed = mine_ref[at] + theirs_ref[at]
        at = slice(group * h + j, group * h + j + 1)
        diag = mine_ref[at] + theirs_ref[at]
        top = jnp.where((lane >= h) | (row > lane), packed, 0.0)
        low = pltpu.roll(jnp.where((lane < h) & (row < lane), packed, 0.0), h, 1)
        c = jnp.concatenate([top, low], axis=0) + jnp.where(eye, diag, 0.0)
        ch, cl = split(c)
        q = prof_ref[start + j]
        fh, fl = hi_ref[q], lo_ref[q]
        w = dot(jnp.concatenate([ch, cl], axis=1), jnp.concatenate([fh, fh], axis=0))
        w = w + dot(ch, fl)
        i = start + j
        out_ref[i : i + 1] = jnp.sum(
            (fh.astype(F32) + fl.astype(F32)) * w, axis=0, keepdims=True
        )


def call(kernel, name, kinds, outs, scratch, limit, products, *args):
    def spec(kind):
        return pl.BlockSpec(memory_space=pltpu.SMEM if kind == "s" else pltpu.VMEM)

    several = isinstance(outs, list)
    return pl.pallas_call(
        kernel,
        out_shape=outs,
        in_specs=[spec(kind) for kind in kinds],
        out_specs=[spec("v")] * len(outs) if several else spec("v"),
        scratch_shapes=scratch,
        compiler_params=pltpu.CompilerParams(vmem_limit_bytes=limit * MIB),
        cost_estimate=pl.CostEstimate(
            flops=products * 6 * 8 * 128**3, bytes_accessed=4 * MIB, transcendentals=0
        ),
        name=name,
    )(*args)


def body(interfaces, cell_profile, cell_section, mode_loss, phase, mode_field, target):
    cells = cell_profile.shape[0]
    profiles, m = mode_loss.shape
    blocks = lax.axis_size("cell")
    waves = lax.axis_size("wl")
    pixels = mode_field.shape[2]
    chips = blocks // 2
    angle = phase.reshape(profiles, m)
    factors = (mode_loss * jnp.cos(angle), mode_loss * jnp.sin(angle))
    wanted = target.reshape(2, m, m)
    me = lax.axis_index("cell").astype(jnp.int32).reshape(1)

    def pairs(*lead):
        return (*lead, 2, m, 2 * m)

    def f32(*shape):
        return jax.ShapeDtypeStruct(shape, F32)

    def bf16(*shape):
        return jax.ShapeDtypeStruct(shape, BF16)

    tables = [f32(profiles, 2, 8, m), f32(profiles, 2, m, m)]
    codes = (cell_profile << SHIFT) | cell_section
    codes = jnp.broadcast_to(codes[None], (blocks, cells))
    all_codes = lax.all_to_all(codes, "cell", 0, 0)
    nodes, own, row_table, col_table = call(
        own_kernel, "own_tree", "ssvvv", [bf16(*pairs(6, 3)), f32(3, m, 2 * m), *tables], [], 12, 28,
        me, all_codes, interfaces, *factors,
    )
    mine = call(
        far_kernel, "far_trees", "ssvvvv", f32(9, m, 2 * m),
        [
            pltpu.VMEM(pairs(chips - 1, cells // 2, 3), BF16),
            pltpu.VMEM(pairs(chips - 1, cells // 4, 3), BF16),
            pltpu.VMEM(pairs(2, 3), BF16),
        ],
        8 + 3 * blocks // 2, 32 * (chips - 1),
        me, all_codes, interfaces, row_table, col_table, own,
    )
    theirs = lax.ppermute(mine, "cell", [(i, i ^ 1) for i in range(blocks)])
    parts_shape = bf16(2, cells, m, 2 * m)
    grown, back, trans = call(
        scan_kernel, "own_scan", "ssvvvvv", [parts_shape] * 3, [], 16, 27,
        me, all_codes, interfaces, row_table, col_table, nodes, own,
    )
    x, part = call(
        chain_kernel, "chain", "svvv", [bf16(2, 2, 2 * m, 2 * m), f32(2, m, 2 * m)], [], 12, 20,
        me, wanted, mine, theirs,
    )
    reflection = call(
        reflect_kernel, "reflection", "svvv", f32(2, m // blocks, m),
        [pltpu.VMEM((2, m, 2 * m), F32)], 12, 10,
        me, mine, theirs, part,
    )

    steps = []
    bit = 1
    while bit < waves:
        steps.append(bit)
        bit *= 2
    orders = (steps, steps[::-1])

    def exchange(part, number):
        pairs_of = [
            (w * blocks + c, (w ^ orders[c & 1][number]) * blocks + c)
            for w in range(waves)
            for c in range(blocks)
        ]
        return lax.ppermute(part, ("wl", "cell"), pairs_of)

    field = bf16(profiles, m, pixels)
    fields = call(field_kernel, "field_parts", "v", [field, field], [], 12, 1, mode_field)
    gradient = []
    start = 0
    for group in (cells - FEWER, FEWER):
        packed = call(
            functools.partial(coupling_kernel, start, group), "couplings", "vvvv",
            f32(group * (m // 2) + 8, m), [], 12, 10,
            x, grown, back, trans,
        )
        other = jnp.zeros_like(packed)
        for number in range(len(steps)):
            if number:
                packed = packed + other
            other = exchange(packed, number)
        gradient = [
            call(
                functools.partial(project_kernel, start, group), "project",
                "svvvv" + "v" * len(gradient), f32(start + group, pixels), [], 12, 4,
                cell_profile, *fields, packed, other, *gradient,
            )
        ]
        start += group
    return reflection[None], gradient[0]


def solution(mesh):
    in_specs = (
        P(),
        P("cell"),
        P("cell"),
        P(),
        P(None, "wl", None),
        P(None, None, "wl"),
        P("wl", None, None, None),
    )
    out_specs = (P("wl", None, "cell", None), P("cell", "wl"))
    return jax.shard_map(body, mesh=mesh, in_specs=in_specs, out_specs=out_specs, check_vma=False)
```

```python
import functools
import jax
import jax.numpy as jnp
from jax import lax
from jax.experimental import pallas as pl
from jax.experimental.pallas import tpu as pltpu
from jax.sharding import PartitionSpec as P

F32 = jnp.float32
BF16 = jnp.bfloat16
MIB = 1024 * 1024
SHIFT = 8
LOW = (1 << SHIFT) - 1
REFL, TRANS, BACK = 0, 1, 2
FEWER = 3


def split(x):
    hi = x.astype(BF16)
    lo = (x - hi.astype(F32)).astype(BF16)
    return hi, lo


def whole(pair):
    return pair[0].astype(F32) + pair[1].astype(F32)


def expand(h):
    m = h.shape[0]
    return jnp.concatenate([h, jnp.concatenate([-h[:, m:], h[:, :m]], axis=1)], axis=0)


def right(pair):
    return expand(pair[0]), expand(pair[1])


def dot(a, b):
    return jnp.dot(a, b, preferred_element_type=F32)


def mul(left, weights):
    hi, lo = left
    m = hi.shape[0]
    both = dot(jnp.concatenate([hi, lo], axis=0), weights[0])
    return both[:m] + both[m:] + dot(hi, weights[1])


def get(ref, *at):
    return ref[(*at, 0)], ref[(*at, 1)]


def keep(ref, pair, *at):
    ref[(*at, 0)], ref[(*at, 1)] = pair


def unit(m):
    row = lax.broadcasted_iota(jnp.int32, (m, 2 * m), 0)
    col = lax.broadcasted_iota(jnp.int32, (m, 2 * m), 1)
    return jnp.where(row == col, 1.0, 0.0).astype(F32)


def merge(former, latter):
    r1, t1, b1 = former
    r2, t2, b2 = latter
    m = t1[0].shape[0]
    z = split(mul(b1, right(r2)))
    back = mul(b1, right(b2))
    both = mul([jnp.concatenate([a, b], axis=0) for a, b in zip(z, t2)], right(t1))
    return split(whole(r1) + both[:m]), split(both[m:]), split(back)


def triple(ref, *at):
    return tuple(get(ref, *at, kind) for kind in range(3))


def keep_triple(ref, values, *at):
    for kind in range(3):
        keep(ref, values[kind], *at, kind)


def spread(factor_refs, row_ref, col_ref):
    for part, ref in enumerate(factor_refs):
        profiles, m = ref.shape
        for q in range(profiles):
            wide = jnp.broadcast_to(ref[q : q + 1], (m, m))
            row_ref[q, part] = wide[:8]
            col_ref[q, part] = wide.T


def trans_leaf(lib_ref, col_ref, code):
    q, s = code >> SHIFT, code & LOW
    re, im = lib_ref[s, TRANS, 0], lib_ref[s, TRANS, 1]
    cr, ci = col_ref[q, 0], col_ref[q, 1]
    return split(jnp.concatenate([cr * re - ci * im, cr * im + ci * re], axis=1))


def back_leaf(lib_ref, row_ref, code):
    q, s = code >> SHIFT, code & LOW
    re, im = lib_ref[s, BACK, 0], lib_ref[s, BACK, 1]
    rr, ri = row_ref[q, 0][:1], row_ref[q, 1][:1]
    return split(jnp.concatenate([re * rr - im * ri, re * ri + im * rr], axis=1))


def refl_leaf(lib_ref, code):
    s = code & LOW
    return split(jnp.concatenate([lib_ref[s, REFL, 0], lib_ref[s, REFL, 1]], axis=1))


def leaf(lib_ref, row_ref, col_ref, code):
    return (
        refl_leaf(lib_ref, code),
        trans_leaf(lib_ref, col_ref, code),
        back_leaf(lib_ref, row_ref, code),
    )


def own_kernel(code_ref, lib_ref, real_ref, imag_ref, nodes_ref, own_ref, row_ref, col_ref):
    cells = code_ref.shape[0]
    spread((real_ref, imag_ref), row_ref, col_ref)

    def cell(i):
        return leaf(lib_ref, row_ref, col_ref, code_ref[i])

    pairs = []
    for j in range(cells // 2):
        pairs.append(merge(cell(2 * j), cell(2 * j + 1)))
        keep_triple(nodes_ref, pairs[j], j)
    fours = []
    for j in range(cells // 4):
        fours.append(merge(pairs[2 * j], pairs[2 * j + 1]))
        keep_triple(nodes_ref, fours[j], cells // 2 + j)
    top = merge(*fours)
    for kind in range(3):
        own_ref[kind] = whole(top[kind])


def scan_kernel(
    code_ref, lib_ref, row_ref, col_ref, nodes_ref, own_ref,
    grown_ref, back_ref, trans_ref,
):
    m = own_ref.shape[1]

    def cell(i):
        return leaf(lib_ref, row_ref, col_ref, code_ref[i])

    def store(ref, i, pair):
        ref[0, i], ref[1, i] = pair

    def put(i, values):
        store(trans_ref, i, values[TRANS])
        store(back_ref, i, values[BACK])
        return values

    def grow(i, refl, before):
        store(grown_ref, i, split(whole(before) + mul(refl, right(before))))

    def trans_of(i):
        return trans_leaf(lib_ref, col_ref, code_ref[i])

    suffix4 = put(4, triple(nodes_ref, 5))
    before2 = get(nodes_ref, 0, TRANS)
    before4 = get(nodes_ref, 4, TRANS)
    suffix2 = put(2, merge(triple(nodes_ref, 1), suffix4))
    suffix3 = put(3, merge(cell(3), suffix4))
    before3 = split(mul(trans_of(2), right(before2)))
    grow(3, suffix3[REFL], before3)
    grow(2, suffix2[REFL], before2)
    grow(4, suffix4[REFL], before4)
    suffix1 = put(1, merge(cell(1), suffix2))
    before6 = split(mul(get(nodes_ref, 2, TRANS), right(before4)))
    suffix6 = put(6, triple(nodes_ref, 3))
    suffix5 = put(5, merge(cell(5), suffix6))
    grow(6, suffix6[REFL], before6)
    before5 = split(mul(trans_of(4), right(before4)))
    before7 = split(mul(trans_of(6), right(before6)))
    grow(5, suffix5[REFL], before5)
    suffix7 = put(7, cell(7))
    grow(7, suffix7[REFL], before7)
    grow(1, suffix1[REFL], trans_of(0))
    store(grown_ref, 0, split(unit(m) + own_ref[REFL]))
    store(trans_ref, 0, split(own_ref[TRANS]))
    store(back_ref, 0, split(own_ref[BACK]))


def far_kernel(
    me_ref, same_ref, other_ref, lib_ref, row_ref, col_ref, own_ref,
    out_ref,
    pairs_ref, fours_ref, acc_ref,
):
    chips, cells = same_ref.shape
    m = own_ref.shape[1]
    chip = me_ref[0] >> 1
    core = me_ref[0] & 1
    right_count = chips - 1 - chip
    right_end = 2 * chip + 2 + (core + 1) * right_count
    left_end = (core + 1) * chip
    out_ref[0:3] = own_ref[...]
    eye = split(unit(m))
    none = (jnp.zeros_like(eye[0]), jnp.zeros_like(eye[0]))
    for side in range(2):
        keep_triple(acc_ref, (none, eye, eye), side)

    def place(i):
        on_right = i < right_count
        return jnp.where(on_right, right_end - 1 - i, left_end - 1 - (i - right_count))

    def pair_step(i, _):
        k = place(i)

        def cell(j):
            same, other = same_ref[k >> 1, j], other_ref[k >> 1, j]
            return leaf(lib_ref, row_ref, col_ref, jnp.where((k & 1) == core, same, other))

        for j in range(cells // 2):
            keep_triple(
                pairs_ref,
                merge(cell(2 * j), cell(2 * j + 1)),
                i,
                j,
            )
        return 0

    lax.fori_loop(0, chips - 1, pair_step, 0)
    for i in range(chips - 1):
        for j in range(cells // 4):
            keep_triple(
                fours_ref, merge(triple(pairs_ref, i, 2 * j), triple(pairs_ref, i, 2 * j + 1)), i, j
            )
    for i in range(chips - 1):
        keep_triple(pairs_ref, merge(triple(fours_ref, i, 0), triple(fours_ref, i, 1)), i, 0)
    for i in range(chips - 1):
        side = jnp.where(i < right_count, 1, 0)
        first = (i == 0) | (i == right_count)

        @pl.when(first)
        def _():
            acc_ref[side] = pairs_ref[i, 0]

        @pl.when(jnp.logical_not(first))
        def _():
            keep_triple(acc_ref, merge(triple(pairs_ref, i, 0), triple(acc_ref, side)), side)

    for side in range(2):
        for kind in range(3):
            out_ref[3 + 3 * side + kind] = whole(get(acc_ref, side, kind))


OWN, LEFT, RIGHT = 0, 3, 6


def sides(me_ref, mine_ref, theirs_ref):
    on_first = (me_ref[0] & 1) == 0

    def first(index):
        return jnp.where(on_first, mine_ref[index], theirs_ref[index])

    def second(index):
        return jnp.where(on_first, theirs_ref[index], mine_ref[index])

    return on_first, first, second


def chain_kernel(me_ref, target_ref, mine_ref, theirs_ref, x_ref, part_ref):
    m = target_ref.shape[1]
    on_first, first, second = sides(me_ref, mine_ref, theirs_ref)
    own0_t = split(first(OWN + TRANS))
    own1_t = split(second(OWN + TRANS))
    own1_tw = right(own1_t)
    far0_tw = right(split(first(RIGHT + TRANS)))
    p_far = mul(split(second(LEFT + TRANS)), right(split(first(LEFT + TRANS))))
    q_far = mul(split(second(RIGHT + TRANS)), far0_tw)
    p_fars, q_fars = split(p_far), split(q_far)
    z = mul(split(first(RIGHT + BACK)), right(split(second(RIGHT + REFL))))
    p_here = mul(own0_t, right(p_fars))
    q_here = mul(q_fars, own1_tw)
    s_far = first(RIGHT + REFL) + mul(split(z), far0_tw)
    total = mul(split(q_here), right(split(p_here)))
    z = mul(split(second(OWN + BACK)), right(split(s_far)))
    miss = jnp.concatenate(
        [(total[:, :m] - target_ref[0]).T, (total[:, m:] - target_ref[1]).T], axis=1
    )
    s_here = second(OWN + REFL) + mul(split(z), own1_tw)
    part_ref[0] = s_here
    part_ref[1] = p_far
    p = split(jnp.where(on_first, p_far, p_here))
    q = split(jnp.where(on_first, q_here, q_far))
    s = split(jnp.where(on_first, s_here, s_far))
    ahead = mul(split(miss), right(q))
    s_block = mul(s, right(split(mine_ref[OWN + TRANS])))
    x1 = right(split(mul(p, right(split(ahead)))))
    x_ref[0, 0], x_ref[0, 1] = x1
    x_ref[1, 0], x_ref[1, 1] = right(split(mul(split(s_block), x1)))


def reflect_kernel(me_ref, mine_ref, theirs_ref, part_ref, out_ref, left_ref):
    rows, m = out_ref.shape[1:]
    _, first, second = sides(me_ref, mine_ref, theirs_ref)
    left_ref[0] = first(LEFT + REFL)
    left_ref[1] = first(LEFT + BACK)
    at = pl.ds(pl.multiple_of(me_ref[0] * rows, rows), rows)
    back = split(left_ref[1, at, :])
    z = mul(split(first(OWN + BACK)), right(split(part_ref[0])))
    refl = first(OWN + REFL) + mul(split(z), right(split(first(OWN + TRANS))))
    z = mul(back, right(split(second(LEFT + REFL))))
    left = left_ref[0, at, :] + mul(split(z), right(split(first(LEFT + TRANS))))
    back = mul(back, right(split(second(LEFT + BACK))))
    z = mul(split(back), right(split(refl)))
    mine = left + mul(split(z), right(split(part_ref[1])))
    out_ref[0] = mine[:, :m]
    out_ref[1] = mine[:, m:]


def coupling_kernel(start, group, x_ref, grown_ref, back_ref, trans_ref, out_ref):
    m = grown_ref.shape[2]
    h = m // 2
    cells = slice(start, start + group)

    def stack(ref):
        return tuple(ref[part, cells].reshape(group * m, 2 * m) for part in range(2))

    row = lax.broadcasted_iota(jnp.int32, (h, m), 0)
    lane = lax.broadcasted_iota(jnp.int32, (h, m), 1)
    use_top = (lane >= h) | (row > lane)
    eye = lax.broadcasted_iota(jnp.int32, (m, m), 0) == lax.broadcasted_iota(jnp.int32, (m, m), 1)
    all_y = mul(stack(grown_ref), (x_ref[0, 0], x_ref[0, 1]))
    all_y = all_y + mul(stack(back_ref), (x_ref[1, 0], x_ref[1, 1]))
    out_ref[group * h :] = jnp.zeros_like(out_ref[group * h :])
    for j in range(group):
        y = all_y[j * m : (j + 1) * m]
        ys = split(jnp.concatenate([y[:, :m], -y[:, m:]], axis=1))
        t = [trans_ref[part, start + j] for part in range(2)]
        c = mul(ys, [jnp.concatenate([a[:, :m], a[:, m:]], axis=0) for a in t])
        both = c + c.T
        low = pltpu.roll(both[h:], h, 1)
        out_ref[j * h : (j + 1) * h] = jnp.where(use_top, both[:h], low)
        out_ref[group * h + j : group * h + j + 1] = jnp.sum(
            jnp.where(eye, c, 0.0), axis=0, keepdims=True
        )


def field_kernel(field_ref, hi_ref, lo_ref):
    for q in range(field_ref.shape[0]):
        hi_ref[q], lo_ref[q] = split(field_ref[q])


def project_kernel(start, group, prof_ref, hi_ref, lo_ref, mine_ref, theirs_ref, *rest):
    out_ref = rest[-1]
    m = hi_ref.shape[1]
    h = m // 2
    if start:
        out_ref[:start] = rest[0][...]
    row = lax.broadcasted_iota(jnp.int32, (h, m), 0)
    lane = lax.broadcasted_iota(jnp.int32, (h, m), 1)
    eye = lax.broadcasted_iota(jnp.int32, (m, m), 0) == lax.broadcasted_iota(jnp.int32, (m, m), 1)
    for j in range(group):
        at = slice(j * h, (j + 1) * h)
        packed = mine_ref[at] + theirs_ref[at]
        at = slice(group * h + j, group * h + j + 1)
        diag = mine_ref[at] + theirs_ref[at]
        top = jnp.where((lane >= h) | (row > lane), packed, 0.0)
        low = pltpu.roll(jnp.where((lane < h) & (row < lane), packed, 0.0), h, 1)
        c = jnp.concatenate([top, low], axis=0) + jnp.where(eye, diag, 0.0)
        ch, cl = split(c)
        q = prof_ref[start + j]
        fh, fl = hi_ref[q], lo_ref[q]
        w = dot(jnp.concatenate([ch, cl], axis=1), jnp.concatenate([fh, fh], axis=0))
        w = w + dot(ch, fl)
        i = start + j
        out_ref[i : i + 1] = jnp.sum(
            (fh.astype(F32) + fl.astype(F32)) * w, axis=0, keepdims=True
        )


def call(kernel, name, kinds, outs, scratch, limit, products, *args):
    def spec(kind):
        return pl.BlockSpec(memory_space=pltpu.SMEM if kind == "s" else pltpu.VMEM)

    several = isinstance(outs, list)
    return pl.pallas_call(
        kernel,
        out_shape=outs,
        in_specs=[spec(kind) for kind in kinds],
        out_specs=[spec("v")] * len(outs) if several else spec("v"),
        scratch_shapes=scratch,
        compiler_params=pltpu.CompilerParams(vmem_limit_bytes=limit * MIB),
        cost_estimate=pl.CostEstimate(
            flops=products * 6 * 8 * 128**3, bytes_accessed=4 * MIB, transcendentals=0
        ),
        name=name,
    )(*args)


def body(interfaces, cell_profile, cell_section, mode_loss, phase, mode_field, target):
    cells = cell_profile.shape[0]
    profiles, m = mode_loss.shape
    blocks = lax.axis_size("cell")
    waves = lax.axis_size("wl")
    pixels = mode_field.shape[2]
    chips = blocks // 2
    angle = phase.reshape(profiles, m)
    factors = (mode_loss * jnp.cos(angle), mode_loss * jnp.sin(angle))
    wanted = target.reshape(2, m, m)
    me = lax.axis_index("cell").astype(jnp.int32).reshape(1)

    def pairs(*lead):
        return (*lead, 2, m, 2 * m)

    def f32(*shape):
        return jax.ShapeDtypeStruct(shape, F32)

    def bf16(*shape):
        return jax.ShapeDtypeStruct(shape, BF16)

    tables = [f32(profiles, 2, 8, m), f32(profiles, 2, m, m)]
    codes = (cell_profile << SHIFT) | cell_section
    same = lax.all_to_all(
        jnp.broadcast_to(codes[None], (chips, cells)), "cell", 0, 0,
        axis_index_groups=[list(range(core, blocks, 2)) for core in range(2)],
    )
    swap = [(i, i ^ 1) for i in range(blocks)]
    other = lax.ppermute(same, "cell", swap)
    nodes, own, row_table, col_table = call(
        own_kernel, "own_tree", "svvv", [bf16(*pairs(6, 3)), f32(3, m, 2 * m), *tables], [], 12, 28,
        codes, interfaces, *factors,
    )
    mine = call(
        far_kernel, "far_trees", "sssvvvv", f32(9, m, 2 * m),
        [
            pltpu.VMEM(pairs(chips - 1, cells // 2, 3), BF16),
            pltpu.VMEM(pairs(chips - 1, cells // 4, 3), BF16),
            pltpu.VMEM(pairs(2, 3), BF16),
        ],
        8 + 3 * blocks // 2, 32 * (chips - 1),
        me, same, other, interfaces, row_table, col_table, own,
    )
    theirs = lax.ppermute(mine, "cell", swap)
    parts_shape = bf16(2, cells, m, 2 * m)
    grown, back, trans = call(
        scan_kernel, "own_scan", "svvvvv", [parts_shape] * 3, [], 16, 27,
        codes, interfaces, row_table, col_table, nodes, own,
    )
    x, part = call(
        chain_kernel, "chain", "svvv", [bf16(2, 2, 2 * m, 2 * m), f32(2, m, 2 * m)], [], 12, 20,
        me, wanted, mine, theirs,
    )
    reflection = call(
        reflect_kernel, "reflection", "svvv", f32(2, m // blocks, m),
        [pltpu.VMEM((2, m, 2 * m), F32)], 12, 10,
        me, mine, theirs, part,
    )

    steps = []
    bit = 1
    while bit < waves:
        steps.append(bit)
        bit *= 2
    orders = (steps, steps[::-1])

    def exchange(part, number):
        pairs_of = [
            (w * blocks + c, (w ^ orders[c & 1][number]) * blocks + c)
            for w in range(waves)
            for c in range(blocks)
        ]
        return lax.ppermute(part, ("wl", "cell"), pairs_of)

    field = bf16(profiles, m, pixels)
    fields = call(field_kernel, "field_parts", "v", [field, field], [], 12, 1, mode_field)
    gradient = []
    start = 0
    for group in (cells - FEWER, FEWER):
        packed = call(
            functools.partial(coupling_kernel, start, group), "couplings", "vvvv",
            f32(group * (m // 2) + 8, m), [], 12, 10,
            x, grown, back, trans,
        )
        other = jnp.zeros_like(packed)
        for number in range(len(steps)):
            if number:
                packed = packed + other
            other = exchange(packed, number)
        gradient = [
            call(
                functools.partial(project_kernel, start, group), "project",
                "svvvv" + "v" * len(gradient), f32(start + group, pixels), [], 12, 4,
                cell_profile, *fields, packed, other, *gradient,
            )
        ]
        start += group
    return reflection[None], gradient[0]


def solution(mesh):
    in_specs = (
        P(),
        P("cell"),
        P("cell"),
        P(),
        P(None, "wl", None),
        P(None, None, "wl"),
        P("wl", None, None, None),
    )
    out_specs = (P("wl", None, "cell", None), P("cell", "wl"))
    return jax.shard_map(body, mesh=mesh, in_specs=in_specs, out_specs=out_specs, check_vma=False)
```

```python
import functools
import jax
import jax.numpy as jnp
from jax import lax
from jax.experimental import pallas as pl
from jax.experimental.pallas import tpu as pltpu
from jax.sharding import PartitionSpec as P

F32 = jnp.float32
BF16 = jnp.bfloat16
MIB = 1024 * 1024
SHIFT = 8
LOW = (1 << SHIFT) - 1
REFL, TRANS, BACK = 0, 1, 2
FEWER = 3


def split(x):
    hi = x.astype(BF16)
    lo = (x - hi.astype(F32)).astype(BF16)
    return hi, lo


def whole(pair):
    return pair[0].astype(F32) + pair[1].astype(F32)


def expand(h):
    m = h.shape[0]
    return jnp.concatenate([h, jnp.concatenate([-h[:, m:], h[:, :m]], axis=1)], axis=0)


def right(pair):
    return expand(pair[0]), expand(pair[1])


def dot(a, b):
    return jnp.dot(a, b, preferred_element_type=F32)


def mul(left, weights):
    hi, lo = left
    return dot(
        jnp.concatenate([hi, lo, hi], axis=1),
        jnp.concatenate([weights[0], weights[0], weights[1]], axis=0),
    )


def get(ref, *at):
    return ref[(*at, 0)], ref[(*at, 1)]


def keep(ref, pair, *at):
    ref[(*at, 0)], ref[(*at, 1)] = pair


def unit(m):
    row = lax.broadcasted_iota(jnp.int32, (m, 2 * m), 0)
    col = lax.broadcasted_iota(jnp.int32, (m, 2 * m), 1)
    return jnp.where(row == col, 1.0, 0.0).astype(F32)


def merge(former, latter):
    r1, t1, b1 = former
    r2, t2, b2 = latter
    t1w = right(t1)
    z = mul(b1, right(r2))
    back = mul(b1, right(b2))
    trans = mul(t2, t1w)
    refl = whole(r1) + mul(split(z), t1w)
    return split(refl), split(trans), split(back)


def triple(ref, *at):
    return tuple(get(ref, *at, kind) for kind in range(3))


def keep_triple(ref, values, *at):
    for kind in range(3):
        keep(ref, values[kind], *at, kind)


def spread(factor_refs, row_ref, col_ref):
    for part, ref in enumerate(factor_refs):
        profiles, m = ref.shape
        for q in range(profiles):
            wide = jnp.broadcast_to(ref[q : q + 1], (m, m))
            row_ref[q, part] = wide[:8]
            col_ref[q, part] = wide.T


def trans_leaf(lib_ref, col_ref, code):
    q, s = code >> SHIFT, code & LOW
    re, im = lib_ref[s, TRANS, 0], lib_ref[s, TRANS, 1]
    cr, ci = col_ref[q, 0], col_ref[q, 1]
    return split(jnp.concatenate([cr * re - ci * im, cr * im + ci * re], axis=1))


def back_leaf(lib_ref, row_ref, code):
    q, s = code >> SHIFT, code & LOW
    re, im = lib_ref[s, BACK, 0], lib_ref[s, BACK, 1]
    rr, ri = row_ref[q, 0][:1], row_ref[q, 1][:1]
    return split(jnp.concatenate([re * rr - im * ri, re * ri + im * rr], axis=1))


def refl_leaf(lib_ref, code):
    s = code & LOW
    return split(jnp.concatenate([lib_ref[s, REFL, 0], lib_ref[s, REFL, 1]], axis=1))


def leaf(lib_ref, row_ref, col_ref, code):
    return (
        refl_leaf(lib_ref, code),
        trans_leaf(lib_ref, col_ref, code),
        back_leaf(lib_ref, row_ref, code),
    )


def own_kernel(code_ref, lib_ref, real_ref, imag_ref, nodes_ref, own_ref, row_ref, col_ref):
    cells = code_ref.shape[0]
    spread((real_ref, imag_ref), row_ref, col_ref)

    def cell(i):
        return leaf(lib_ref, row_ref, col_ref, code_ref[i])

    pairs = []
    for j in range(cells // 2):
        pairs.append(merge(cell(2 * j), cell(2 * j + 1)))
        keep_triple(nodes_ref, pairs[j], j)
    fours = []
    for j in range(cells // 4):
        fours.append(merge(pairs[2 * j], pairs[2 * j + 1]))
        keep_triple(nodes_ref, fours[j], cells // 2 + j)
    top = merge(*fours)
    for kind in range(3):
        own_ref[kind] = whole(top[kind])


def scan_kernel(
    code_ref, lib_ref, row_ref, col_ref, nodes_ref, own_ref,
    grown_ref, back_ref, trans_ref,
):
    m = own_ref.shape[1]

    def cell(i):
        return leaf(lib_ref, row_ref, col_ref, code_ref[i])

    def store(ref, i, pair):
        ref[0, i], ref[1, i] = pair

    def put(i, values):
        store(trans_ref, i, values[TRANS])
        store(back_ref, i, values[BACK])
        return values

    def grow(i, refl, before):
        store(grown_ref, i, split(whole(before) + mul(refl, right(before))))

    def trans_of(i):
        return trans_leaf(lib_ref, col_ref, code_ref[i])

    suffix4 = put(4, triple(nodes_ref, 5))
    before2 = get(nodes_ref, 0, TRANS)
    before4 = get(nodes_ref, 4, TRANS)
    suffix2 = put(2, merge(triple(nodes_ref, 1), suffix4))
    suffix3 = put(3, merge(cell(3), suffix4))
    before3 = split(mul(trans_of(2), right(before2)))
    grow(3, suffix3[REFL], before3)
    grow(2, suffix2[REFL], before2)
    grow(4, suffix4[REFL], before4)
    suffix1 = put(1, merge(cell(1), suffix2))
    before6 = split(mul(get(nodes_ref, 2, TRANS), right(before4)))
    suffix6 = put(6, triple(nodes_ref, 3))
    suffix5 = put(5, merge(cell(5), suffix6))
    grow(6, suffix6[REFL], before6)
    before5 = split(mul(trans_of(4), right(before4)))
    before7 = split(mul(trans_of(6), right(before6)))
    grow(5, suffix5[REFL], before5)
    suffix7 = put(7, cell(7))
    grow(7, suffix7[REFL], before7)
    grow(1, suffix1[REFL], trans_of(0))
    store(grown_ref, 0, split(unit(m) + own_ref[REFL]))
    store(trans_ref, 0, split(own_ref[TRANS]))
    store(back_ref, 0, split(own_ref[BACK]))


def far_core(chip, block, chips):
    if block < 2 * chip:
        return int(block >= chip)
    return int(block >= 2 * chip + 2 + chips - 1 - chip)


def routes(chips):
    blocks = 2 * chips
    wanted = [
        {2 * chip + far_core(chip, block, chips) for chip in range(chips) if chip != block // 2}
        for block in range(blocks)
    ]
    found = []
    for _ in range(chips - 1):
        source = [None] * blocks

        def place(block, seen):
            for device in sorted(wanted[block] - seen):
                seen.add(device)
                if source[device] is None or place(source[device], seen):
                    source[device] = block
                    return True
            return False

        for block in range(blocks):
            place(block, set())
        for device, block in enumerate(source):
            wanted[block].discard(device)
        found.append(source)
    return found


def far_kernel(*refs):
    me_ref, *got_refs = refs[:-9]
    lib_ref, row_ref, col_ref, own_ref, out_ref, code_ref, pairs_ref, fours_ref, acc_ref = refs[-9:]
    blocks, cells = code_ref.shape
    chips = blocks // 2
    m = own_ref.shape[1]
    for ref, source in zip(got_refs, routes(chips)):
        k = source[0]
        for device in range(1, blocks):
            k = jnp.where(me_ref[0] == device, source[device], k)
        for i in range(cells):
            code_ref[k, i] = ref[i]
    chip = me_ref[0] >> 1
    core = me_ref[0] & 1
    right_count = chips - 1 - chip
    right_end = 2 * chip + 2 + (core + 1) * right_count
    left_end = (core + 1) * chip
    out_ref[0:3] = own_ref[...]
    eye = split(unit(m))
    none = (jnp.zeros_like(eye[0]), jnp.zeros_like(eye[0]))
    for side in range(2):
        keep_triple(acc_ref, (none, eye, eye), side)

    def place(i):
        on_right = i < right_count
        return jnp.where(on_right, right_end - 1 - i, left_end - 1 - (i - right_count))

    def pair_step(i, _):
        k = place(i)

        def cell(j):
            return leaf(lib_ref, row_ref, col_ref, code_ref[k, j])

        for j in range(cells // 2):
            keep_triple(
                pairs_ref,
                merge(cell(2 * j), cell(2 * j + 1)),
                i,
                j,
            )
        return 0

    lax.fori_loop(0, chips - 1, pair_step, 0)
    for i in range(chips - 1):
        for j in range(cells // 4):
            keep_triple(
                fours_ref, merge(triple(pairs_ref, i, 2 * j), triple(pairs_ref, i, 2 * j + 1)), i, j
            )
    for i in range(chips - 1):
        keep_triple(pairs_ref, merge(triple(fours_ref, i, 0), triple(fours_ref, i, 1)), i, 0)
    for i in range(chips - 1):
        side = jnp.where(i < right_count, 1, 0)
        first = (i == 0) | (i == right_count)

        @pl.when(first)
        def _():
            acc_ref[side] = pairs_ref[i, 0]

        @pl.when(jnp.logical_not(first))
        def _():
            keep_triple(acc_ref, merge(triple(pairs_ref, i, 0), triple(acc_ref, side)), side)

    for side in range(2):
        for kind in range(3):
            out_ref[3 + 3 * side + kind] = whole(get(acc_ref, side, kind))


OWN, LEFT, RIGHT = 0, 3, 6


def sides(me_ref, mine_ref, theirs_ref):
    on_first = (me_ref[0] & 1) == 0

    def first(index):
        return jnp.where(on_first, mine_ref[index], theirs_ref[index])

    def second(index):
        return jnp.where(on_first, theirs_ref[index], mine_ref[index])

    return on_first, first, second


def chain_kernel(me_ref, target_ref, mine_ref, theirs_ref, x_ref, part_ref):
    m = target_ref.shape[1]
    on_first, first, second = sides(me_ref, mine_ref, theirs_ref)
    own0_t = split(first(OWN + TRANS))
    own1_t = split(second(OWN + TRANS))
    own1_tw = right(own1_t)
    far0_tw = right(split(first(RIGHT + TRANS)))
    p_far = mul(split(second(LEFT + TRANS)), right(split(first(LEFT + TRANS))))
    q_far = mul(split(second(RIGHT + TRANS)), far0_tw)
    p_fars, q_fars = split(p_far), split(q_far)
    z = mul(split(first(RIGHT + BACK)), right(split(second(RIGHT + REFL))))
    p_here = mul(own0_t, right(p_fars))
    q_here = mul(q_fars, own1_tw)
    s_far = first(RIGHT + REFL) + mul(split(z), far0_tw)
    total = mul(split(q_here), right(split(p_here)))
    z = mul(split(second(OWN + BACK)), right(split(s_far)))
    miss = jnp.concatenate(
        [(total[:, :m] - target_ref[0]).T, (total[:, m:] - target_ref[1]).T], axis=1
    )
    s_here = second(OWN + REFL) + mul(split(z), own1_tw)
    part_ref[0] = s_here
    part_ref[1] = p_far
    p = split(jnp.where(on_first, p_far, p_here))
    q = split(jnp.where(on_first, q_here, q_far))
    s = split(jnp.where(on_first, s_here, s_far))
    ahead = mul(split(miss), right(q))
    s_block = mul(s, right(split(mine_ref[OWN + TRANS])))
    x1 = right(split(mul(p, right(split(ahead)))))
    x_ref[0, 0], x_ref[0, 1] = x1
    x_ref[1, 0], x_ref[1, 1] = right(split(mul(split(s_block), x1)))


def reflect_kernel(me_ref, mine_ref, theirs_ref, part_ref, out_ref, left_ref):
    rows, m = out_ref.shape[1:]
    _, first, second = sides(me_ref, mine_ref, theirs_ref)
    left_ref[0] = first(LEFT + REFL)
    left_ref[1] = first(LEFT + BACK)
    at = pl.ds(pl.multiple_of(me_ref[0] * rows, rows), rows)
    back = split(left_ref[1, at, :])
    z = mul(split(first(OWN + BACK)), right(split(part_ref[0])))
    refl = first(OWN + REFL) + mul(split(z), right(split(first(OWN + TRANS))))
    z = mul(back, right(split(second(LEFT + REFL))))
    left = left_ref[0, at, :] + mul(split(z), right(split(first(LEFT + TRANS))))
    back = mul(back, right(split(second(LEFT + BACK))))
    z = mul(split(back), right(split(refl)))
    mine = left + mul(split(z), right(split(part_ref[1])))
    out_ref[0] = mine[:, :m]
    out_ref[1] = mine[:, m:]


def coupling_kernel(start, group, x_ref, grown_ref, back_ref, trans_ref, out_ref):
    m = grown_ref.shape[2]
    h = m // 2
    cells = slice(start, start + group)

    def stack(ref):
        return tuple(ref[part, cells].reshape(group * m, 2 * m) for part in range(2))

    row = lax.broadcasted_iota(jnp.int32, (h, m), 0)
    lane = lax.broadcasted_iota(jnp.int32, (h, m), 1)
    use_top = (lane >= h) | (row > lane)
    eye = lax.broadcasted_iota(jnp.int32, (m, m), 0) == lax.broadcasted_iota(jnp.int32, (m, m), 1)
    all_y = mul(stack(grown_ref), (x_ref[0, 0], x_ref[0, 1]))
    all_y = all_y + mul(stack(back_ref), (x_ref[1, 0], x_ref[1, 1]))
    out_ref[group * h :] = jnp.zeros_like(out_ref[group * h :])
    for j in range(group):
        y = all_y[j * m : (j + 1) * m]
        ys = split(jnp.concatenate([y[:, :m], -y[:, m:]], axis=1))
        t = [trans_ref[part, start + j] for part in range(2)]
        c = mul(ys, [jnp.concatenate([a[:, :m], a[:, m:]], axis=0) for a in t])
        both = c + c.T
        low = pltpu.roll(both[h:], h, 1)
        out_ref[j * h : (j + 1) * h] = jnp.where(use_top, both[:h], low)
        out_ref[group * h + j : group * h + j + 1] = jnp.sum(
            jnp.where(eye, c, 0.0), axis=0, keepdims=True
        )


def field_kernel(field_ref, hi_ref, lo_ref):
    for q in range(field_ref.shape[0]):
        hi_ref[q], lo_ref[q] = split(field_ref[q])


def project_kernel(start, group, prof_ref, hi_ref, lo_ref, mine_ref, theirs_ref, *rest):
    out_ref = rest[-1]
    m = hi_ref.shape[1]
    h = m // 2
    if start:
        out_ref[:start] = rest[0][...]
    row = lax.broadcasted_iota(jnp.int32, (h, m), 0)
    lane = lax.broadcasted_iota(jnp.int32, (h, m), 1)
    eye = lax.broadcasted_iota(jnp.int32, (m, m), 0) == lax.broadcasted_iota(jnp.int32, (m, m), 1)
    for j in range(group):
        at = slice(j * h, (j + 1) * h)
        packed = mine_ref[at] + theirs_ref[at]
        at = slice(group * h + j, group * h + j + 1)
        diag = mine_ref[at] + theirs_ref[at]
        top = jnp.where((lane >= h) | (row > lane), packed, 0.0)
        low = pltpu.roll(jnp.where((lane < h) & (row < lane), packed, 0.0), h, 1)
        c = jnp.concatenate([top, low], axis=0) + jnp.where(eye, diag, 0.0)
        ch, cl = split(c)
        q = prof_ref[start + j]
        fh, fl = hi_ref[q], lo_ref[q]
        w = dot(jnp.concatenate([ch, cl], axis=1), jnp.concatenate([fh, fh], axis=0))
        w = w + dot(ch, fl)
        i = start + j
        out_ref[i : i + 1] = jnp.sum(
            (fh.astype(F32) + fl.astype(F32)) * w, axis=0, keepdims=True
        )


def call(kernel, name, kinds, outs, scratch, limit, products, *args):
    def spec(kind):
        return pl.BlockSpec(memory_space=pltpu.SMEM if kind == "s" else pltpu.VMEM)

    several = isinstance(outs, list)
    return pl.pallas_call(
        kernel,
        out_shape=outs,
        in_specs=[spec(kind) for kind in kinds],
        out_specs=[spec("v")] * len(outs) if several else spec("v"),
        scratch_shapes=scratch,
        compiler_params=pltpu.CompilerParams(vmem_limit_bytes=limit * MIB),
        cost_estimate=pl.CostEstimate(
            flops=products * 6 * 8 * 128**3, bytes_accessed=4 * MIB, transcendentals=0
        ),
        name=name,
    )(*args)


def body(interfaces, cell_profile, cell_section, mode_loss, phase, mode_field, target):
    cells = cell_profile.shape[0]
    profiles, m = mode_loss.shape
    blocks = lax.axis_size("cell")
    waves = lax.axis_size("wl")
    pixels = mode_field.shape[2]
    chips = blocks // 2
    angle = phase.reshape(profiles, m)
    factors = (mode_loss * jnp.cos(angle), mode_loss * jnp.sin(angle))
    wanted = target.reshape(2, m, m)
    me = lax.axis_index("cell").astype(jnp.int32).reshape(1)

    def pairs(*lead):
        return (*lead, 2, m, 2 * m)

    def f32(*shape):
        return jax.ShapeDtypeStruct(shape, F32)

    def bf16(*shape):
        return jax.ShapeDtypeStruct(shape, BF16)

    tables = [f32(profiles, 2, 8, m), f32(profiles, 2, m, m)]
    codes = (cell_profile << SHIFT) | cell_section
    got = [
        lax.ppermute(codes, "cell", [(block, device) for device, block in enumerate(source)])
        for source in routes(chips)
    ]
    nodes, own, row_table, col_table = call(
        own_kernel, "own_tree", "svvv", [bf16(*pairs(6, 3)), f32(3, m, 2 * m), *tables], [], 12, 28,
        codes, interfaces, *factors,
    )
    mine = call(
        far_kernel, "far_trees", "s" * chips + "vvvv", f32(9, m, 2 * m),
        [
            pltpu.SMEM((blocks, cells), jnp.int32),
            pltpu.VMEM(pairs(chips - 1, cells // 2, 3), BF16),
            pltpu.VMEM(pairs(chips - 1, cells // 4, 3), BF16),
            pltpu.VMEM(pairs(2, 3), BF16),
        ],
        8 + 3 * blocks // 2, 32 * (chips - 1),
        me, *got, interfaces, row_table, col_table, own,
    )
    theirs = lax.ppermute(mine, "cell", [(i, i ^ 1) for i in range(blocks)])
    parts_shape = bf16(2, cells, m, 2 * m)
    grown, back, trans = call(
        scan_kernel, "own_scan", "svvvvv", [parts_shape] * 3, [], 16, 27,
        codes, interfaces, row_table, col_table, nodes, own,
    )
    x, part = call(
        chain_kernel, "chain", "svvv", [bf16(2, 2, 2 * m, 2 * m), f32(2, m, 2 * m)], [], 12, 20,
        me, wanted, mine, theirs,
    )
    reflection = call(
        reflect_kernel, "reflection", "svvv", f32(2, m // blocks, m),
        [pltpu.VMEM((2, m, 2 * m), F32)], 12, 10,
        me, mine, theirs, part,
    )

    steps = []
    bit = 1
    while bit < waves:
        steps.append(bit)
        bit *= 2
    orders = (steps, steps[::-1])

    def exchange(part, number):
        pairs_of = [
            (w * blocks + c, (w ^ orders[c & 1][number]) * blocks + c)
            for w in range(waves)
            for c in range(blocks)
        ]
        return lax.ppermute(part, ("wl", "cell"), pairs_of)

    field = bf16(profiles, m, pixels)
    fields = call(field_kernel, "field_parts", "v", [field, field], [], 12, 1, mode_field)
    gradient = []
    start = 0
    for group in (cells - FEWER, FEWER):
        packed = call(
            functools.partial(coupling_kernel, start, group), "couplings", "vvvv",
            f32(group * (m // 2) + 8, m), [], 12, 10,
            x, grown, back, trans,
        )
        other = jnp.zeros_like(packed)
        for number in range(len(steps)):
            if number:
                packed = packed + other
            other = exchange(packed, number)
        gradient = [
            call(
                functools.partial(project_kernel, start, group), "project",
                "svvvv" + "v" * len(gradient), f32(start + group, pixels), [], 12, 4,
                cell_profile, *fields, packed, other, *gradient,
            )
        ]
        start += group
    return reflection[None], gradient[0]


def solution(mesh):
    in_specs = (
        P(),
        P("cell"),
        P("cell"),
        P(),
        P(None, "wl", None),
        P(None, None, "wl"),
        P("wl", None, None, None),
    )
    out_specs = (P("wl", None, "cell", None), P("cell", "wl"))
    return jax.shard_map(body, mesh=mesh, in_specs=in_specs, out_specs=out_specs, check_vma=False)
```

```python
import functools
import jax
import jax.numpy as jnp
from jax import lax
from jax.experimental import pallas as pl
from jax.experimental.pallas import tpu as pltpu
from jax.sharding import PartitionSpec as P

F32 = jnp.float32
BF16 = jnp.bfloat16
MIB = 1024 * 1024
SHIFT = 8
LOW = (1 << SHIFT) - 1
REFL, TRANS, BACK = 0, 1, 2
FEWER = 3


def split(x):
    hi = x.astype(BF16)
    lo = (x - hi.astype(F32)).astype(BF16)
    return hi, lo


def whole(pair):
    return pair[0].astype(F32) + pair[1].astype(F32)


def expand(h):
    m = h.shape[0]
    return jnp.concatenate([h, jnp.concatenate([-h[:, m:], h[:, :m]], axis=1)], axis=0)


def right(pair):
    return expand(pair[0]), expand(pair[1])


def dot(a, b):
    return jnp.dot(a, b, preferred_element_type=F32)


def deep(left):
    return jnp.concatenate([left[0], left[1], left[0]], axis=1)


def tall(weights):
    return jnp.concatenate([weights[0], weights[0], weights[1]], axis=0)


def mul(left, weights):
    return dot(deep(left), tall(weights))


def get(ref, *at):
    return ref[(*at, 0)], ref[(*at, 1)]


def keep(ref, pair, *at):
    ref[(*at, 0)], ref[(*at, 1)] = pair


def unit(m):
    row = lax.broadcasted_iota(jnp.int32, (m, 2 * m), 0)
    col = lax.broadcasted_iota(jnp.int32, (m, 2 * m), 1)
    return jnp.where(row == col, 1.0, 0.0).astype(F32)


def merge(former, latter):
    r1, t1, b1 = former
    r2, t2, b2 = latter
    m = t1[0].shape[0]
    t1w = tall(right(t1))
    both = dot(deep(b1), jnp.concatenate([tall(right(r2)), tall(right(b2))], axis=1))
    trans = dot(deep(t2), t1w)
    refl = whole(r1) + dot(deep(split(both[:, : 2 * m])), t1w)
    return split(refl), split(trans), split(both[:, 2 * m :])


def triple(ref, *at):
    return tuple(get(ref, *at, kind) for kind in range(3))


def keep_triple(ref, values, *at):
    for kind in range(3):
        keep(ref, values[kind], *at, kind)


def spread(factor_refs, row_ref, col_ref):
    for part, ref in enumerate(factor_refs):
        profiles, m = ref.shape
        for q in range(profiles):
            wide = jnp.broadcast_to(ref[q : q + 1], (m, m))
            row_ref[q, part] = wide[:8]
            col_ref[q, part] = wide.T


def trans_leaf(lib_ref, col_ref, code):
    q, s = code >> SHIFT, code & LOW
    re, im = lib_ref[s, TRANS, 0], lib_ref[s, TRANS, 1]
    cr, ci = col_ref[q, 0], col_ref[q, 1]
    return split(jnp.concatenate([cr * re - ci * im, cr * im + ci * re], axis=1))


def back_leaf(lib_ref, row_ref, code):
    q, s = code >> SHIFT, code & LOW
    re, im = lib_ref[s, BACK, 0], lib_ref[s, BACK, 1]
    rr, ri = row_ref[q, 0][:1], row_ref[q, 1][:1]
    return split(jnp.concatenate([re * rr - im * ri, re * ri + im * rr], axis=1))


def refl_leaf(lib_ref, code):
    s = code & LOW
    return split(jnp.concatenate([lib_ref[s, REFL, 0], lib_ref[s, REFL, 1]], axis=1))


def leaf(lib_ref, row_ref, col_ref, code):
    return (
        refl_leaf(lib_ref, code),
        trans_leaf(lib_ref, col_ref, code),
        back_leaf(lib_ref, row_ref, code),
    )


def own_kernel(code_ref, lib_ref, real_ref, imag_ref, nodes_ref, own_ref, row_ref, col_ref):
    cells = code_ref.shape[0]
    spread((real_ref, imag_ref), row_ref, col_ref)

    def cell(i):
        return leaf(lib_ref, row_ref, col_ref, code_ref[i])

    pairs = []
    for j in range(cells // 2):
        pairs.append(merge(cell(2 * j), cell(2 * j + 1)))
        keep_triple(nodes_ref, pairs[j], j)
    fours = []
    for j in range(cells // 4):
        fours.append(merge(pairs[2 * j], pairs[2 * j + 1]))
        keep_triple(nodes_ref, fours[j], cells // 2 + j)
    top = merge(*fours)
    for kind in range(3):
        own_ref[kind] = whole(top[kind])


def scan_kernel(
    code_ref, lib_ref, row_ref, col_ref, nodes_ref, own_ref,
    grown_ref, back_ref, trans_ref,
):
    m = own_ref.shape[1]

    def cell(i):
        return leaf(lib_ref, row_ref, col_ref, code_ref[i])

    def store(ref, i, pair):
        ref[0, i], ref[1, i] = pair

    def put(i, values):
        store(trans_ref, i, values[TRANS])
        store(back_ref, i, values[BACK])
        return values

    def grow(i, refl, before):
        store(grown_ref, i, split(whole(before) + mul(refl, right(before))))

    def trans_of(i):
        return trans_leaf(lib_ref, col_ref, code_ref[i])

    suffix4 = put(4, triple(nodes_ref, 5))
    before2 = get(nodes_ref, 0, TRANS)
    before4 = get(nodes_ref, 4, TRANS)
    suffix2 = put(2, merge(triple(nodes_ref, 1), suffix4))
    suffix3 = put(3, merge(cell(3), suffix4))
    before3 = split(mul(trans_of(2), right(before2)))
    grow(3, suffix3[REFL], before3)
    grow(2, suffix2[REFL], before2)
    grow(4, suffix4[REFL], before4)
    suffix1 = put(1, merge(cell(1), suffix2))
    before6 = split(mul(get(nodes_ref, 2, TRANS), right(before4)))
    suffix6 = put(6, triple(nodes_ref, 3))
    suffix5 = put(5, merge(cell(5), suffix6))
    grow(6, suffix6[REFL], before6)
    before5 = split(mul(trans_of(4), right(before4)))
    before7 = split(mul(trans_of(6), right(before6)))
    grow(5, suffix5[REFL], before5)
    suffix7 = put(7, cell(7))
    grow(7, suffix7[REFL], before7)
    grow(1, suffix1[REFL], trans_of(0))
    store(grown_ref, 0, split(unit(m) + own_ref[REFL]))
    store(trans_ref, 0, split(own_ref[TRANS]))
    store(back_ref, 0, split(own_ref[BACK]))


def far_core(chip, block, chips):
    if block < 2 * chip:
        return int(block >= chip)
    return int(block >= 2 * chip + 2 + chips - 1 - chip)


def routes(chips):
    blocks = 2 * chips
    wanted = [
        {2 * chip + far_core(chip, block, chips) for chip in range(chips) if chip != block // 2}
        for block in range(blocks)
    ]
    found = []
    for _ in range(chips - 1):
        source = [None] * blocks

        def place(block, seen):
            for device in sorted(wanted[block] - seen):
                seen.add(device)
                if source[device] is None or place(source[device], seen):
                    source[device] = block
                    return True
            return False

        for block in range(blocks):
            place(block, set())
        for device, block in enumerate(source):
            wanted[block].discard(device)
        found.append(source)
    return found


def far_kernel(*refs):
    me_ref, *got_refs = refs[:-9]
    lib_ref, row_ref, col_ref, own_ref, out_ref, code_ref, pairs_ref, fours_ref, acc_ref = refs[-9:]
    blocks, cells = code_ref.shape
    chips = blocks // 2
    m = own_ref.shape[1]
    for ref, source in zip(got_refs, routes(chips)):
        k = source[0]
        for device in range(1, blocks):
            k = jnp.where(me_ref[0] == device, source[device], k)
        for i in range(cells):
            code_ref[k, i] = ref[i]
    chip = me_ref[0] >> 1
    core = me_ref[0] & 1
    right_count = chips - 1 - chip
    right_end = 2 * chip + 2 + (core + 1) * right_count
    left_end = (core + 1) * chip
    out_ref[0:3] = own_ref[...]
    eye = split(unit(m))
    none = (jnp.zeros_like(eye[0]), jnp.zeros_like(eye[0]))
    for side in range(2):
        keep_triple(acc_ref, (none, eye, eye), side)

    def place(i):
        on_right = i < right_count
        return jnp.where(on_right, right_end - 1 - i, left_end - 1 - (i - right_count))

    def pair_step(i, _):
        k = place(i)

        def cell(j):
            return leaf(lib_ref, row_ref, col_ref, code_ref[k, j])

        for j in range(cells // 2):
            keep_triple(
                pairs_ref,
                merge(cell(2 * j), cell(2 * j + 1)),
                i,
                j,
            )
        return 0

    if chips <= 4:
        for i in range(chips - 1):
            pair_step(i, 0)
    else:
        lax.fori_loop(0, chips - 1, pair_step, 0)
    for i in range(chips - 1):
        for j in range(cells // 4):
            keep_triple(
                fours_ref, merge(triple(pairs_ref, i, 2 * j), triple(pairs_ref, i, 2 * j + 1)), i, j
            )
    for i in range(chips - 1):
        keep_triple(pairs_ref, merge(triple(fours_ref, i, 0), triple(fours_ref, i, 1)), i, 0)
    for i in range(chips - 1):
        side = jnp.where(i < right_count, 1, 0)
        first = (i == 0) | (i == right_count)

        @pl.when(first)
        def _():
            acc_ref[side] = pairs_ref[i, 0]

        @pl.when(jnp.logical_not(first))
        def _():
            keep_triple(acc_ref, merge(triple(pairs_ref, i, 0), triple(acc_ref, side)), side)

    for side in range(2):
        for kind in range(3):
            out_ref[3 + 3 * side + kind] = whole(get(acc_ref, side, kind))


OWN, LEFT, RIGHT = 0, 3, 6


def sides(me_ref, mine_ref, theirs_ref):
    on_first = (me_ref[0] & 1) == 0

    def first(index):
        return jnp.where(on_first, mine_ref[index], theirs_ref[index])

    def second(index):
        return jnp.where(on_first, theirs_ref[index], mine_ref[index])

    return on_first, first, second


def chain_kernel(me_ref, target_ref, mine_ref, theirs_ref, x_ref, part_ref):
    m = target_ref.shape[1]
    on_first, first, second = sides(me_ref, mine_ref, theirs_ref)
    own0_t = split(first(OWN + TRANS))
    own1_t = split(second(OWN + TRANS))
    own1_tw = right(own1_t)
    far0_tw = right(split(first(RIGHT + TRANS)))
    p_far = mul(split(second(LEFT + TRANS)), right(split(first(LEFT + TRANS))))
    q_far = mul(split(second(RIGHT + TRANS)), far0_tw)
    p_fars, q_fars = split(p_far), split(q_far)
    z = mul(split(first(RIGHT + BACK)), right(split(second(RIGHT + REFL))))
    p_here = mul(own0_t, right(p_fars))
    q_here = mul(q_fars, own1_tw)
    s_far = first(RIGHT + REFL) + mul(split(z), far0_tw)
    total = mul(split(q_here), right(split(p_here)))
    z = mul(split(second(OWN + BACK)), right(split(s_far)))
    miss = jnp.concatenate(
        [(total[:, :m] - target_ref[0]).T, (total[:, m:] - target_ref[1]).T], axis=1
    )
    s_here = second(OWN + REFL) + mul(split(z), own1_tw)
    part_ref[0] = s_here
    part_ref[1] = p_far
    p = split(jnp.where(on_first, p_far, p_here))
    q = split(jnp.where(on_first, q_here, q_far))
    s = split(jnp.where(on_first, s_here, s_far))
    ahead = mul(split(miss), right(q))
    s_block = mul(s, right(split(mine_ref[OWN + TRANS])))
    x1 = right(split(mul(p, right(split(ahead)))))
    x_ref[0, 0], x_ref[0, 1] = x1
    x_ref[1, 0], x_ref[1, 1] = right(split(mul(split(s_block), x1)))


def reflect_kernel(me_ref, mine_ref, theirs_ref, part_ref, out_ref, left_ref):
    rows, m = out_ref.shape[1:]
    _, first, second = sides(me_ref, mine_ref, theirs_ref)
    left_ref[0] = first(LEFT + REFL)
    left_ref[1] = first(LEFT + BACK)
    at = pl.ds(pl.multiple_of(me_ref[0] * rows, rows), rows)
    back = split(left_ref[1, at, :])
    z = mul(split(first(OWN + BACK)), right(split(part_ref[0])))
    refl = first(OWN + REFL) + mul(split(z), right(split(first(OWN + TRANS))))
    z = mul(back, right(split(second(LEFT + REFL))))
    left = left_ref[0, at, :] + mul(split(z), right(split(first(LEFT + TRANS))))
    back = mul(back, right(split(second(LEFT + BACK))))
    z = mul(split(back), right(split(refl)))
    mine = left + mul(split(z), right(split(part_ref[1])))
    out_ref[0] = mine[:, :m]
    out_ref[1] = mine[:, m:]


def coupling_kernel(start, group, x_ref, grown_ref, back_ref, trans_ref, out_ref):
    m = grown_ref.shape[2]
    h = m // 2
    cells = slice(start, start + group)

    def stack(ref):
        return tuple(ref[part, cells].reshape(group * m, 2 * m) for part in range(2))

    row = lax.broadcasted_iota(jnp.int32, (h, m), 0)
    lane = lax.broadcasted_iota(jnp.int32, (h, m), 1)
    use_top = (lane >= h) | (row > lane)
    eye = lax.broadcasted_iota(jnp.int32, (m, m), 0) == lax.broadcasted_iota(jnp.int32, (m, m), 1)
    all_y = mul(stack(grown_ref), (x_ref[0, 0], x_ref[0, 1]))
    all_y = all_y + mul(stack(back_ref), (x_ref[1, 0], x_ref[1, 1]))
    out_ref[group * h :] = jnp.zeros_like(out_ref[group * h :])
    for j in range(group):
        y = all_y[j * m : (j + 1) * m]
        ys = split(jnp.concatenate([y[:, :m], -y[:, m:]], axis=1))
        t = [trans_ref[part, start + j] for part in range(2)]
        c = mul(ys, [jnp.concatenate([a[:, :m], a[:, m:]], axis=0) for a in t])
        both = c + c.T
        low = pltpu.roll(both[h:], h, 1)
        out_ref[j * h : (j + 1) * h] = jnp.where(use_top, both[:h], low)
        out_ref[group * h + j : group * h + j + 1] = jnp.sum(
            jnp.where(eye, c, 0.0), axis=0, keepdims=True
        )


def first_kernel(
    group, me_ref, target_ref, mine_ref, theirs_ref, grown_ref, back_ref, trans_ref,
    x_ref, part_ref, out_ref,
):
    chain_kernel(me_ref, target_ref, mine_ref, theirs_ref, x_ref, part_ref)
    coupling_kernel(0, group, x_ref, grown_ref, back_ref, trans_ref, out_ref)


def field_kernel(field_ref, hi_ref, lo_ref):
    for q in range(field_ref.shape[0]):
        hi_ref[q], lo_ref[q] = split(field_ref[q])


def project_kernel(start, group, prof_ref, hi_ref, lo_ref, mine_ref, theirs_ref, *rest):
    out_ref = rest[-1]
    m = hi_ref.shape[1]
    h = m // 2
    if start:
        out_ref[:start] = rest[0][...]
    row = lax.broadcasted_iota(jnp.int32, (h, m), 0)
    lane = lax.broadcasted_iota(jnp.int32, (h, m), 1)
    eye = lax.broadcasted_iota(jnp.int32, (m, m), 0) == lax.broadcasted_iota(jnp.int32, (m, m), 1)
    for j in range(group):
        at = slice(j * h, (j + 1) * h)
        packed = mine_ref[at] + theirs_ref[at]
        at = slice(group * h + j, group * h + j + 1)
        diag = mine_ref[at] + theirs_ref[at]
        top = jnp.where((lane >= h) | (row > lane), packed, 0.0)
        low = pltpu.roll(jnp.where((lane < h) & (row < lane), packed, 0.0), h, 1)
        c = jnp.concatenate([top, low], axis=0) + jnp.where(eye, diag, 0.0)
        ch, cl = split(c)
        q = prof_ref[start + j]
        fh, fl = hi_ref[q], lo_ref[q]
        both = dot(jnp.concatenate([ch, cl], axis=0), fh)
        w = both[:m] + both[m:] + dot(ch, fl)
        i = start + j
        out_ref[i : i + 1] = jnp.sum(
            (fh.astype(F32) + fl.astype(F32)) * w, axis=0, keepdims=True
        )


def call(kernel, name, kinds, outs, scratch, limit, products, *args):
    def spec(kind):
        return pl.BlockSpec(memory_space=pltpu.SMEM if kind == "s" else pltpu.VMEM)

    several = isinstance(outs, list)
    return pl.pallas_call(
        kernel,
        out_shape=outs,
        in_specs=[spec(kind) for kind in kinds],
        out_specs=[spec("v")] * len(outs) if several else spec("v"),
        scratch_shapes=scratch,
        compiler_params=pltpu.CompilerParams(vmem_limit_bytes=limit * MIB),
        cost_estimate=pl.CostEstimate(
            flops=products * 6 * 8 * 128**3, bytes_accessed=4 * MIB, transcendentals=0
        ),
        name=name,
    )(*args)


def body(interfaces, cell_profile, cell_section, mode_loss, phase, mode_field, target):
    cells = cell_profile.shape[0]
    profiles, m = mode_loss.shape
    blocks = lax.axis_size("cell")
    waves = lax.axis_size("wl")
    pixels = mode_field.shape[2]
    chips = blocks // 2
    angle = phase.reshape(profiles, m)
    factors = (mode_loss * jnp.cos(angle), mode_loss * jnp.sin(angle))
    wanted = target.reshape(2, m, m)
    me = lax.axis_index("cell").astype(jnp.int32).reshape(1)

    def pairs(*lead):
        return (*lead, 2, m, 2 * m)

    def f32(*shape):
        return jax.ShapeDtypeStruct(shape, F32)

    def bf16(*shape):
        return jax.ShapeDtypeStruct(shape, BF16)

    tables = [f32(profiles, 2, 8, m), f32(profiles, 2, m, m)]
    codes = (cell_profile << SHIFT) | cell_section
    got = [
        lax.ppermute(codes, "cell", [(block, device) for device, block in enumerate(source)])
        for source in routes(chips)
    ]
    nodes, own, row_table, col_table = call(
        own_kernel, "own_tree", "svvv", [bf16(*pairs(6, 3)), f32(3, m, 2 * m), *tables], [], 12, 28,
        codes, interfaces, *factors,
    )
    mine = call(
        far_kernel, "far_trees", "s" * chips + "vvvv", f32(9, m, 2 * m),
        [
            pltpu.SMEM((blocks, cells), jnp.int32),
            pltpu.VMEM(pairs(chips - 1, cells // 2, 3), BF16),
            pltpu.VMEM(pairs(chips - 1, cells // 4, 3), BF16),
            pltpu.VMEM(pairs(2, 3), BF16),
        ],
        8 + 3 * blocks // 2, 32 * (chips - 1),
        me, *got, interfaces, row_table, col_table, own,
    )
    theirs = lax.ppermute(mine, "cell", [(i, i ^ 1) for i in range(blocks)])
    parts_shape = bf16(2, cells, m, 2 * m)
    grown, back, trans = call(
        scan_kernel, "own_scan", "svvvvv", [parts_shape] * 3, [], 16, 27,
        codes, interfaces, row_table, col_table, nodes, own,
    )
    def packed_shape(group):
        return f32(group * (m // 2) + 8, m)

    more = cells - FEWER
    x, part, packed = call(
        functools.partial(first_kernel, more), "couplings", "svvvvvv",
        [bf16(2, 2, 2 * m, 2 * m), f32(2, m, 2 * m), packed_shape(more)], [], 12, 35,
        me, wanted, mine, theirs, grown, back, trans,
    )
    groups = [packed]
    groups.append(
        call(
            functools.partial(coupling_kernel, more, FEWER), "couplings", "vvvv",
            packed_shape(FEWER), [], 12, 10,
            x, grown, back, trans,
        )
    )
    reflection = call(
        reflect_kernel, "reflection", "svvv", f32(2, m // blocks, m),
        [pltpu.VMEM((2, m, 2 * m), F32)], 12, 10,
        me, mine, theirs, part,
    )

    steps = []
    bit = 1
    while bit < waves:
        steps.append(bit)
        bit *= 2
    orders = (steps, steps[::-1])

    def exchange(part, number):
        pairs_of = [
            (w * blocks + c, (w ^ orders[c & 1][number]) * blocks + c)
            for w in range(waves)
            for c in range(blocks)
        ]
        return lax.ppermute(part, ("wl", "cell"), pairs_of)

    field = bf16(profiles, m, pixels)
    fields = call(field_kernel, "field_parts", "v", [field, field], [], 12, 1, mode_field)
    gradient = []
    start = 0
    for group, packed in zip((more, FEWER), groups):
        other = jnp.zeros_like(packed)
        for number in range(len(steps)):
            if number:
                packed = packed + other
            other = exchange(packed, number)
        gradient = [
            call(
                functools.partial(project_kernel, start, group), "project",
                "svvvv" + "v" * len(gradient), f32(start + group, pixels), [], 12, 4,
                cell_profile, *fields, packed, other, *gradient,
            )
        ]
        start += group
    return reflection[None], gradient[0]


def solution(mesh):
    in_specs = (
        P(),
        P("cell"),
        P("cell"),
        P(),
        P(None, "wl", None),
        P(None, None, "wl"),
        P("wl", None, None, None),
    )
    out_specs = (P("wl", None, "cell", None), P("cell", "wl"))
    return jax.shard_map(body, mesh=mesh, in_specs=in_specs, out_specs=out_specs, check_vma=False)
```

```python
import functools
import jax
import jax.numpy as jnp
from jax import lax
from jax.experimental import pallas as pl
from jax.experimental.pallas import tpu as pltpu
from jax.sharding import PartitionSpec as P

F32 = jnp.float32
BF16 = jnp.bfloat16
MIB = 1024 * 1024
SHIFT = 8
LOW = (1 << SHIFT) - 1
REFL, TRANS, BACK = 0, 1, 2
FEWER = 4


def split(x):
    hi = x.astype(BF16)
    lo = (x - hi.astype(F32)).astype(BF16)
    return hi, lo


def whole(pair):
    return pair[0].astype(F32) + pair[1].astype(F32)


def expand(h):
    m = h.shape[0]
    return jnp.concatenate([h, jnp.concatenate([-h[:, m:], h[:, :m]], axis=1)], axis=0)


def right(pair):
    return expand(pair[0]), expand(pair[1])


def dot(a, b):
    return jnp.dot(a, b, preferred_element_type=F32)


def deep(left):
    return jnp.concatenate([left[0], left[1], left[0]], axis=1)


def tall(weights):
    return jnp.concatenate([weights[0], weights[0], weights[1]], axis=0)


def mul(left, weights):
    return dot(deep(left), tall(weights))


def get(ref, *at):
    return ref[(*at, 0)], ref[(*at, 1)]


def keep(ref, pair, *at):
    ref[(*at, 0)], ref[(*at, 1)] = pair


def unit(m):
    row = lax.broadcasted_iota(jnp.int32, (m, 2 * m), 0)
    col = lax.broadcasted_iota(jnp.int32, (m, 2 * m), 1)
    return jnp.where(row == col, 1.0, 0.0).astype(F32)


def merge(former, latter):
    r1, t1, b1 = former
    r2, t2, b2 = latter
    m = t1[0].shape[0]
    t1w = tall(right(t1))
    both = dot(deep(b1), jnp.concatenate([tall(right(r2)), tall(right(b2))], axis=1))
    trans = dot(deep(t2), t1w)
    refl = whole(r1) + dot(deep(split(both[:, : 2 * m])), t1w)
    return split(refl), split(trans), split(both[:, 2 * m :])


def triple(ref, *at):
    return tuple(get(ref, *at, kind) for kind in range(3))


def keep_triple(ref, values, *at):
    for kind in range(3):
        keep(ref, values[kind], *at, kind)


def spread(factor_refs, row_ref, col_ref):
    for part, ref in enumerate(factor_refs):
        profiles, m = ref.shape
        for q in range(profiles):
            wide = jnp.broadcast_to(ref[q : q + 1], (m, m))
            row_ref[q, part] = wide[:8]
            col_ref[q, part] = wide.T


def trans_leaf(lib_ref, col_ref, code):
    q, s = code >> SHIFT, code & LOW
    re, im = lib_ref[s, TRANS, 0], lib_ref[s, TRANS, 1]
    cr, ci = col_ref[q, 0], col_ref[q, 1]
    return split(jnp.concatenate([cr * re - ci * im, cr * im + ci * re], axis=1))


def back_leaf(lib_ref, row_ref, code):
    q, s = code >> SHIFT, code & LOW
    re, im = lib_ref[s, BACK, 0], lib_ref[s, BACK, 1]
    rr, ri = row_ref[q, 0][:1], row_ref[q, 1][:1]
    return split(jnp.concatenate([re * rr - im * ri, re * ri + im * rr], axis=1))


def refl_leaf(lib_ref, code):
    s = code & LOW
    return split(jnp.concatenate([lib_ref[s, REFL, 0], lib_ref[s, REFL, 1]], axis=1))


def leaf(lib_ref, row_ref, col_ref, code):
    return (
        refl_leaf(lib_ref, code),
        trans_leaf(lib_ref, col_ref, code),
        back_leaf(lib_ref, row_ref, code),
    )


def own_kernel(code_ref, lib_ref, real_ref, imag_ref, nodes_ref, own_ref, row_ref, col_ref):
    cells = code_ref.shape[0]
    spread((real_ref, imag_ref), row_ref, col_ref)

    def cell(i):
        return leaf(lib_ref, row_ref, col_ref, code_ref[i])

    pairs = []
    for j in range(cells // 2):
        pairs.append(merge(cell(2 * j), cell(2 * j + 1)))
        keep_triple(nodes_ref, pairs[j], j)
    fours = []
    for j in range(cells // 4):
        fours.append(merge(pairs[2 * j], pairs[2 * j + 1]))
        keep_triple(nodes_ref, fours[j], cells // 2 + j)
    top = merge(*fours)
    for kind in range(3):
        own_ref[kind] = whole(top[kind])


def scan_kernel(
    code_ref, lib_ref, row_ref, col_ref, nodes_ref, own_ref,
    grown_ref, back_ref, trans_ref,
):
    m = own_ref.shape[1]

    def cell(i):
        return leaf(lib_ref, row_ref, col_ref, code_ref[i])

    def store(ref, i, pair):
        ref[0, i], ref[1, i] = pair

    def put(i, values):
        store(trans_ref, i, values[TRANS])
        store(back_ref, i, values[BACK])
        return values

    def grow(i, refl, before):
        store(grown_ref, i, split(whole(before) + mul(refl, right(before))))

    def trans_of(i):
        return trans_leaf(lib_ref, col_ref, code_ref[i])

    suffix4 = put(4, triple(nodes_ref, 5))
    before2 = get(nodes_ref, 0, TRANS)
    before4 = get(nodes_ref, 4, TRANS)
    suffix2 = put(2, merge(triple(nodes_ref, 1), suffix4))
    suffix3 = put(3, merge(cell(3), suffix4))
    before3 = split(mul(trans_of(2), right(before2)))
    grow(3, suffix3[REFL], before3)
    grow(2, suffix2[REFL], before2)
    grow(4, suffix4[REFL], before4)
    suffix1 = put(1, merge(cell(1), suffix2))
    before6 = split(mul(get(nodes_ref, 2, TRANS), right(before4)))
    suffix6 = put(6, triple(nodes_ref, 3))
    suffix5 = put(5, merge(cell(5), suffix6))
    grow(6, suffix6[REFL], before6)
    before5 = split(mul(trans_of(4), right(before4)))
    before7 = split(mul(trans_of(6), right(before6)))
    grow(5, suffix5[REFL], before5)
    suffix7 = put(7, cell(7))
    grow(7, suffix7[REFL], before7)
    grow(1, suffix1[REFL], trans_of(0))
    store(grown_ref, 0, split(unit(m) + own_ref[REFL]))
    store(trans_ref, 0, split(own_ref[TRANS]))
    store(back_ref, 0, split(own_ref[BACK]))


def far_core(chip, block, chips):
    if block < 2 * chip:
        return int(block >= chip)
    return int(block >= 2 * chip + 2 + chips - 1 - chip)


def routes(chips):
    blocks = 2 * chips
    wanted = [
        {2 * chip + far_core(chip, block, chips) for chip in range(chips) if chip != block // 2}
        for block in range(blocks)
    ]
    found = []
    for _ in range(chips - 1):
        source = [None] * blocks

        def place(block, seen):
            for device in sorted(wanted[block] - seen):
                seen.add(device)
                if source[device] is None or place(source[device], seen):
                    source[device] = block
                    return True
            return False

        for block in range(blocks):
            place(block, set())
        for device, block in enumerate(source):
            wanted[block].discard(device)
        found.append(source)
    return found


def far_kernel(*refs):
    me_ref, *got_refs = refs[:-9]
    lib_ref, row_ref, col_ref, own_ref, out_ref, code_ref, pairs_ref, fours_ref, acc_ref = refs[-9:]
    blocks, cells = code_ref.shape
    chips = blocks // 2
    m = own_ref.shape[1]
    for ref, source in zip(got_refs, routes(chips)):
        k = source[0]
        for device in range(1, blocks):
            k = jnp.where(me_ref[0] == device, source[device], k)
        for i in range(cells):
            code_ref[k, i] = ref[i]
    chip = me_ref[0] >> 1
    core = me_ref[0] & 1
    right_count = chips - 1 - chip
    right_end = 2 * chip + 2 + (core + 1) * right_count
    left_end = (core + 1) * chip
    out_ref[0:3] = own_ref[...]
    eye = split(unit(m))
    none = (jnp.zeros_like(eye[0]), jnp.zeros_like(eye[0]))
    for side in range(2):
        keep_triple(acc_ref, (none, eye, eye), side)

    def place(i):
        on_right = i < right_count
        return jnp.where(on_right, right_end - 1 - i, left_end - 1 - (i - right_count))

    def pair_step(i, _):
        k = place(i)

        def cell(j):
            return leaf(lib_ref, row_ref, col_ref, code_ref[k, j])

        for j in range(cells // 2):
            keep_triple(
                pairs_ref,
                merge(cell(2 * j), cell(2 * j + 1)),
                i,
                j,
            )
        return 0

    if chips <= 4:
        for i in range(chips - 1):
            pair_step(i, 0)
    else:
        lax.fori_loop(0, chips - 1, pair_step, 0)
    for i in range(chips - 1):
        for j in range(cells // 4):
            keep_triple(
                fours_ref, merge(triple(pairs_ref, i, 2 * j), triple(pairs_ref, i, 2 * j + 1)), i, j
            )
    for i in range(chips - 1):
        keep_triple(pairs_ref, merge(triple(fours_ref, i, 0), triple(fours_ref, i, 1)), i, 0)
    for i in range(chips - 1):
        side = jnp.where(i < right_count, 1, 0)
        first = (i == 0) | (i == right_count)

        @pl.when(first)
        def _():
            acc_ref[side] = pairs_ref[i, 0]

        @pl.when(jnp.logical_not(first))
        def _():
            keep_triple(acc_ref, merge(triple(pairs_ref, i, 0), triple(acc_ref, side)), side)

    for side in range(2):
        for kind in range(3):
            out_ref[3 + 3 * side + kind] = whole(get(acc_ref, side, kind))


OWN, LEFT, RIGHT = 0, 3, 6


def sides(me_ref, mine_ref, theirs_ref):
    on_first = (me_ref[0] & 1) == 0

    def first(index):
        return jnp.where(on_first, mine_ref[index], theirs_ref[index])

    def second(index):
        return jnp.where(on_first, theirs_ref[index], mine_ref[index])

    return on_first, first, second


def chain_kernel(me_ref, target_ref, mine_ref, theirs_ref, x_ref, part_ref):
    m = target_ref.shape[1]
    on_first, first, second = sides(me_ref, mine_ref, theirs_ref)
    own0_t = split(first(OWN + TRANS))
    own1_t = split(second(OWN + TRANS))
    own1_tw = right(own1_t)
    far0_tw = right(split(first(RIGHT + TRANS)))
    p_far = mul(split(second(LEFT + TRANS)), right(split(first(LEFT + TRANS))))
    q_far = mul(split(second(RIGHT + TRANS)), far0_tw)
    p_fars, q_fars = split(p_far), split(q_far)
    z = mul(split(first(RIGHT + BACK)), right(split(second(RIGHT + REFL))))
    p_here = mul(own0_t, right(p_fars))
    q_here = mul(q_fars, own1_tw)
    s_far = first(RIGHT + REFL) + mul(split(z), far0_tw)
    total = mul(split(q_here), right(split(p_here)))
    z = mul(split(second(OWN + BACK)), right(split(s_far)))
    miss = jnp.concatenate(
        [(total[:, :m] - target_ref[0]).T, (total[:, m:] - target_ref[1]).T], axis=1
    )
    s_here = second(OWN + REFL) + mul(split(z), own1_tw)
    part_ref[0] = s_here
    part_ref[1] = p_far
    p = split(jnp.where(on_first, p_far, p_here))
    q = split(jnp.where(on_first, q_here, q_far))
    s = split(jnp.where(on_first, s_here, s_far))
    ahead = mul(split(miss), right(q))
    s_block = mul(s, right(split(mine_ref[OWN + TRANS])))
    x1 = right(split(mul(p, right(split(ahead)))))
    x_ref[0, 0], x_ref[0, 1] = x1
    x_ref[1, 0], x_ref[1, 1] = right(split(mul(split(s_block), x1)))


def reflect_kernel(me_ref, mine_ref, theirs_ref, part_ref, out_ref, mark_ref, left_ref):
    rows, m = out_ref.shape[1:]
    mark_ref[...] = jnp.zeros_like(mark_ref)
    _, first, second = sides(me_ref, mine_ref, theirs_ref)
    left_ref[0] = first(LEFT + REFL)
    left_ref[1] = first(LEFT + BACK)
    at = pl.ds(pl.multiple_of(me_ref[0] * rows, rows), rows)
    back = split(left_ref[1, at, :])
    z = mul(split(first(OWN + BACK)), right(split(part_ref[0])))
    refl = first(OWN + REFL) + mul(split(z), right(split(first(OWN + TRANS))))
    z = mul(back, right(split(second(LEFT + REFL))))
    left = left_ref[0, at, :] + mul(split(z), right(split(first(LEFT + TRANS))))
    back = mul(back, right(split(second(LEFT + BACK))))
    z = mul(split(back), right(split(refl)))
    mine = left + mul(split(z), right(split(part_ref[1])))
    out_ref[0] = mine[:, :m]
    out_ref[1] = mine[:, m:]


def coupling_kernel(start, group, x_ref, grown_ref, back_ref, trans_ref, out_ref):
    m = grown_ref.shape[2]
    h = m // 2
    cells = slice(start, start + group)

    def stack(ref):
        return tuple(ref[part, cells].reshape(group * m, 2 * m) for part in range(2))

    row = lax.broadcasted_iota(jnp.int32, (h, m), 0)
    lane = lax.broadcasted_iota(jnp.int32, (h, m), 1)
    use_top = (lane >= h) | (row > lane)
    eye = lax.broadcasted_iota(jnp.int32, (m, m), 0) == lax.broadcasted_iota(jnp.int32, (m, m), 1)
    all_y = mul(stack(grown_ref), (x_ref[0, 0], x_ref[0, 1]))
    all_y = all_y + mul(stack(back_ref), (x_ref[1, 0], x_ref[1, 1]))
    out_ref[group * h :] = jnp.zeros_like(out_ref[group * h :])
    for j in range(group):
        y = all_y[j * m : (j + 1) * m]
        ys = split(jnp.concatenate([y[:, :m], -y[:, m:]], axis=1))
        t = [trans_ref[part, start + j] for part in range(2)]
        c = mul(ys, [jnp.concatenate([a[:, :m], a[:, m:]], axis=0) for a in t])
        both = c + c.T
        low = pltpu.roll(both[h:], h, 1)
        out_ref[j * h : (j + 1) * h] = jnp.where(use_top, both[:h], low)
        out_ref[group * h + j : group * h + j + 1] = jnp.sum(
            jnp.where(eye, c, 0.0), axis=0, keepdims=True
        )


def add_kernel(a_ref, b_ref, *refs):
    refs[-1][...] = a_ref[...] + b_ref[...]


def field_kernel(field_ref, hi_ref, lo_ref):
    for q in range(field_ref.shape[0]):
        hi_ref[q], lo_ref[q] = split(field_ref[q])


def project_kernel(start, group, prof_ref, hi_ref, lo_ref, mine_ref, theirs_ref, *rest):
    out_ref = rest[-1]
    m = hi_ref.shape[1]
    h = m // 2
    if start:
        out_ref[:start] = rest[0][...]
    row = lax.broadcasted_iota(jnp.int32, (h, m), 0)
    lane = lax.broadcasted_iota(jnp.int32, (h, m), 1)
    eye = lax.broadcasted_iota(jnp.int32, (m, m), 0) == lax.broadcasted_iota(jnp.int32, (m, m), 1)
    for j in range(group):
        at = slice(j * h, (j + 1) * h)
        packed = mine_ref[at] + theirs_ref[at]
        at = slice(group * h + j, group * h + j + 1)
        diag = mine_ref[at] + theirs_ref[at]
        top = jnp.where((lane >= h) | (row > lane), packed, 0.0)
        low = pltpu.roll(jnp.where((lane < h) & (row < lane), packed, 0.0), h, 1)
        c = jnp.concatenate([top, low], axis=0) + jnp.where(eye, diag, 0.0)
        ch, cl = split(c)
        q = prof_ref[start + j]
        fh, fl = hi_ref[q], lo_ref[q]
        w = dot(jnp.concatenate([ch, cl], axis=1), jnp.concatenate([fh, fh], axis=0))
        w = w + dot(ch, fl)
        i = start + j
        out_ref[i : i + 1] = jnp.sum(
            (fh.astype(F32) + fl.astype(F32)) * w, axis=0, keepdims=True
        )


def call(kernel, name, kinds, outs, scratch, limit, products, *args):
    def spec(kind):
        spaces = {"s": pltpu.SMEM, "v": pltpu.VMEM, "a": pl.ANY}
        return pl.BlockSpec(memory_space=spaces[kind])

    several = isinstance(outs, list)
    return pl.pallas_call(
        kernel,
        out_shape=outs,
        in_specs=[spec(kind) for kind in kinds],
        out_specs=[spec("v")] * len(outs) if several else spec("v"),
        scratch_shapes=scratch,
        compiler_params=pltpu.CompilerParams(vmem_limit_bytes=limit * MIB),
        cost_estimate=pl.CostEstimate(
            flops=products * 6 * 8 * 128**3, bytes_accessed=4 * MIB, transcendentals=0
        ),
        name=name,
    )(*args)


def body(interfaces, cell_profile, cell_section, mode_loss, phase, mode_field, target):
    cells = cell_profile.shape[0]
    profiles, m = mode_loss.shape
    blocks = lax.axis_size("cell")
    waves = lax.axis_size("wl")
    pixels = mode_field.shape[2]
    chips = blocks // 2
    angle = phase.reshape(profiles, m)
    factors = (mode_loss * jnp.cos(angle), mode_loss * jnp.sin(angle))
    wanted = target.reshape(2, m, m)
    me = lax.axis_index("cell").astype(jnp.int32).reshape(1)

    def pairs(*lead):
        return (*lead, 2, m, 2 * m)

    def f32(*shape):
        return jax.ShapeDtypeStruct(shape, F32)

    def bf16(*shape):
        return jax.ShapeDtypeStruct(shape, BF16)

    tables = [f32(profiles, 2, 8, m), f32(profiles, 2, m, m)]
    codes = (cell_profile << SHIFT) | cell_section
    got = [
        lax.ppermute(codes, "cell", [(block, device) for device, block in enumerate(source)])
        for source in routes(chips)
    ]
    nodes, own, row_table, col_table = call(
        own_kernel, "own_tree", "svvv", [bf16(*pairs(6, 3)), f32(3, m, 2 * m), *tables], [], 12, 28,
        codes, interfaces, *factors,
    )
    mine = call(
        far_kernel, "far_trees", "s" * chips + "vvvv", f32(9, m, 2 * m),
        [
            pltpu.SMEM((blocks, cells), jnp.int32),
            pltpu.VMEM(pairs(chips - 1, cells // 2, 3), BF16),
            pltpu.VMEM(pairs(chips - 1, cells // 4, 3), BF16),
            pltpu.VMEM(pairs(2, 3), BF16),
        ],
        8 + 3 * blocks // 2, 32 * (chips - 1),
        me, *got, interfaces, row_table, col_table, own,
    )
    theirs = lax.ppermute(mine, "cell", [(i, i ^ 1) for i in range(blocks)])
    parts_shape = bf16(2, cells, m, 2 * m)
    grown, back, trans = call(
        scan_kernel, "own_scan", "svvvvv", [parts_shape] * 3, [], 16, 27,
        codes, interfaces, row_table, col_table, nodes, own,
    )
    def packed_shape(group):
        return f32(group * (m // 2) + 8, m)

    more = cells - FEWER
    x, part = call(
        chain_kernel, "chain", "svvv", [bf16(2, 2, 2 * m, 2 * m), f32(2, m, 2 * m)], [], 12, 20,
        me, wanted, mine, theirs,
    )
    groups = [
        call(
            functools.partial(coupling_kernel, start, group), "couplings", "vvvv",
            packed_shape(group), [], 12, 10,
            x, grown, back, trans,
        )
        for start, group in ((0, more), (more, FEWER))
    ]
    reflection, mark = call(
        reflect_kernel, "reflection", "svvv", [f32(2, m // blocks, m), f32(8, m)],
        [pltpu.VMEM((2, m, 2 * m), F32)], 12, 10,
        me, mine, theirs, part,
    )

    steps = []
    bit = 1
    while bit < waves:
        steps.append(bit)
        bit *= 2
    orders = (steps, steps[::-1])

    def exchange(part, number):
        pairs_of = [
            (w * blocks + c, (w ^ orders[c & 1][number]) * blocks + c)
            for w in range(waves)
            for c in range(blocks)
        ]
        return lax.ppermute(part, ("wl", "cell"), pairs_of)

    field = bf16(profiles, m, pixels)
    fields = call(field_kernel, "field_parts", "v", [field, field], [], 12, 1, mode_field)
    gradient = []
    start = 0
    for group, packed in zip((more, FEWER), groups):
        other = jnp.zeros_like(packed)
        for number in range(len(steps)):
            if number == 1 and not start:
                packed = call(
                    add_kernel, "sum_of_two", "vvaa", packed_shape(group), [], 12, 0,
                    packed, other, mark, fields[0],
                )
            elif number:
                packed = packed + other
            other = exchange(packed, number)
        gradient = [
            call(
                functools.partial(project_kernel, start, group), "project",
                "svvvv" + "v" * len(gradient), f32(start + group, pixels), [], 12, 4,
                cell_profile, *fields, packed, other, *gradient,
            )
        ]
        start += group
    return reflection[None], gradient[0]


def solution(mesh):
    in_specs = (
        P(),
        P("cell"),
        P("cell"),
        P(),
        P(None, "wl", None),
        P(None, None, "wl"),
        P("wl", None, None, None),
    )
    out_specs = (P("wl", None, "cell", None), P("cell", "wl"))
    return jax.shard_map(body, mesh=mesh, in_specs=in_specs, out_specs=out_specs, check_vma=False)
```

```python
import functools
import jax
import jax.numpy as jnp
from jax import lax
from jax.experimental import pallas as pl
from jax.experimental.pallas import tpu as pltpu
from jax.sharding import PartitionSpec as P

F32 = jnp.float32
BF16 = jnp.bfloat16
MIB = 1024 * 1024
SHIFT = 8
LOW = (1 << SHIFT) - 1
REFL, TRANS, BACK = 0, 1, 2
FEWER = 3


def split(x):
    hi = x.astype(BF16)
    lo = (x - hi.astype(F32)).astype(BF16)
    return hi, lo


def whole(pair):
    return pair[0].astype(F32) + pair[1].astype(F32)


def expand(h):
    m = h.shape[0]
    return jnp.concatenate([h, jnp.concatenate([-h[:, m:], h[:, :m]], axis=1)], axis=0)


def right(pair):
    return expand(pair[0]), expand(pair[1])


def dot(a, b):
    return jnp.dot(a, b, preferred_element_type=F32)


def deep(left):
    return jnp.concatenate([left[0], left[1], left[0]], axis=1)


def tall(weights):
    return jnp.concatenate([weights[0], weights[0], weights[1]], axis=0)


def mul(left, weights):
    return dot(deep(left), tall(weights))


def get(ref, *at):
    return ref[(*at, 0)], ref[(*at, 1)]


def keep(ref, pair, *at):
    ref[(*at, 0)], ref[(*at, 1)] = pair


def unit(m):
    row = lax.broadcasted_iota(jnp.int32, (m, 2 * m), 0)
    col = lax.broadcasted_iota(jnp.int32, (m, 2 * m), 1)
    return jnp.where(row == col, 1.0, 0.0).astype(F32)


def merge(former, latter):
    r1, t1, b1 = former
    r2, t2, b2 = latter
    m = t1[0].shape[0]
    t1w = tall(right(t1))
    both = dot(deep(b1), jnp.concatenate([tall(right(r2)), tall(right(b2))], axis=1))
    trans = dot(deep(t2), t1w)
    refl = whole(r1) + dot(deep(split(both[:, : 2 * m])), t1w)
    return split(refl), split(trans), split(both[:, 2 * m :])


def triple(ref, *at):
    return tuple(get(ref, *at, kind) for kind in range(3))


def keep_triple(ref, values, *at):
    for kind in range(3):
        keep(ref, values[kind], *at, kind)


def trans_leaf(lib_ref, col_ref, code):
    q, s = code >> SHIFT, code & LOW
    re, im = lib_ref[s, TRANS, 0], lib_ref[s, TRANS, 1]
    cr, ci = col_ref[q, 0], col_ref[q, 1]
    return split(jnp.concatenate([cr * re - ci * im, cr * im + ci * re], axis=1))


def back_leaf(lib_ref, row_ref, code):
    q, s = code >> SHIFT, code & LOW
    re, im = lib_ref[s, BACK, 0], lib_ref[s, BACK, 1]
    rr, ri = row_ref[q, 0][:1], row_ref[q, 1][:1]
    return split(jnp.concatenate([re * rr - im * ri, re * ri + im * rr], axis=1))


def refl_leaf(lib_ref, code):
    s = code & LOW
    return split(jnp.concatenate([lib_ref[s, REFL, 0], lib_ref[s, REFL, 1]], axis=1))


def leaf(lib_ref, row_ref, col_ref, code):
    return (
        refl_leaf(lib_ref, code),
        trans_leaf(lib_ref, col_ref, code),
        back_leaf(lib_ref, row_ref, code),
    )


def table_kernel(code_ref, real_ref, imag_ref, sent_ref, row_ref, col_ref):
    sent_ref[...] = code_ref[...]
    for part, ref in enumerate((real_ref, imag_ref)):
        profiles, m = ref.shape
        for q in range(profiles):
            wide = jnp.broadcast_to(ref[q : q + 1], (m, m))
            row_ref[q, part] = wide[:8]
            col_ref[q, part] = wide.T


def own_kernel(code_ref, lib_ref, row_ref, col_ref, nodes_ref, own_ref):
    cells = code_ref.shape[1]

    def cell(i):
        return leaf(lib_ref, row_ref, col_ref, code_ref[0, i])

    pairs = []
    for j in range(cells // 2):
        pairs.append(merge(cell(2 * j), cell(2 * j + 1)))
        keep_triple(nodes_ref, pairs[j], j)
    fours = []
    for j in range(cells // 4):
        fours.append(merge(pairs[2 * j], pairs[2 * j + 1]))
        keep_triple(nodes_ref, fours[j], cells // 2 + j)
    top = merge(*fours)
    for kind in range(3):
        own_ref[kind] = whole(top[kind])


def scan_kernel(
    code_ref, lib_ref, row_ref, col_ref, nodes_ref, own_ref,
    grown_ref, back_ref, trans_ref,
):
    m = own_ref.shape[1]

    def cell(i):
        return leaf(lib_ref, row_ref, col_ref, code_ref[0, i])

    def store(ref, i, pair):
        ref[0, i], ref[1, i] = pair

    def put(i, values):
        store(trans_ref, i, values[TRANS])
        store(back_ref, i, values[BACK])
        return values

    def grow(i, refl, before):
        store(grown_ref, i, split(whole(before) + mul(refl, right(before))))

    def trans_of(i):
        return trans_leaf(lib_ref, col_ref, code_ref[0, i])

    suffix4 = put(4, triple(nodes_ref, 5))
    before2 = get(nodes_ref, 0, TRANS)
    before4 = get(nodes_ref, 4, TRANS)
    suffix2 = put(2, merge(triple(nodes_ref, 1), suffix4))
    suffix3 = put(3, merge(cell(3), suffix4))
    before3 = split(mul(trans_of(2), right(before2)))
    grow(3, suffix3[REFL], before3)
    grow(2, suffix2[REFL], before2)
    grow(4, suffix4[REFL], before4)
    suffix1 = put(1, merge(cell(1), suffix2))
    before6 = split(mul(get(nodes_ref, 2, TRANS), right(before4)))
    suffix6 = put(6, triple(nodes_ref, 3))
    suffix5 = put(5, merge(cell(5), suffix6))
    grow(6, suffix6[REFL], before6)
    before5 = split(mul(trans_of(4), right(before4)))
    before7 = split(mul(trans_of(6), right(before6)))
    grow(5, suffix5[REFL], before5)
    suffix7 = put(7, cell(7))
    grow(7, suffix7[REFL], before7)
    grow(1, suffix1[REFL], trans_of(0))
    store(grown_ref, 0, split(unit(m) + own_ref[REFL]))
    store(trans_ref, 0, split(own_ref[TRANS]))
    store(back_ref, 0, split(own_ref[BACK]))


def far_core(chip, block, chips):
    if block < 2 * chip:
        return int(block >= chip)
    return int(block >= 2 * chip + 2 + chips - 1 - chip)


def routes(chips):
    blocks = 2 * chips
    wanted = [
        {2 * chip + far_core(chip, block, chips) for chip in range(chips) if chip != block // 2}
        for block in range(blocks)
    ]
    found = []
    for _ in range(chips - 1):
        source = [None] * blocks

        def place(block, seen):
            for device in sorted(wanted[block] - seen):
                seen.add(device)
                if source[device] is None or place(source[device], seen):
                    source[device] = block
                    return True
            return False

        for block in range(blocks):
            place(block, set())
        for device, block in enumerate(source):
            wanted[block].discard(device)
        found.append(source)
    return found


def far_kernel(*refs):
    me_ref, *got_refs = refs[:-9]
    lib_ref, row_ref, col_ref, own_ref, out_ref, code_ref, pairs_ref, fours_ref, acc_ref = refs[-9:]
    blocks, cells = code_ref.shape
    chips = blocks // 2
    m = own_ref.shape[1]
    for ref, source in zip(got_refs, routes(chips)):
        k = source[0]
        for device in range(1, blocks):
            k = jnp.where(me_ref[0] == device, source[device], k)
        for i in range(cells):
            code_ref[k, i] = ref[0, i]
    chip = me_ref[0] >> 1
    core = me_ref[0] & 1
    right_count = chips - 1 - chip
    right_end = 2 * chip + 2 + (core + 1) * right_count
    left_end = (core + 1) * chip
    out_ref[0:3] = own_ref[...]
    eye = split(unit(m))
    none = (jnp.zeros_like(eye[0]), jnp.zeros_like(eye[0]))
    for side in range(2):
        keep_triple(acc_ref, (none, eye, eye), side)

    def place(i):
        on_right = i < right_count
        return jnp.where(on_right, right_end - 1 - i, left_end - 1 - (i - right_count))

    def pair_step(i, _):
        k = place(i)

        def cell(j):
            return leaf(lib_ref, row_ref, col_ref, code_ref[k, j])

        for j in range(cells // 2):
            keep_triple(
                pairs_ref,
                merge(cell(2 * j), cell(2 * j + 1)),
                i,
                j,
            )
        return 0

    if chips <= 4:
        for i in range(chips - 1):
            pair_step(i, 0)
    else:
        lax.fori_loop(0, chips - 1, pair_step, 0)
    for i in range(chips - 1):
        for j in range(cells // 4):
            keep_triple(
                fours_ref, merge(triple(pairs_ref, i, 2 * j), triple(pairs_ref, i, 2 * j + 1)), i, j
            )
    for i in range(chips - 1):
        keep_triple(pairs_ref, merge(triple(fours_ref, i, 0), triple(fours_ref, i, 1)), i, 0)
    for i in range(chips - 1):
        side = jnp.where(i < right_count, 1, 0)
        first = (i == 0) | (i == right_count)

        @pl.when(first)
        def _():
            acc_ref[side] = pairs_ref[i, 0]

        @pl.when(jnp.logical_not(first))
        def _():
            keep_triple(acc_ref, merge(triple(pairs_ref, i, 0), triple(acc_ref, side)), side)

    for side in range(2):
        for kind in range(3):
            out_ref[3 + 3 * side + kind] = whole(get(acc_ref, side, kind))


OWN, LEFT, RIGHT = 0, 3, 6


def sides(me_ref, mine_ref, theirs_ref):
    on_first = (me_ref[0] & 1) == 0

    def first(index):
        return jnp.where(on_first, mine_ref[index], theirs_ref[index])

    def second(index):
        return jnp.where(on_first, theirs_ref[index], mine_ref[index])

    return on_first, first, second


def chain_kernel(me_ref, target_ref, mine_ref, theirs_ref, x_ref, part_ref):
    m = target_ref.shape[1]
    on_first, first, second = sides(me_ref, mine_ref, theirs_ref)
    own0_t = split(first(OWN + TRANS))
    own1_t = split(second(OWN + TRANS))
    own1_tw = right(own1_t)
    far0_tw = right(split(first(RIGHT + TRANS)))
    p_far = mul(split(second(LEFT + TRANS)), right(split(first(LEFT + TRANS))))
    q_far = mul(split(second(RIGHT + TRANS)), far0_tw)
    p_fars, q_fars = split(p_far), split(q_far)
    z = mul(split(first(RIGHT + BACK)), right(split(second(RIGHT + REFL))))
    p_here = mul(own0_t, right(p_fars))
    q_here = mul(q_fars, own1_tw)
    s_far = first(RIGHT + REFL) + mul(split(z), far0_tw)
    total = mul(split(q_here), right(split(p_here)))
    z = mul(split(second(OWN + BACK)), right(split(s_far)))
    miss = jnp.concatenate(
        [(total[:, :m] - target_ref[0]).T, (total[:, m:] - target_ref[1]).T], axis=1
    )
    s_here = second(OWN + REFL) + mul(split(z), own1_tw)
    part_ref[0] = s_here
    part_ref[1] = p_far
    p = split(jnp.where(on_first, p_far, p_here))
    q = split(jnp.where(on_first, q_here, q_far))
    s = split(jnp.where(on_first, s_here, s_far))
    ahead = mul(split(miss), right(q))
    s_block = mul(s, right(split(mine_ref[OWN + TRANS])))
    x1 = right(split(mul(p, right(split(ahead)))))
    x_ref[0, 0], x_ref[0, 1] = x1
    x_ref[1, 0], x_ref[1, 1] = right(split(mul(split(s_block), x1)))


def reflect_kernel(me_ref, mine_ref, theirs_ref, part_ref, out_ref, mark_ref, left_ref):
    rows, m = out_ref.shape[1:]
    mark_ref[...] = jnp.zeros_like(mark_ref)
    _, first, second = sides(me_ref, mine_ref, theirs_ref)
    left_ref[0] = first(LEFT + REFL)
    left_ref[1] = first(LEFT + BACK)
    at = pl.ds(pl.multiple_of(me_ref[0] * rows, rows), rows)
    back = split(left_ref[1, at, :])
    z = mul(split(first(OWN + BACK)), right(split(part_ref[0])))
    refl = first(OWN + REFL) + mul(split(z), right(split(first(OWN + TRANS))))
    z = mul(back, right(split(second(LEFT + REFL))))
    left = left_ref[0, at, :] + mul(split(z), right(split(first(LEFT + TRANS))))
    back = mul(back, right(split(second(LEFT + BACK))))
    z = mul(split(back), right(split(refl)))
    mine = left + mul(split(z), right(split(part_ref[1])))
    out_ref[0] = mine[:, :m]
    out_ref[1] = mine[:, m:]


def coupling_kernel(start, group, x_ref, grown_ref, back_ref, trans_ref, out_ref):
    m = grown_ref.shape[2]
    h = m // 2
    cells = slice(start, start + group)

    def stack(ref):
        return tuple(ref[part, cells].reshape(group * m, 2 * m) for part in range(2))

    row = lax.broadcasted_iota(jnp.int32, (h, m), 0)
    lane = lax.broadcasted_iota(jnp.int32, (h, m), 1)
    use_top = (lane >= h) | (row > lane)
    eye = lax.broadcasted_iota(jnp.int32, (m, m), 0) == lax.broadcasted_iota(jnp.int32, (m, m), 1)
    all_y = mul(stack(grown_ref), (x_ref[0, 0], x_ref[0, 1]))
    all_y = all_y + mul(stack(back_ref), (x_ref[1, 0], x_ref[1, 1]))
    out_ref[group * h :] = jnp.zeros_like(out_ref[group * h :])
    for j in range(group):
        y = all_y[j * m : (j + 1) * m]
        ys = split(jnp.concatenate([y[:, :m], -y[:, m:]], axis=1))
        t = [trans_ref[part, start + j] for part in range(2)]
        c = mul(ys, [jnp.concatenate([a[:, :m], a[:, m:]], axis=0) for a in t])
        both = c + c.T
        low = pltpu.roll(both[h:], h, 1)
        out_ref[j * h : (j + 1) * h] = jnp.where(use_top, both[:h], low)
        out_ref[group * h + j : group * h + j + 1] = jnp.sum(
            jnp.where(eye, c, 0.0), axis=0, keepdims=True
        )


def add_kernel(a_ref, b_ref, *refs):
    refs[-1][...] = a_ref[...] + b_ref[...]


def field_kernel(field_ref, hi_ref, lo_ref):
    for q in range(field_ref.shape[0]):
        hi_ref[q], lo_ref[q] = split(field_ref[q])


def project_kernel(start, group, prof_ref, hi_ref, lo_ref, mine_ref, theirs_ref, *rest):
    out_ref = rest[-1]
    m = hi_ref.shape[1]
    h = m // 2
    if start:
        out_ref[:start] = rest[0][...]
    row = lax.broadcasted_iota(jnp.int32, (h, m), 0)
    lane = lax.broadcasted_iota(jnp.int32, (h, m), 1)
    eye = lax.broadcasted_iota(jnp.int32, (m, m), 0) == lax.broadcasted_iota(jnp.int32, (m, m), 1)
    for j in range(group):
        at = slice(j * h, (j + 1) * h)
        packed = mine_ref[at] + theirs_ref[at]
        at = slice(group * h + j, group * h + j + 1)
        diag = mine_ref[at] + theirs_ref[at]
        top = jnp.where((lane >= h) | (row > lane), packed, 0.0)
        low = pltpu.roll(jnp.where((lane < h) & (row < lane), packed, 0.0), h, 1)
        c = jnp.concatenate([top, low], axis=0) + jnp.where(eye, diag, 0.0)
        ch, cl = split(c)
        q = prof_ref[start + j]
        fh, fl = hi_ref[q], lo_ref[q]
        w = dot(jnp.concatenate([ch, cl], axis=1), jnp.concatenate([fh, fh], axis=0))
        w = w + dot(ch, fl)
        i = start + j
        out_ref[i : i + 1] = jnp.sum(
            (fh.astype(F32) + fl.astype(F32)) * w, axis=0, keepdims=True
        )


def call(kernel, name, kinds, outs, scratch, limit, products, *args):
    def spec(kind):
        spaces = {"s": pltpu.SMEM, "v": pltpu.VMEM, "a": pl.ANY}
        return pl.BlockSpec(memory_space=spaces[kind])

    several = isinstance(outs, list)
    return pl.pallas_call(
        kernel,
        out_shape=outs,
        in_specs=[spec(kind) for kind in kinds],
        out_specs=[spec("v")] * len(outs) if several else spec("v"),
        scratch_shapes=scratch,
        compiler_params=pltpu.CompilerParams(vmem_limit_bytes=limit * MIB),
        cost_estimate=pl.CostEstimate(
            flops=products * 6 * 8 * 128**3, bytes_accessed=4 * MIB, transcendentals=0
        ),
        name=name,
    )(*args)


def body(interfaces, cell_profile, cell_section, mode_loss, phase, mode_field, target):
    cells = cell_profile.shape[0]
    profiles, m = mode_loss.shape
    blocks = lax.axis_size("cell")
    waves = lax.axis_size("wl")
    pixels = mode_field.shape[2]
    chips = blocks // 2
    angle = phase.reshape(profiles, m)
    factors = (mode_loss * jnp.cos(angle), mode_loss * jnp.sin(angle))
    wanted = target.reshape(2, m, m)
    me = lax.axis_index("cell").astype(jnp.int32).reshape(1)

    def pairs(*lead):
        return (*lead, 2, m, 2 * m)

    def f32(*shape):
        return jax.ShapeDtypeStruct(shape, F32)

    def bf16(*shape):
        return jax.ShapeDtypeStruct(shape, BF16)

    tables = [f32(profiles, 2, 8, m), f32(profiles, 2, m, m)]
    codes = ((cell_profile << SHIFT) | cell_section).reshape(1, cells)
    codes, row_table, col_table = call(
        table_kernel, "tables", "vvv", [jax.ShapeDtypeStruct((1, cells), jnp.int32), *tables], [],
        12, 60, codes, *factors,
    )
    got = [
        lax.ppermute(codes, "cell", [(block, device) for device, block in enumerate(source)])
        for source in routes(chips)
    ]
    nodes, own = call(
        own_kernel, "own_tree", "svvv", [bf16(*pairs(6, 3)), f32(3, m, 2 * m)], [], 12, 28,
        codes, interfaces, row_table, col_table,
    )
    mine = call(
        far_kernel, "far_trees", "s" * chips + "vvvv", f32(9, m, 2 * m),
        [
            pltpu.SMEM((blocks, cells), jnp.int32),
            pltpu.VMEM(pairs(chips - 1, cells // 2, 3), BF16),
            pltpu.VMEM(pairs(chips - 1, cells // 4, 3), BF16),
            pltpu.VMEM(pairs(2, 3), BF16),
        ],
        8 + 3 * blocks // 2, 32 * (chips - 1),
        me, *got, interfaces, row_table, col_table, own,
    )
    theirs = lax.ppermute(mine, "cell", [(i, i ^ 1) for i in range(blocks)])
    parts_shape = bf16(2, cells, m, 2 * m)
    grown, back, trans = call(
        scan_kernel, "own_scan", "svvvvv", [parts_shape] * 3, [], 16, 27,
        codes, interfaces, row_table, col_table, nodes, own,
    )
    def packed_shape(group):
        return f32(group * (m // 2) + 8, m)

    more = cells - FEWER
    x, part = call(
        chain_kernel, "chain", "svvv", [bf16(2, 2, 2 * m, 2 * m), f32(2, m, 2 * m)], [], 12, 20,
        me, wanted, mine, theirs,
    )
    groups = [
        call(
            functools.partial(coupling_kernel, start, group), "couplings", "vvvv",
            packed_shape(group), [], 12, 10,
            x, grown, back, trans,
        )
        for start, group in ((0, more), (more, FEWER))
    ]
    reflection, mark = call(
        reflect_kernel, "reflection", "svvv", [f32(2, m // blocks, m), f32(8, m)],
        [pltpu.VMEM((2, m, 2 * m), F32)], 12, 10,
        me, mine, theirs, part,
    )

    steps = []
    bit = 1
    while bit < waves:
        steps.append(bit)
        bit *= 2
    orders = (steps, steps[::-1])

    def exchange(part, number):
        pairs_of = [
            (w * blocks + c, (w ^ orders[c & 1][number]) * blocks + c)
            for w in range(waves)
            for c in range(blocks)
        ]
        return lax.ppermute(part, ("wl", "cell"), pairs_of)

    field = bf16(profiles, m, pixels)
    fields = call(field_kernel, "field_parts", "v", [field, field], [], 12, 1, mode_field)
    gradient = []
    start = 0
    for group, packed in zip((more, FEWER), groups):
        other = jnp.zeros_like(packed)
        for number in range(len(steps)):
            if number == 1 and not start:
                packed = call(
                    add_kernel, "sum_of_two", "vvaa", packed_shape(group), [], 12, 0,
                    packed, other, mark, fields[0],
                )
            elif number:
                packed = packed + other
            other = exchange(packed, number)
        gradient = [
            call(
                functools.partial(project_kernel, start, group), "project",
                "svvvv" + "v" * len(gradient), f32(start + group, pixels), [], 12, 4,
                cell_profile, *fields, packed, other, *gradient,
            )
        ]
        start += group
    return reflection[None], gradient[0]


def solution(mesh):
    in_specs = (
        P(),
        P("cell"),
        P("cell"),
        P(),
        P(None, "wl", None),
        P(None, None, "wl"),
        P("wl", None, None, None),
    )
    out_specs = (P("wl", None, "cell", None), P("cell", "wl"))
    return jax.shard_map(body, mesh=mesh, in_specs=in_specs, out_specs=out_specs, check_vma=False)
```

```python
import functools
import jax
import jax.numpy as jnp
from jax import lax
from jax.experimental import pallas as pl
from jax.experimental.pallas import tpu as pltpu
from jax.sharding import PartitionSpec as P

F32 = jnp.float32
BF16 = jnp.bfloat16
MIB = 1024 * 1024
SHIFT = 8
LOW = (1 << SHIFT) - 1
REFL, TRANS, BACK = 0, 1, 2
FEWER = 3


def split(x):
    hi = x.astype(BF16)
    lo = (x - hi.astype(F32)).astype(BF16)
    return hi, lo


def whole(pair):
    return pair[0].astype(F32) + pair[1].astype(F32)


def expand(h):
    m = h.shape[0]
    return jnp.concatenate([h, jnp.concatenate([-h[:, m:], h[:, :m]], axis=1)], axis=0)


def right(pair):
    return expand(pair[0]), expand(pair[1])


def dot(a, b):
    return jnp.dot(a, b, preferred_element_type=F32)


def deep(left):
    return jnp.concatenate([left[0], left[1], left[0]], axis=1)


def tall(weights):
    return jnp.concatenate([weights[0], weights[0], weights[1]], axis=0)


def mul(left, weights):
    return dot(deep(left), tall(weights))


def get(ref, *at):
    return ref[(*at, 0)], ref[(*at, 1)]


def keep(ref, pair, *at):
    ref[(*at, 0)], ref[(*at, 1)] = pair


def unit(m):
    row = lax.broadcasted_iota(jnp.int32, (m, 2 * m), 0)
    col = lax.broadcasted_iota(jnp.int32, (m, 2 * m), 1)
    return jnp.where(row == col, 1.0, 0.0).astype(F32)


def merge(former, latter):
    r1, t1, b1 = former
    r2, t2, b2 = latter
    m = t1[0].shape[0]
    t1w = tall(right(t1))
    both = dot(deep(b1), jnp.concatenate([tall(right(r2)), tall(right(b2))], axis=1))
    trans = dot(deep(t2), t1w)
    refl = whole(r1) + dot(deep(split(both[:, : 2 * m])), t1w)
    return split(refl), split(trans), split(both[:, 2 * m :])


def triple(ref, *at):
    return tuple(get(ref, *at, kind) for kind in range(3))


def keep_triple(ref, values, *at):
    for kind in range(3):
        keep(ref, values[kind], *at, kind)


def trans_leaf(lib_ref, col_ref, code):
    q, s = code >> SHIFT, code & LOW
    re, im = lib_ref[s, TRANS, 0], lib_ref[s, TRANS, 1]
    cr, ci = col_ref[q, 0], col_ref[q, 1]
    return split(jnp.concatenate([cr * re - ci * im, cr * im + ci * re], axis=1))


def back_leaf(lib_ref, row_ref, code):
    q, s = code >> SHIFT, code & LOW
    re, im = lib_ref[s, BACK, 0], lib_ref[s, BACK, 1]
    rr, ri = row_ref[q, 0][:1], row_ref[q, 1][:1]
    return split(jnp.concatenate([re * rr - im * ri, re * ri + im * rr], axis=1))


def refl_leaf(lib_ref, code):
    s = code & LOW
    return split(jnp.concatenate([lib_ref[s, REFL, 0], lib_ref[s, REFL, 1]], axis=1))


def leaf(lib_ref, row_ref, col_ref, code):
    return (
        refl_leaf(lib_ref, code),
        trans_leaf(lib_ref, col_ref, code),
        back_leaf(lib_ref, row_ref, code),
    )


def table_kernel(code_ref, real_ref, imag_ref, sent_ref, row_ref):
    sent_ref[...] = code_ref[...]
    for part, ref in enumerate((real_ref, imag_ref)):
        profiles, m = ref.shape
        for q in range(profiles):
            row_ref[q, part] = jnp.broadcast_to(ref[q : q + 1], (8, m))


def own_kernel(code_ref, lib_ref, row_ref, nodes_ref, own_ref, col_ref):
    profiles, parts, _, m = row_ref.shape
    for q in range(profiles):
        for part in range(parts):
            col_ref[q, part] = jnp.broadcast_to(row_ref[q, part][:1], (m, m)).T
    cells = code_ref.shape[1]

    def cell(i):
        return leaf(lib_ref, row_ref, col_ref, code_ref[0, i])

    pairs = []
    for j in range(cells // 2):
        pairs.append(merge(cell(2 * j), cell(2 * j + 1)))
        keep_triple(nodes_ref, pairs[j], j)
    fours = []
    for j in range(cells // 4):
        fours.append(merge(pairs[2 * j], pairs[2 * j + 1]))
        keep_triple(nodes_ref, fours[j], cells // 2 + j)
    top = merge(*fours)
    for kind in range(3):
        own_ref[kind] = whole(top[kind])


def scan_kernel(
    code_ref, lib_ref, row_ref, col_ref, nodes_ref, own_ref,
    grown_ref, back_ref, trans_ref,
):
    m = own_ref.shape[1]

    def cell(i):
        return leaf(lib_ref, row_ref, col_ref, code_ref[0, i])

    def store(ref, i, pair):
        ref[0, i], ref[1, i] = pair

    def put(i, values):
        store(trans_ref, i, values[TRANS])
        store(back_ref, i, values[BACK])
        return values

    def grow(i, refl, before):
        store(grown_ref, i, split(whole(before) + mul(refl, right(before))))

    def trans_of(i):
        return trans_leaf(lib_ref, col_ref, code_ref[0, i])

    suffix4 = put(4, triple(nodes_ref, 5))
    before2 = get(nodes_ref, 0, TRANS)
    before4 = get(nodes_ref, 4, TRANS)
    suffix2 = put(2, merge(triple(nodes_ref, 1), suffix4))
    suffix3 = put(3, merge(cell(3), suffix4))
    before3 = split(mul(trans_of(2), right(before2)))
    grow(3, suffix3[REFL], before3)
    grow(2, suffix2[REFL], before2)
    grow(4, suffix4[REFL], before4)
    suffix1 = put(1, merge(cell(1), suffix2))
    before6 = split(mul(get(nodes_ref, 2, TRANS), right(before4)))
    suffix6 = put(6, triple(nodes_ref, 3))
    suffix5 = put(5, merge(cell(5), suffix6))
    grow(6, suffix6[REFL], before6)
    before5 = split(mul(trans_of(4), right(before4)))
    before7 = split(mul(trans_of(6), right(before6)))
    grow(5, suffix5[REFL], before5)
    suffix7 = put(7, cell(7))
    grow(7, suffix7[REFL], before7)
    grow(1, suffix1[REFL], trans_of(0))
    store(grown_ref, 0, split(unit(m) + own_ref[REFL]))
    store(trans_ref, 0, split(own_ref[TRANS]))
    store(back_ref, 0, split(own_ref[BACK]))


def far_core(chip, block, chips):
    if block < 2 * chip:
        return int(block >= chip)
    return int(block >= 2 * chip + 2 + chips - 1 - chip)


def routes(chips):
    blocks = 2 * chips
    wanted = [
        {2 * chip + far_core(chip, block, chips) for chip in range(chips) if chip != block // 2}
        for block in range(blocks)
    ]
    found = []
    for _ in range(chips - 1):
        source = [None] * blocks

        def place(block, seen):
            for device in sorted(wanted[block] - seen):
                seen.add(device)
                if source[device] is None or place(source[device], seen):
                    source[device] = block
                    return True
            return False

        for block in range(blocks):
            place(block, set())
        for device, block in enumerate(source):
            wanted[block].discard(device)
        found.append(source)
    return found


def far_kernel(*refs):
    me_ref, *got_refs = refs[:-9]
    lib_ref, row_ref, col_ref, own_ref, out_ref, code_ref, pairs_ref, fours_ref, acc_ref = refs[-9:]
    blocks, cells = code_ref.shape
    chips = blocks // 2
    m = own_ref.shape[1]
    for ref, source in zip(got_refs, routes(chips)):
        k = source[0]
        for device in range(1, blocks):
            k = jnp.where(me_ref[0] == device, source[device], k)
        for i in range(cells):
            code_ref[k, i] = ref[0, i]
    chip = me_ref[0] >> 1
    core = me_ref[0] & 1
    right_count = chips - 1 - chip
    right_end = 2 * chip + 2 + (core + 1) * right_count
    left_end = (core + 1) * chip
    out_ref[0:3] = own_ref[...]
    eye = split(unit(m))
    none = (jnp.zeros_like(eye[0]), jnp.zeros_like(eye[0]))
    for side in range(2):
        keep_triple(acc_ref, (none, eye, eye), side)

    def place(i):
        on_right = i < right_count
        return jnp.where(on_right, right_end - 1 - i, left_end - 1 - (i - right_count))

    def pair_step(i, _):
        k = place(i)

        def cell(j):
            return leaf(lib_ref, row_ref, col_ref, code_ref[k, j])

        for j in range(cells // 2):
            keep_triple(
                pairs_ref,
                merge(cell(2 * j), cell(2 * j + 1)),
                i,
                j,
            )
        return 0

    if chips <= 4:
        for i in range(chips - 1):
            pair_step(i, 0)
    else:
        lax.fori_loop(0, chips - 1, pair_step, 0)
    for i in range(chips - 1):
        for j in range(cells // 4):
            keep_triple(
                fours_ref, merge(triple(pairs_ref, i, 2 * j), triple(pairs_ref, i, 2 * j + 1)), i, j
            )
    for i in range(chips - 1):
        keep_triple(pairs_ref, merge(triple(fours_ref, i, 0), triple(fours_ref, i, 1)), i, 0)
    for i in range(chips - 1):
        side = jnp.where(i < right_count, 1, 0)
        first = (i == 0) | (i == right_count)

        @pl.when(first)
        def _():
            acc_ref[side] = pairs_ref[i, 0]

        @pl.when(jnp.logical_not(first))
        def _():
            keep_triple(acc_ref, merge(triple(pairs_ref, i, 0), triple(acc_ref, side)), side)

    for side in range(2):
        for kind in range(3):
            out_ref[3 + 3 * side + kind] = whole(get(acc_ref, side, kind))


OWN, LEFT, RIGHT = 0, 3, 6


def sides(me_ref, mine_ref, theirs_ref):
    on_first = (me_ref[0] & 1) == 0

    def first(index):
        return jnp.where(on_first, mine_ref[index], theirs_ref[index])

    def second(index):
        return jnp.where(on_first, theirs_ref[index], mine_ref[index])

    return on_first, first, second


def chain_kernel(me_ref, target_ref, mine_ref, theirs_ref, x_ref, part_ref):
    m = target_ref.shape[1]
    on_first, first, second = sides(me_ref, mine_ref, theirs_ref)
    own0_t = split(first(OWN + TRANS))
    own1_t = split(second(OWN + TRANS))
    own1_tw = right(own1_t)
    far0_tw = right(split(first(RIGHT + TRANS)))
    p_far = mul(split(second(LEFT + TRANS)), right(split(first(LEFT + TRANS))))
    q_far = mul(split(second(RIGHT + TRANS)), far0_tw)
    p_fars, q_fars = split(p_far), split(q_far)
    z = mul(split(first(RIGHT + BACK)), right(split(second(RIGHT + REFL))))
    p_here = mul(own0_t, right(p_fars))
    q_here = mul(q_fars, own1_tw)
    s_far = first(RIGHT + REFL) + mul(split(z), far0_tw)
    total = mul(split(q_here), right(split(p_here)))
    z = mul(split(second(OWN + BACK)), right(split(s_far)))
    miss = jnp.concatenate(
        [(total[:, :m] - target_ref[0]).T, (total[:, m:] - target_ref[1]).T], axis=1
    )
    s_here = second(OWN + REFL) + mul(split(z), own1_tw)
    part_ref[0] = s_here
    part_ref[1] = p_far
    p = split(jnp.where(on_first, p_far, p_here))
    q = split(jnp.where(on_first, q_here, q_far))
    s = split(jnp.where(on_first, s_here, s_far))
    ahead = mul(split(miss), right(q))
    s_block = mul(s, right(split(mine_ref[OWN + TRANS])))
    x1 = right(split(mul(p, right(split(ahead)))))
    x_ref[0, 0], x_ref[0, 1] = x1
    x_ref[1, 0], x_ref[1, 1] = right(split(mul(split(s_block), x1)))


def reflect_kernel(me_ref, mine_ref, theirs_ref, part_ref, out_ref, left_ref):
    rows, m = out_ref.shape[1:]
    _, first, second = sides(me_ref, mine_ref, theirs_ref)
    left_ref[0] = first(LEFT + REFL)
    left_ref[1] = first(LEFT + BACK)
    at = pl.ds(pl.multiple_of(me_ref[0] * rows, rows), rows)
    back = split(left_ref[1, at, :])
    z = mul(split(first(OWN + BACK)), right(split(part_ref[0])))
    refl = first(OWN + REFL) + mul(split(z), right(split(first(OWN + TRANS))))
    z = mul(back, right(split(second(LEFT + REFL))))
    left = left_ref[0, at, :] + mul(split(z), right(split(first(LEFT + TRANS))))
    back = mul(back, right(split(second(LEFT + BACK))))
    z = mul(split(back), right(split(refl)))
    mine = left + mul(split(z), right(split(part_ref[1])))
    out_ref[0] = mine[:, :m]
    out_ref[1] = mine[:, m:]


def coupling_kernel(start, group, x_ref, grown_ref, back_ref, trans_ref, out_ref):
    m = grown_ref.shape[2]
    h = m // 2
    cells = slice(start, start + group)

    def stack(ref):
        return tuple(ref[part, cells].reshape(group * m, 2 * m) for part in range(2))

    row = lax.broadcasted_iota(jnp.int32, (h, m), 0)
    lane = lax.broadcasted_iota(jnp.int32, (h, m), 1)
    use_top = (lane >= h) | (row > lane)
    eye = lax.broadcasted_iota(jnp.int32, (m, m), 0) == lax.broadcasted_iota(jnp.int32, (m, m), 1)
    all_y = mul(stack(grown_ref), (x_ref[0, 0], x_ref[0, 1]))
    all_y = all_y + mul(stack(back_ref), (x_ref[1, 0], x_ref[1, 1]))
    out_ref[group * h :] = jnp.zeros_like(out_ref[group * h :])
    for j in range(group):
        y = all_y[j * m : (j + 1) * m]
        ys = split(jnp.concatenate([y[:, :m], -y[:, m:]], axis=1))
        t = [trans_ref[part, start + j] for part in range(2)]
        c = mul(ys, [jnp.concatenate([a[:, :m], a[:, m:]], axis=0) for a in t])
        both = c + c.T
        low = pltpu.roll(both[h:], h, 1)
        out_ref[j * h : (j + 1) * h] = jnp.where(use_top, both[:h], low)
        out_ref[group * h + j : group * h + j + 1] = jnp.sum(
            jnp.where(eye, c, 0.0), axis=0, keepdims=True
        )


def field_kernel(field_ref, hi_ref, lo_ref):
    for q in range(field_ref.shape[0]):
        hi_ref[q], lo_ref[q] = split(field_ref[q])


def project_kernel(start, group, prof_ref, hi_ref, lo_ref, mine_ref, theirs_ref, *rest):
    out_ref = rest[-1]
    m = hi_ref.shape[1]
    h = m // 2
    if start:
        out_ref[:start] = rest[0][...]
    row = lax.broadcasted_iota(jnp.int32, (h, m), 0)
    lane = lax.broadcasted_iota(jnp.int32, (h, m), 1)
    eye = lax.broadcasted_iota(jnp.int32, (m, m), 0) == lax.broadcasted_iota(jnp.int32, (m, m), 1)
    for j in range(group):
        at = slice(j * h, (j + 1) * h)
        packed = mine_ref[at] + theirs_ref[at]
        at = slice(group * h + j, group * h + j + 1)
        diag = mine_ref[at] + theirs_ref[at]
        top = jnp.where((lane >= h) | (row > lane), packed, 0.0)
        low = pltpu.roll(jnp.where((lane < h) & (row < lane), packed, 0.0), h, 1)
        c = jnp.concatenate([top, low], axis=0) + jnp.where(eye, diag, 0.0)
        ch, cl = split(c)
        q = prof_ref[start + j]
        fh, fl = hi_ref[q], lo_ref[q]
        w = dot(jnp.concatenate([ch, cl], axis=1), jnp.concatenate([fh, fh], axis=0))
        w = w + dot(ch, fl)
        i = start + j
        out_ref[i : i + 1] = jnp.sum(
            (fh.astype(F32) + fl.astype(F32)) * w, axis=0, keepdims=True
        )


def call(kernel, name, kinds, outs, scratch, limit, products, *args):
    def spec(kind):
        return pl.BlockSpec(memory_space=pltpu.SMEM if kind == "s" else pltpu.VMEM)

    several = isinstance(outs, list)
    return pl.pallas_call(
        kernel,
        out_shape=outs,
        in_specs=[spec(kind) for kind in kinds],
        out_specs=[spec("v")] * len(outs) if several else spec("v"),
        scratch_shapes=scratch,
        compiler_params=pltpu.CompilerParams(vmem_limit_bytes=limit * MIB),
        cost_estimate=pl.CostEstimate(
            flops=products * 6 * 8 * 128**3, bytes_accessed=4 * MIB, transcendentals=0
        ),
        name=name,
    )(*args)


def body(interfaces, cell_profile, cell_section, mode_loss, phase, mode_field, target):
    cells = cell_profile.shape[0]
    profiles, m = mode_loss.shape
    blocks = lax.axis_size("cell")
    waves = lax.axis_size("wl")
    pixels = mode_field.shape[2]
    chips = blocks // 2
    angle = phase.reshape(profiles, m)
    factors = (mode_loss * jnp.cos(angle), mode_loss * jnp.sin(angle))
    wanted = target.reshape(2, m, m)
    me = lax.axis_index("cell").astype(jnp.int32).reshape(1)

    def pairs(*lead):
        return (*lead, 2, m, 2 * m)

    def f32(*shape):
        return jax.ShapeDtypeStruct(shape, F32)

    def bf16(*shape):
        return jax.ShapeDtypeStruct(shape, BF16)

    codes = ((cell_profile << SHIFT) | cell_section).reshape(1, cells)
    codes, row_table = call(
        table_kernel, "tables", "vvv",
        [jax.ShapeDtypeStruct((1, cells), jnp.int32), f32(profiles, 2, 8, m)], [], 12, 60,
        codes, *factors,
    )
    got = [
        lax.ppermute(codes, "cell", [(block, device) for device, block in enumerate(source)])
        for source in routes(chips)
    ]
    nodes, own, col_table = call(
        own_kernel, "own_tree", "svv",
        [bf16(*pairs(6, 3)), f32(3, m, 2 * m), f32(profiles, 2, m, m)], [], 12, 28,
        codes, interfaces, row_table,
    )
    mine = call(
        far_kernel, "far_trees", "s" * chips + "vvvv", f32(9, m, 2 * m),
        [
            pltpu.SMEM((blocks, cells), jnp.int32),
            pltpu.VMEM(pairs(chips - 1, cells // 2, 3), BF16),
            pltpu.VMEM(pairs(chips - 1, cells // 4, 3), BF16),
            pltpu.VMEM(pairs(2, 3), BF16),
        ],
        8 + 3 * blocks // 2, 32 * (chips - 1),
        me, *got, interfaces, row_table, col_table, own,
    )
    theirs = lax.ppermute(mine, "cell", [(i, i ^ 1) for i in range(blocks)])
    parts_shape = bf16(2, cells, m, 2 * m)
    grown, back, trans = call(
        scan_kernel, "own_scan", "svvvvv", [parts_shape] * 3, [], 16, 27,
        codes, interfaces, row_table, col_table, nodes, own,
    )
    def packed_shape(group):
        return f32(group * (m // 2) + 8, m)

    more = cells - FEWER
    x, part = call(
        chain_kernel, "chain", "svvv", [bf16(2, 2, 2 * m, 2 * m), f32(2, m, 2 * m)], [], 12, 20,
        me, wanted, mine, theirs,
    )
    groups = [
        call(
            functools.partial(coupling_kernel, start, group), "couplings", "vvvv",
            packed_shape(group), [], 12, 10,
            x, grown, back, trans,
        )
        for start, group in ((0, more), (more, FEWER))
    ]
    reflection = call(
        reflect_kernel, "reflection", "svvv", f32(2, m // blocks, m),
        [pltpu.VMEM((2, m, 2 * m), F32)], 12, 10,
        me, mine, theirs, part,
    )

    steps = []
    bit = 1
    while bit < waves:
        steps.append(bit)
        bit *= 2
    orders = (steps, steps[::-1])

    def exchange(part, number):
        pairs_of = [
            (w * blocks + c, (w ^ orders[c & 1][number]) * blocks + c)
            for w in range(waves)
            for c in range(blocks)
        ]
        return lax.ppermute(part, ("wl", "cell"), pairs_of)

    field = bf16(profiles, m, pixels)
    fields = call(field_kernel, "field_parts", "v", [field, field], [], 12, 1, mode_field)
    gradient = []
    start = 0
    for group, packed in zip((more, FEWER), groups):
        other = jnp.zeros_like(packed)
        for number in range(len(steps)):
            if number:
                packed = packed + other
            other = exchange(packed, number)
        gradient = [
            call(
                functools.partial(project_kernel, start, group), "project",
                "svvvv" + "v" * len(gradient), f32(start + group, pixels), [], 12, 4,
                cell_profile, *fields, packed, other, *gradient,
            )
        ]
        start += group
    return reflection[None], gradient[0]


def solution(mesh):
    in_specs = (
        P(),
        P("cell"),
        P("cell"),
        P(),
        P(None, "wl", None),
        P(None, None, "wl"),
        P("wl", None, None, None),
    )
    out_specs = (P("wl", None, "cell", None), P("cell", "wl"))
    return jax.shard_map(body, mesh=mesh, in_specs=in_specs, out_specs=out_specs, check_vma=False)
```

```python
import functools
import jax
import jax.numpy as jnp
from jax import lax
from jax.experimental import pallas as pl
from jax.experimental.pallas import tpu as pltpu
from jax.sharding import PartitionSpec as P

F32 = jnp.float32
BF16 = jnp.bfloat16
MIB = 1024 * 1024
SHIFT = 8
LOW = (1 << SHIFT) - 1
REFL, TRANS, BACK = 0, 1, 2
FEWER = 3


def split(x):
    hi = x.astype(BF16)
    lo = (x - hi.astype(F32)).astype(BF16)
    return hi, lo


def whole(pair):
    return pair[0].astype(F32) + pair[1].astype(F32)


def expand(h):
    m = h.shape[0]
    return jnp.concatenate([h, jnp.concatenate([-h[:, m:], h[:, :m]], axis=1)], axis=0)


def right(pair):
    return expand(pair[0]), expand(pair[1])


def dot(a, b):
    return jnp.dot(a, b, preferred_element_type=F32)


def deep(left):
    return jnp.concatenate([left[0], left[1], left[0]], axis=1)


def tall(weights):
    return jnp.concatenate([weights[0], weights[0], weights[1]], axis=0)


def mul(left, weights):
    return dot(deep(left), tall(weights))


def get(ref, *at):
    return ref[(*at, 0)], ref[(*at, 1)]


def keep(ref, pair, *at):
    ref[(*at, 0)], ref[(*at, 1)] = pair


def unit(m):
    row = lax.broadcasted_iota(jnp.int32, (m, 2 * m), 0)
    col = lax.broadcasted_iota(jnp.int32, (m, 2 * m), 1)
    return jnp.where(row == col, 1.0, 0.0).astype(F32)


def merge(former, latter):
    r1, t1, b1 = former
    r2, t2, b2 = latter
    m = t1[0].shape[0]
    t1w = tall(right(t1))
    both = dot(deep(b1), jnp.concatenate([tall(right(r2)), tall(right(b2))], axis=1))
    trans = dot(deep(t2), t1w)
    refl = whole(r1) + dot(deep(split(both[:, : 2 * m])), t1w)
    return split(refl), split(trans), split(both[:, 2 * m :])


def triple(ref, *at):
    return tuple(get(ref, *at, kind) for kind in range(3))


def keep_triple(ref, values, *at):
    for kind in range(3):
        keep(ref, values[kind], *at, kind)


def trans_leaf(lib_ref, col_ref, code):
    q, s = code >> SHIFT, code & LOW
    re, im = lib_ref[s, TRANS, 0], lib_ref[s, TRANS, 1]
    cr, ci = col_ref[q, 0], col_ref[q, 1]
    return split(jnp.concatenate([cr * re - ci * im, cr * im + ci * re], axis=1))


def back_leaf(lib_ref, row_ref, code):
    q, s = code >> SHIFT, code & LOW
    re, im = lib_ref[s, BACK, 0], lib_ref[s, BACK, 1]
    rr, ri = row_ref[q, 0][:1], row_ref[q, 1][:1]
    return split(jnp.concatenate([re * rr - im * ri, re * ri + im * rr], axis=1))


def refl_leaf(lib_ref, code):
    s = code & LOW
    return split(jnp.concatenate([lib_ref[s, REFL, 0], lib_ref[s, REFL, 1]], axis=1))


def leaf(lib_ref, row_ref, col_ref, code):
    return (
        refl_leaf(lib_ref, code),
        trans_leaf(lib_ref, col_ref, code),
        back_leaf(lib_ref, row_ref, code),
    )


def pass_kernel(code_ref, sent_ref):
    sent_ref[...] = code_ref[...]


def own_kernel(code_ref, lib_ref, loss_ref, phase_ref, nodes_ref, own_ref, row_ref, col_ref):
    profiles, m = loss_ref.shape
    amp, angle = loss_ref[...], phase_ref[...]
    for part, values in enumerate((amp * jnp.cos(angle), amp * jnp.sin(angle))):
        for q in range(profiles):
            wide = jnp.broadcast_to(values[q : q + 1], (m, m))
            row_ref[q, part] = wide[:8]
            col_ref[q, part] = wide.T
    cells = code_ref.shape[1]

    def cell(i):
        return leaf(lib_ref, row_ref, col_ref, code_ref[0, i])

    pairs = []
    for j in range(cells // 2):
        pairs.append(merge(cell(2 * j), cell(2 * j + 1)))
        keep_triple(nodes_ref, pairs[j], j)
    fours = []
    for j in range(cells // 4):
        fours.append(merge(pairs[2 * j], pairs[2 * j + 1]))
        keep_triple(nodes_ref, fours[j], cells // 2 + j)
    top = merge(*fours)
    for kind in range(3):
        own_ref[kind] = whole(top[kind])


def scan_kernel(
    code_ref, lib_ref, row_ref, col_ref, nodes_ref, own_ref,
    grown_ref, back_ref, trans_ref,
):
    m = own_ref.shape[1]

    def cell(i):
        return leaf(lib_ref, row_ref, col_ref, code_ref[0, i])

    def store(ref, i, pair):
        ref[0, i], ref[1, i] = pair

    def put(i, values):
        store(trans_ref, i, values[TRANS])
        store(back_ref, i, values[BACK])
        return values

    def grow(i, refl, before):
        store(grown_ref, i, split(whole(before) + mul(refl, right(before))))

    def trans_of(i):
        return trans_leaf(lib_ref, col_ref, code_ref[0, i])

    suffix4 = put(4, triple(nodes_ref, 5))
    before2 = get(nodes_ref, 0, TRANS)
    before4 = get(nodes_ref, 4, TRANS)
    suffix2 = put(2, merge(triple(nodes_ref, 1), suffix4))
    suffix3 = put(3, merge(cell(3), suffix4))
    before3 = split(mul(trans_of(2), right(before2)))
    grow(3, suffix3[REFL], before3)
    grow(2, suffix2[REFL], before2)
    grow(4, suffix4[REFL], before4)
    suffix1 = put(1, merge(cell(1), suffix2))
    before6 = split(mul(get(nodes_ref, 2, TRANS), right(before4)))
    suffix6 = put(6, triple(nodes_ref, 3))
    suffix5 = put(5, merge(cell(5), suffix6))
    grow(6, suffix6[REFL], before6)
    before5 = split(mul(trans_of(4), right(before4)))
    before7 = split(mul(trans_of(6), right(before6)))
    grow(5, suffix5[REFL], before5)
    suffix7 = put(7, cell(7))
    grow(7, suffix7[REFL], before7)
    grow(1, suffix1[REFL], trans_of(0))
    store(grown_ref, 0, split(unit(m) + own_ref[REFL]))
    store(trans_ref, 0, split(own_ref[TRANS]))
    store(back_ref, 0, split(own_ref[BACK]))


def far_core(chip, block, chips):
    if block < 2 * chip:
        return int(block >= chip)
    return int(block >= 2 * chip + 2 + chips - 1 - chip)


def routes(chips):
    blocks = 2 * chips
    wanted = [
        {2 * chip + far_core(chip, block, chips) for chip in range(chips) if chip != block // 2}
        for block in range(blocks)
    ]
    found = []
    for _ in range(chips - 1):
        source = [None] * blocks

        def place(block, seen):
            for device in sorted(wanted[block] - seen):
                seen.add(device)
                if source[device] is None or place(source[device], seen):
                    source[device] = block
                    return True
            return False

        for block in range(blocks):
            place(block, set())
        for device, block in enumerate(source):
            wanted[block].discard(device)
        found.append(source)
    return found


def far_kernel(*refs):
    me_ref, *got_refs = refs[:-9]
    lib_ref, row_ref, col_ref, own_ref, out_ref, code_ref, pairs_ref, fours_ref, acc_ref = refs[-9:]
    blocks, cells = code_ref.shape
    chips = blocks // 2
    m = own_ref.shape[1]
    for ref, source in zip(got_refs, routes(chips)):
        k = source[0]
        for device in range(1, blocks):
            k = jnp.where(me_ref[0] == device, source[device], k)
        for i in range(cells):
            code_ref[k, i] = ref[0, i]
    chip = me_ref[0] >> 1
    core = me_ref[0] & 1
    right_count = chips - 1 - chip
    right_end = 2 * chip + 2 + (core + 1) * right_count
    left_end = (core + 1) * chip
    out_ref[0:3] = own_ref[...]
    eye = split(unit(m))
    none = (jnp.zeros_like(eye[0]), jnp.zeros_like(eye[0]))
    for side in range(2):
        keep_triple(acc_ref, (none, eye, eye), side)

    def place(i):
        on_right = i < right_count
        return jnp.where(on_right, right_end - 1 - i, left_end - 1 - (i - right_count))

    def pair_step(i, _):
        k = place(i)

        def cell(j):
            return leaf(lib_ref, row_ref, col_ref, code_ref[k, j])

        for j in range(cells // 2):
            keep_triple(
                pairs_ref,
                merge(cell(2 * j), cell(2 * j + 1)),
                i,
                j,
            )
        return 0

    if chips <= 4:
        for i in range(chips - 1):
            pair_step(i, 0)
    else:
        lax.fori_loop(0, chips - 1, pair_step, 0)
    for i in range(chips - 1):
        for j in range(cells // 4):
            keep_triple(
                fours_ref, merge(triple(pairs_ref, i, 2 * j), triple(pairs_ref, i, 2 * j + 1)), i, j
            )
    for i in range(chips - 1):
        keep_triple(pairs_ref, merge(triple(fours_ref, i, 0), triple(fours_ref, i, 1)), i, 0)
    for i in range(chips - 1):
        side = jnp.where(i < right_count, 1, 0)
        first = (i == 0) | (i == right_count)

        @pl.when(first)
        def _():
            acc_ref[side] = pairs_ref[i, 0]

        @pl.when(jnp.logical_not(first))
        def _():
            keep_triple(acc_ref, merge(triple(pairs_ref, i, 0), triple(acc_ref, side)), side)

    for side in range(2):
        for kind in range(3):
            out_ref[3 + 3 * side + kind] = whole(get(acc_ref, side, kind))


OWN, LEFT, RIGHT = 0, 3, 6


def sides(me_ref, mine_ref, theirs_ref):
    on_first = (me_ref[0] & 1) == 0

    def first(index):
        return jnp.where(on_first, mine_ref[index], theirs_ref[index])

    def second(index):
        return jnp.where(on_first, theirs_ref[index], mine_ref[index])

    return on_first, first, second


def chain_kernel(me_ref, target_ref, mine_ref, theirs_ref, x_ref, part_ref):
    m = target_ref.shape[1]
    on_first, first, second = sides(me_ref, mine_ref, theirs_ref)
    own0_t = split(first(OWN + TRANS))
    own1_t = split(second(OWN + TRANS))
    own1_tw = right(own1_t)
    far0_tw = right(split(first(RIGHT + TRANS)))
    p_far = mul(split(second(LEFT + TRANS)), right(split(first(LEFT + TRANS))))
    q_far = mul(split(second(RIGHT + TRANS)), far0_tw)
    p_fars, q_fars = split(p_far), split(q_far)
    z = mul(split(first(RIGHT + BACK)), right(split(second(RIGHT + REFL))))
    p_here = mul(own0_t, right(p_fars))
    q_here = mul(q_fars, own1_tw)
    s_far = first(RIGHT + REFL) + mul(split(z), far0_tw)
    total = mul(split(q_here), right(split(p_here)))
    z = mul(split(second(OWN + BACK)), right(split(s_far)))
    miss = jnp.concatenate(
        [(total[:, :m] - target_ref[0]).T, (total[:, m:] - target_ref[1]).T], axis=1
    )
    s_here = second(OWN + REFL) + mul(split(z), own1_tw)
    part_ref[0] = s_here
    part_ref[1] = p_far
    p = split(jnp.where(on_first, p_far, p_here))
    q = split(jnp.where(on_first, q_here, q_far))
    s = split(jnp.where(on_first, s_here, s_far))
    ahead = mul(split(miss), right(q))
    s_block = mul(s, right(split(mine_ref[OWN + TRANS])))
    x1 = right(split(mul(p, right(split(ahead)))))
    x_ref[0, 0], x_ref[0, 1] = x1
    x_ref[1, 0], x_ref[1, 1] = right(split(mul(split(s_block), x1)))


def reflect_kernel(me_ref, mine_ref, theirs_ref, part_ref, out_ref, left_ref):
    rows, m = out_ref.shape[1:]
    _, first, second = sides(me_ref, mine_ref, theirs_ref)
    left_ref[0] = first(LEFT + REFL)
    left_ref[1] = first(LEFT + BACK)
    at = pl.ds(pl.multiple_of(me_ref[0] * rows, rows), rows)
    back = split(left_ref[1, at, :])
    z = mul(split(first(OWN + BACK)), right(split(part_ref[0])))
    refl = first(OWN + REFL) + mul(split(z), right(split(first(OWN + TRANS))))
    z = mul(back, right(split(second(LEFT + REFL))))
    left = left_ref[0, at, :] + mul(split(z), right(split(first(LEFT + TRANS))))
    back = mul(back, right(split(second(LEFT + BACK))))
    z = mul(split(back), right(split(refl)))
    mine = left + mul(split(z), right(split(part_ref[1])))
    out_ref[0] = mine[:, :m]
    out_ref[1] = mine[:, m:]


def coupling_kernel(start, group, x_ref, grown_ref, back_ref, trans_ref, out_ref):
    m = grown_ref.shape[2]
    h = m // 2
    cells = slice(start, start + group)

    def stack(ref):
        return tuple(ref[part, cells].reshape(group * m, 2 * m) for part in range(2))

    row = lax.broadcasted_iota(jnp.int32, (h, m), 0)
    lane = lax.broadcasted_iota(jnp.int32, (h, m), 1)
    use_top = (lane >= h) | (row > lane)
    eye = lax.broadcasted_iota(jnp.int32, (m, m), 0) == lax.broadcasted_iota(jnp.int32, (m, m), 1)
    all_y = mul(stack(grown_ref), (x_ref[0, 0], x_ref[0, 1]))
    all_y = all_y + mul(stack(back_ref), (x_ref[1, 0], x_ref[1, 1]))
    out_ref[group * h :] = jnp.zeros_like(out_ref[group * h :])
    for j in range(group):
        y = all_y[j * m : (j + 1) * m]
        ys = split(jnp.concatenate([y[:, :m], -y[:, m:]], axis=1))
        t = [trans_ref[part, start + j] for part in range(2)]
        c = mul(ys, [jnp.concatenate([a[:, :m], a[:, m:]], axis=0) for a in t])
        both = c + c.T
        low = pltpu.roll(both[h:], h, 1)
        out_ref[j * h : (j + 1) * h] = jnp.where(use_top, both[:h], low)
        out_ref[group * h + j : group * h + j + 1] = jnp.sum(
            jnp.where(eye, c, 0.0), axis=0, keepdims=True
        )


def field_kernel(field_ref, hi_ref, lo_ref):
    for q in range(field_ref.shape[0]):
        hi_ref[q], lo_ref[q] = split(field_ref[q])


def project_kernel(start, group, prof_ref, hi_ref, lo_ref, mine_ref, theirs_ref, *rest):
    out_ref = rest[-1]
    m = hi_ref.shape[1]
    h = m // 2
    if start:
        out_ref[:start] = rest[0][...]
    row = lax.broadcasted_iota(jnp.int32, (h, m), 0)
    lane = lax.broadcasted_iota(jnp.int32, (h, m), 1)
    eye = lax.broadcasted_iota(jnp.int32, (m, m), 0) == lax.broadcasted_iota(jnp.int32, (m, m), 1)
    for j in range(group):
        at = slice(j * h, (j + 1) * h)
        packed = mine_ref[at] + theirs_ref[at]
        at = slice(group * h + j, group * h + j + 1)
        diag = mine_ref[at] + theirs_ref[at]
        top = jnp.where((lane >= h) | (row > lane), packed, 0.0)
        low = pltpu.roll(jnp.where((lane < h) & (row < lane), packed, 0.0), h, 1)
        c = jnp.concatenate([top, low], axis=0) + jnp.where(eye, diag, 0.0)
        ch, cl = split(c)
        q = prof_ref[start + j]
        fh, fl = hi_ref[q], lo_ref[q]
        w = dot(jnp.concatenate([ch, cl], axis=1), jnp.concatenate([fh, fh], axis=0))
        w = w + dot(ch, fl)
        i = start + j
        out_ref[i : i + 1] = jnp.sum(
            (fh.astype(F32) + fl.astype(F32)) * w, axis=0, keepdims=True
        )


def call(kernel, name, kinds, outs, scratch, limit, products, *args):
    def spec(kind):
        return pl.BlockSpec(memory_space=pltpu.SMEM if kind == "s" else pltpu.VMEM)

    several = isinstance(outs, list)
    return pl.pallas_call(
        kernel,
        out_shape=outs,
        in_specs=[spec(kind) for kind in kinds],
        out_specs=[spec("v")] * len(outs) if several else spec("v"),
        scratch_shapes=scratch,
        compiler_params=pltpu.CompilerParams(vmem_limit_bytes=limit * MIB),
        cost_estimate=pl.CostEstimate(
            flops=products * 6 * 8 * 128**3, bytes_accessed=4 * MIB, transcendentals=0
        ),
        name=name,
    )(*args)


def body(interfaces, cell_profile, cell_section, mode_loss, phase, mode_field, target):
    cells = cell_profile.shape[0]
    profiles, m = mode_loss.shape
    blocks = lax.axis_size("cell")
    waves = lax.axis_size("wl")
    pixels = mode_field.shape[2]
    chips = blocks // 2
    wanted = target.reshape(2, m, m)
    me = lax.axis_index("cell").astype(jnp.int32).reshape(1)

    def pairs(*lead):
        return (*lead, 2, m, 2 * m)

    def f32(*shape):
        return jax.ShapeDtypeStruct(shape, F32)

    def bf16(*shape):
        return jax.ShapeDtypeStruct(shape, BF16)

    codes = ((cell_profile << SHIFT) | cell_section).reshape(1, cells)
    codes = call(
        pass_kernel, "codes", "v", jax.ShapeDtypeStruct((1, cells), jnp.int32), [], 12, 60, codes
    )
    got = [
        lax.ppermute(codes, "cell", [(block, device) for device, block in enumerate(source)])
        for source in routes(chips)
    ]
    nodes, own, row_table, col_table = call(
        own_kernel, "own_tree", "svvv",
        [
            bf16(*pairs(6, 3)), f32(3, m, 2 * m),
            f32(profiles, 2, 8, m), f32(profiles, 2, m, m),
        ],
        [], 12, 28,
        codes, interfaces, mode_loss, phase.reshape(profiles, m),
    )
    mine = call(
        far_kernel, "far_trees", "s" * chips + "vvvv", f32(9, m, 2 * m),
        [
            pltpu.SMEM((blocks, cells), jnp.int32),
            pltpu.VMEM(pairs(chips - 1, cells // 2, 3), BF16),
            pltpu.VMEM(pairs(chips - 1, cells // 4, 3), BF16),
            pltpu.VMEM(pairs(2, 3), BF16),
        ],
        8 + 3 * blocks // 2, 32 * (chips - 1),
        me, *got, interfaces, row_table, col_table, own,
    )
    theirs = lax.ppermute(mine, "cell", [(i, i ^ 1) for i in range(blocks)])
    parts_shape = bf16(2, cells, m, 2 * m)
    grown, back, trans = call(
        scan_kernel, "own_scan", "svvvvv", [parts_shape] * 3, [], 16, 27,
        codes, interfaces, row_table, col_table, nodes, own,
    )
    def packed_shape(group):
        return f32(group * (m // 2) + 8, m)

    more = cells - FEWER
    x, part = call(
        chain_kernel, "chain", "svvv", [bf16(2, 2, 2 * m, 2 * m), f32(2, m, 2 * m)], [], 12, 20,
        me, wanted, mine, theirs,
    )
    groups = [
        call(
            functools.partial(coupling_kernel, start, group), "couplings", "vvvv",
            packed_shape(group), [], 12, 10,
            x, grown, back, trans,
        )
        for start, group in ((0, more), (more, FEWER))
    ]
    reflection = call(
        reflect_kernel, "reflection", "svvv", f32(2, m // blocks, m),
        [pltpu.VMEM((2, m, 2 * m), F32)], 12, 10,
        me, mine, theirs, part,
    )

    steps = []
    bit = 1
    while bit < waves:
        steps.append(bit)
        bit *= 2
    orders = (steps, steps[::-1])

    def exchange(part, number):
        pairs_of = [
            (w * blocks + c, (w ^ orders[c & 1][number]) * blocks + c)
            for w in range(waves)
            for c in range(blocks)
        ]
        return lax.ppermute(part, ("wl", "cell"), pairs_of)

    field = bf16(profiles, m, pixels)
    fields = call(field_kernel, "field_parts", "v", [field, field], [], 12, 1, mode_field)
    gradient = []
    start = 0
    for group, packed in zip((more, FEWER), groups):
        other = jnp.zeros_like(packed)
        for number in range(len(steps)):
            if number:
                packed = packed + other
            other = exchange(packed, number)
        gradient = [
            call(
                functools.partial(project_kernel, start, group), "project",
                "svvvv" + "v" * len(gradient), f32(start + group, pixels), [], 12, 4,
                cell_profile, *fields, packed, other, *gradient,
            )
        ]
        start += group
    return reflection[None], gradient[0]


def solution(mesh):
    in_specs = (
        P(),
        P("cell"),
        P("cell"),
        P(),
        P(None, "wl", None),
        P(None, None, "wl"),
        P("wl", None, None, None),
    )
    out_specs = (P("wl", None, "cell", None), P("cell", "wl"))
    return jax.shard_map(body, mesh=mesh, in_specs=in_specs, out_specs=out_specs, check_vma=False)
```

```python
import functools
import jax
import jax.numpy as jnp
from jax import lax
from jax.experimental import pallas as pl
from jax.experimental.pallas import tpu as pltpu
from jax.sharding import PartitionSpec as P

F32 = jnp.float32
BF16 = jnp.bfloat16
MIB = 1024 * 1024
SHIFT = 8
LOW = (1 << SHIFT) - 1
REFL, TRANS, BACK = 0, 1, 2
FEWER = 3


def split(x):
    hi = x.astype(BF16)
    lo = (x - hi.astype(F32)).astype(BF16)
    return hi, lo


def whole(pair):
    return pair[0].astype(F32) + pair[1].astype(F32)


def expand(h):
    m = h.shape[0]
    return jnp.concatenate([h, jnp.concatenate([-h[:, m:], h[:, :m]], axis=1)], axis=0)


def right(pair):
    return expand(pair[0]), expand(pair[1])


def dot(a, b):
    return jnp.dot(a, b, preferred_element_type=F32)


def deep(left):
    return jnp.concatenate([left[0], left[1], left[0]], axis=1)


def tall(weights):
    return jnp.concatenate([weights[0], weights[0], weights[1]], axis=0)


def mul(left, weights):
    return dot(deep(left), tall(weights))


def get(ref, *at):
    return ref[(*at, 0)], ref[(*at, 1)]


def keep(ref, pair, *at):
    ref[(*at, 0)], ref[(*at, 1)] = pair


def unit(m):
    row = lax.broadcasted_iota(jnp.int32, (m, 2 * m), 0)
    col = lax.broadcasted_iota(jnp.int32, (m, 2 * m), 1)
    return jnp.where(row == col, 1.0, 0.0).astype(F32)


def merge(former, latter):
    r1, t1, b1 = former
    r2, t2, b2 = latter
    m = t1[0].shape[0]
    t1w = tall(right(t1))
    both = dot(deep(b1), jnp.concatenate([tall(right(r2)), tall(right(b2))], axis=1))
    trans = dot(deep(t2), t1w)
    refl = whole(r1) + dot(deep(split(both[:, : 2 * m])), t1w)
    return split(refl), split(trans), split(both[:, 2 * m :])


def triple(ref, *at):
    return tuple(get(ref, *at, kind) for kind in range(3))


def keep_triple(ref, values, *at):
    for kind in range(3):
        keep(ref, values[kind], *at, kind)


def trans_leaf(lib_ref, col_ref, code):
    q, s = code >> SHIFT, code & LOW
    re, im = lib_ref[s, TRANS, 0], lib_ref[s, TRANS, 1]
    cr, ci = col_ref[q, 0], col_ref[q, 1]
    return split(jnp.concatenate([cr * re - ci * im, cr * im + ci * re], axis=1))


def back_leaf(lib_ref, row_ref, code):
    q, s = code >> SHIFT, code & LOW
    re, im = lib_ref[s, BACK, 0], lib_ref[s, BACK, 1]
    rr, ri = row_ref[q, 0][:1], row_ref[q, 1][:1]
    return split(jnp.concatenate([re * rr - im * ri, re * ri + im * rr], axis=1))


def refl_leaf(lib_ref, code):
    s = code & LOW
    return split(jnp.concatenate([lib_ref[s, REFL, 0], lib_ref[s, REFL, 1]], axis=1))


def leaf(lib_ref, row_ref, col_ref, code):
    return (
        refl_leaf(lib_ref, code),
        trans_leaf(lib_ref, col_ref, code),
        back_leaf(lib_ref, row_ref, code),
    )


def pass_kernel(code_ref, sent_ref):
    sent_ref[...] = code_ref[...]


def own_kernel(code_ref, lib_ref, loss_ref, phase_ref, nodes_ref, own_ref, row_ref, col_ref):
    profiles, m = loss_ref.shape
    amp, angle = loss_ref[...], phase_ref[...]
    for part, values in enumerate((amp * jnp.cos(angle), amp * jnp.sin(angle))):
        for q in range(profiles):
            wide = jnp.broadcast_to(values[q : q + 1], (m, m))
            row_ref[q, part] = wide[:8]
            col_ref[q, part] = wide.T
    cells = code_ref.shape[1]

    def cell(i):
        return leaf(lib_ref, row_ref, col_ref, code_ref[0, i])

    pairs = []
    for j in range(cells // 2):
        pairs.append(merge(cell(2 * j), cell(2 * j + 1)))
        keep_triple(nodes_ref, pairs[j], j)
    fours = []
    for j in range(cells // 4):
        fours.append(merge(pairs[2 * j], pairs[2 * j + 1]))
        keep_triple(nodes_ref, fours[j], cells // 2 + j)
    top = merge(*fours)
    for kind in range(3):
        own_ref[kind] = whole(top[kind])


def scan_kernel(
    code_ref, lib_ref, row_ref, col_ref, nodes_ref, own_ref,
    grown_ref, back_ref, trans_ref,
):
    m = own_ref.shape[1]

    def cell(i):
        return leaf(lib_ref, row_ref, col_ref, code_ref[0, i])

    def store(ref, i, pair):
        ref[0, i], ref[1, i] = pair

    def put(i, values):
        store(trans_ref, i, values[TRANS])
        store(back_ref, i, values[BACK])
        return values

    def grow(i, refl, before):
        store(grown_ref, i, split(whole(before) + mul(refl, right(before))))

    def trans_of(i):
        return trans_leaf(lib_ref, col_ref, code_ref[0, i])

    suffix4 = put(4, triple(nodes_ref, 5))
    before2 = get(nodes_ref, 0, TRANS)
    before4 = get(nodes_ref, 4, TRANS)
    suffix2 = put(2, merge(triple(nodes_ref, 1), suffix4))
    suffix3 = put(3, merge(cell(3), suffix4))
    before3 = split(mul(trans_of(2), right(before2)))
    grow(3, suffix3[REFL], before3)
    grow(2, suffix2[REFL], before2)
    grow(4, suffix4[REFL], before4)
    suffix1 = put(1, merge(cell(1), suffix2))
    before6 = split(mul(get(nodes_ref, 2, TRANS), right(before4)))
    suffix6 = put(6, triple(nodes_ref, 3))
    suffix5 = put(5, merge(cell(5), suffix6))
    grow(6, suffix6[REFL], before6)
    before5 = split(mul(trans_of(4), right(before4)))
    before7 = split(mul(trans_of(6), right(before6)))
    grow(5, suffix5[REFL], before5)
    suffix7 = put(7, cell(7))
    grow(7, suffix7[REFL], before7)
    grow(1, suffix1[REFL], trans_of(0))
    store(grown_ref, 0, split(unit(m) + own_ref[REFL]))
    store(trans_ref, 0, split(own_ref[TRANS]))
    store(back_ref, 0, split(own_ref[BACK]))


def far_core(chip, block, chips):
    if block < 2 * chip:
        return int(block >= chip)
    return int(block >= 2 * chip + 2 + chips - 1 - chip)


def routes(chips):
    blocks = 2 * chips
    wanted = [
        {2 * chip + far_core(chip, block, chips) for chip in range(chips) if chip != block // 2}
        for block in range(blocks)
    ]
    found = []
    for _ in range(chips - 1):
        source = [None] * blocks

        def place(block, seen):
            for device in sorted(wanted[block] - seen):
                seen.add(device)
                if source[device] is None or place(source[device], seen):
                    source[device] = block
                    return True
            return False

        for block in range(blocks):
            place(block, set())
        for device, block in enumerate(source):
            wanted[block].discard(device)
        found.append(source)
    return found


def far_kernel(*refs):
    me_ref, *got_refs = refs[:-9]
    lib_ref, row_ref, col_ref, own_ref, out_ref, code_ref, pairs_ref, fours_ref, acc_ref = refs[-9:]
    blocks, cells = code_ref.shape
    chips = blocks // 2
    m = own_ref.shape[1]
    for ref, source in zip(got_refs, routes(chips)):
        k = source[0]
        for device in range(1, blocks):
            k = jnp.where(me_ref[0] == device, source[device], k)
        for i in range(cells):
            code_ref[k, i] = ref[0, i]
    chip = me_ref[0] >> 1
    core = me_ref[0] & 1
    right_count = chips - 1 - chip
    right_end = 2 * chip + 2 + (core + 1) * right_count
    left_end = (core + 1) * chip
    out_ref[0:3] = own_ref[...]
    eye = split(unit(m))
    none = (jnp.zeros_like(eye[0]), jnp.zeros_like(eye[0]))
    for side in range(2):
        keep_triple(acc_ref, (none, eye, eye), side)

    def place(i):
        on_right = i < right_count
        return jnp.where(on_right, right_end - 1 - i, left_end - 1 - (i - right_count))

    def pair_step(i, _):
        k = place(i)

        def cell(j):
            return leaf(lib_ref, row_ref, col_ref, code_ref[k, j])

        for j in range(cells // 2):
            keep_triple(
                pairs_ref,
                merge(cell(2 * j), cell(2 * j + 1)),
                i,
                j,
            )
        return 0

    if chips <= 4:
        for i in range(chips - 1):
            pair_step(i, 0)
    else:
        lax.fori_loop(0, chips - 1, pair_step, 0)
    for i in range(chips - 1):
        for j in range(cells // 4):
            keep_triple(
                fours_ref, merge(triple(pairs_ref, i, 2 * j), triple(pairs_ref, i, 2 * j + 1)), i, j
            )
    for i in range(chips - 1):
        keep_triple(pairs_ref, merge(triple(fours_ref, i, 0), triple(fours_ref, i, 1)), i, 0)
    for i in range(chips - 1):
        side = jnp.where(i < right_count, 1, 0)
        first = (i == 0) | (i == right_count)

        @pl.when(first)
        def _():
            acc_ref[side] = pairs_ref[i, 0]

        @pl.when(jnp.logical_not(first))
        def _():
            keep_triple(acc_ref, merge(triple(pairs_ref, i, 0), triple(acc_ref, side)), side)

    for side in range(2):
        for kind in range(3):
            out_ref[3 + 3 * side + kind] = whole(get(acc_ref, side, kind))


OWN, LEFT, RIGHT = 0, 3, 6


def sides(me_ref, mine_ref, theirs_ref):
    on_first = (me_ref[0] & 1) == 0

    def first(index):
        return jnp.where(on_first, mine_ref[index], theirs_ref[index])

    def second(index):
        return jnp.where(on_first, theirs_ref[index], mine_ref[index])

    return on_first, first, second


def chain_kernel(me_ref, target_ref, mine_ref, theirs_ref, x_ref, part_ref):
    m = target_ref.shape[1]
    on_first, first, second = sides(me_ref, mine_ref, theirs_ref)
    own0_t = split(first(OWN + TRANS))
    own1_t = split(second(OWN + TRANS))
    own1_tw = right(own1_t)
    far0_tw = right(split(first(RIGHT + TRANS)))
    p_far = mul(split(second(LEFT + TRANS)), right(split(first(LEFT + TRANS))))
    q_far = mul(split(second(RIGHT + TRANS)), far0_tw)
    p_fars, q_fars = split(p_far), split(q_far)
    z = mul(split(first(RIGHT + BACK)), right(split(second(RIGHT + REFL))))
    p_here = mul(own0_t, right(p_fars))
    q_here = mul(q_fars, own1_tw)
    s_far = first(RIGHT + REFL) + mul(split(z), far0_tw)
    total = mul(split(q_here), right(split(p_here)))
    z = mul(split(second(OWN + BACK)), right(split(s_far)))
    miss = jnp.concatenate(
        [(total[:, :m] - target_ref[0]).T, (total[:, m:] - target_ref[1]).T], axis=1
    )
    s_here = second(OWN + REFL) + mul(split(z), own1_tw)
    part_ref[0] = s_here
    part_ref[1] = p_far
    p = split(jnp.where(on_first, p_far, p_here))
    q = split(jnp.where(on_first, q_here, q_far))
    s = split(jnp.where(on_first, s_here, s_far))
    ahead = mul(split(miss), right(q))
    s_block = mul(s, right(split(mine_ref[OWN + TRANS])))
    x1 = right(split(mul(p, right(split(ahead)))))
    x_ref[0, 0], x_ref[0, 1] = x1
    x_ref[1, 0], x_ref[1, 1] = right(split(mul(split(s_block), x1)))


def reflect_kernel(me_ref, mine_ref, theirs_ref, part_ref, out_ref, left_ref):
    rows, m = out_ref.shape[1:]
    _, first, second = sides(me_ref, mine_ref, theirs_ref)
    left_ref[0] = first(LEFT + REFL)
    left_ref[1] = first(LEFT + BACK)
    at = pl.ds(pl.multiple_of(me_ref[0] * rows, rows), rows)
    back = split(left_ref[1, at, :])
    z = mul(split(first(OWN + BACK)), right(split(part_ref[0])))
    refl = first(OWN + REFL) + mul(split(z), right(split(first(OWN + TRANS))))
    z = mul(back, right(split(second(LEFT + REFL))))
    left = left_ref[0, at, :] + mul(split(z), right(split(first(LEFT + TRANS))))
    back = mul(back, right(split(second(LEFT + BACK))))
    z = mul(split(back), right(split(refl)))
    mine = left + mul(split(z), right(split(part_ref[1])))
    out_ref[0] = mine[:, :m]
    out_ref[1] = mine[:, m:]


def coupling_kernel(start, group, x_ref, grown_ref, back_ref, trans_ref, out_ref):
    m = grown_ref.shape[2]
    h = m // 2
    cells = slice(start, start + group)

    def stack(ref):
        return tuple(ref[part, cells].reshape(group * m, 2 * m) for part in range(2))

    row = lax.broadcasted_iota(jnp.int32, (h, m), 0)
    lane = lax.broadcasted_iota(jnp.int32, (h, m), 1)
    use_top = (lane >= h) | (row > lane)
    eye = lax.broadcasted_iota(jnp.int32, (m, m), 0) == lax.broadcasted_iota(jnp.int32, (m, m), 1)
    all_y = mul(stack(grown_ref), (x_ref[0, 0], x_ref[0, 1]))
    all_y = all_y + mul(stack(back_ref), (x_ref[1, 0], x_ref[1, 1]))
    out_ref[group * h :] = jnp.zeros_like(out_ref[group * h :])
    for j in range(group):
        y = all_y[j * m : (j + 1) * m]
        ys = split(jnp.concatenate([y[:, :m], -y[:, m:]], axis=1))
        t = [trans_ref[part, start + j] for part in range(2)]
        c = mul(ys, [jnp.concatenate([a[:, :m], a[:, m:]], axis=0) for a in t])
        both = c + c.T
        low = pltpu.roll(both[h:], h, 1)
        out_ref[j * h : (j + 1) * h] = jnp.where(use_top, both[:h], low)
        out_ref[group * h + j : group * h + j + 1] = jnp.sum(
            jnp.where(eye, c, 0.0), axis=0, keepdims=True
        )


def field_kernel(field_ref, hi_ref, lo_ref):
    for q in range(field_ref.shape[0]):
        hi_ref[q], lo_ref[q] = split(field_ref[q])


def project_kernel(start, group, prof_ref, hi_ref, lo_ref, mine_ref, theirs_ref, *rest):
    out_ref = rest[-1]
    m = hi_ref.shape[1]
    h = m // 2
    if start:
        out_ref[:start] = rest[0][...]
    row = lax.broadcasted_iota(jnp.int32, (h, m), 0)
    lane = lax.broadcasted_iota(jnp.int32, (h, m), 1)
    eye = lax.broadcasted_iota(jnp.int32, (m, m), 0) == lax.broadcasted_iota(jnp.int32, (m, m), 1)
    for j in range(group):
        at = slice(j * h, (j + 1) * h)
        packed = mine_ref[at] + theirs_ref[at]
        at = slice(group * h + j, group * h + j + 1)
        diag = mine_ref[at] + theirs_ref[at]
        top = jnp.where((lane >= h) | (row > lane), packed, 0.0)
        low = pltpu.roll(jnp.where((lane < h) & (row < lane), packed, 0.0), h, 1)
        c = jnp.concatenate([top, low], axis=0) + jnp.where(eye, diag, 0.0)
        ch, cl = split(c)
        q = prof_ref[start + j]
        fh, fl = hi_ref[q], lo_ref[q]
        w = dot(
            jnp.concatenate([ch, cl, ch], axis=1), jnp.concatenate([fh, fh, fl], axis=0)
        )
        i = start + j
        out_ref[i : i + 1] = jnp.sum(
            (fh.astype(F32) + fl.astype(F32)) * w, axis=0, keepdims=True
        )


def call(kernel, name, kinds, outs, scratch, limit, products, *args):
    def spec(kind):
        return pl.BlockSpec(memory_space=pltpu.SMEM if kind == "s" else pltpu.VMEM)

    several = isinstance(outs, list)
    return pl.pallas_call(
        kernel,
        out_shape=outs,
        in_specs=[spec(kind) for kind in kinds],
        out_specs=[spec("v")] * len(outs) if several else spec("v"),
        scratch_shapes=scratch,
        compiler_params=pltpu.CompilerParams(vmem_limit_bytes=limit * MIB),
        cost_estimate=pl.CostEstimate(
            flops=products * 6 * 8 * 128**3, bytes_accessed=4 * MIB, transcendentals=0
        ),
        name=name,
    )(*args)


def body(interfaces, cell_profile, cell_section, mode_loss, phase, mode_field, target):
    cells = cell_profile.shape[0]
    profiles, m = mode_loss.shape
    blocks = lax.axis_size("cell")
    waves = lax.axis_size("wl")
    pixels = mode_field.shape[2]
    chips = blocks // 2
    wanted = target.reshape(2, m, m)
    me = lax.axis_index("cell").astype(jnp.int32).reshape(1)

    def pairs(*lead):
        return (*lead, 2, m, 2 * m)

    def f32(*shape):
        return jax.ShapeDtypeStruct(shape, F32)

    def bf16(*shape):
        return jax.ShapeDtypeStruct(shape, BF16)

    codes = ((cell_profile << SHIFT) | cell_section).reshape(1, cells)
    codes = call(
        pass_kernel, "codes", "v", jax.ShapeDtypeStruct((1, cells), jnp.int32), [], 12, 60, codes
    )
    got = [
        lax.ppermute(codes, "cell", [(block, device) for device, block in enumerate(source)])
        for source in routes(chips)
    ]
    nodes, own, row_table, col_table = call(
        own_kernel, "own_tree", "svvv",
        [
            bf16(*pairs(6, 3)), f32(3, m, 2 * m),
            f32(profiles, 2, 8, m), f32(profiles, 2, m, m),
        ],
        [], 12, 28,
        codes, interfaces, mode_loss, phase.reshape(profiles, m),
    )
    mine = call(
        far_kernel, "far_trees", "s" * chips + "vvvv", f32(9, m, 2 * m),
        [
            pltpu.SMEM((blocks, cells), jnp.int32),
            pltpu.VMEM(pairs(chips - 1, cells // 2, 3), BF16),
            pltpu.VMEM(pairs(chips - 1, cells // 4, 3), BF16),
            pltpu.VMEM(pairs(2, 3), BF16),
        ],
        8 + 3 * blocks // 2, 32 * (chips - 1),
        me, *got, interfaces, row_table, col_table, own,
    )
    theirs = lax.ppermute(mine, "cell", [(i, i ^ 1) for i in range(blocks)])
    parts_shape = bf16(2, cells, m, 2 * m)
    grown, back, trans = call(
        scan_kernel, "own_scan", "svvvvv", [parts_shape] * 3, [], 16, 27,
        codes, interfaces, row_table, col_table, nodes, own,
    )
    def packed_shape(group):
        return f32(group * (m // 2) + 8, m)

    more = cells - FEWER
    x, part = call(
        chain_kernel, "chain", "svvv", [bf16(2, 2, 2 * m, 2 * m), f32(2, m, 2 * m)], [], 12, 20,
        me, wanted, mine, theirs,
    )
    groups = [
        call(
            functools.partial(coupling_kernel, start, group), "couplings", "vvvv",
            packed_shape(group), [], 12, 10,
            x, grown, back, trans,
        )
        for start, group in ((0, more), (more, FEWER))
    ]
    reflection = call(
        reflect_kernel, "reflection", "svvv", f32(2, m // blocks, m),
        [pltpu.VMEM((2, m, 2 * m), F32)], 12, 10,
        me, mine, theirs, part,
    )

    steps = []
    bit = 1
    while bit < waves:
        steps.append(bit)
        bit *= 2
    orders = (steps, steps[::-1])

    def exchange(part, number):
        pairs_of = [
            (w * blocks + c, (w ^ orders[c & 1][number]) * blocks + c)
            for w in range(waves)
            for c in range(blocks)
        ]
        return lax.ppermute(part, ("wl", "cell"), pairs_of)

    field = bf16(profiles, m, pixels)
    fields = call(field_kernel, "field_parts", "v", [field, field], [], 12, 1, mode_field)
    gradient = []
    start = 0
    for group, packed in zip((more, FEWER), groups):
        other = jnp.zeros_like(packed)
        for number in range(len(steps)):
            if number:
                packed = packed + other
            other = exchange(packed, number)
        gradient = [
            call(
                functools.partial(project_kernel, start, group), "project",
                "svvvv" + "v" * len(gradient), f32(start + group, pixels), [], 12, 4,
                cell_profile, *fields, packed, other, *gradient,
            )
        ]
        start += group
    return reflection[None], gradient[0]


def solution(mesh):
    in_specs = (
        P(),
        P("cell"),
        P("cell"),
        P(),
        P(None, "wl", None),
        P(None, None, "wl"),
        P("wl", None, None, None),
    )
    out_specs = (P("wl", None, "cell", None), P("cell", "wl"))
    return jax.shard_map(body, mesh=mesh, in_specs=in_specs, out_specs=out_specs, check_vma=False)
```

```python
import functools
import jax
import jax.numpy as jnp
from jax import lax
from jax.experimental import pallas as pl
from jax.experimental.pallas import tpu as pltpu
from jax.sharding import PartitionSpec as P

F32 = jnp.float32
BF16 = jnp.bfloat16
MIB = 1024 * 1024
SHIFT = 8
LOW = (1 << SHIFT) - 1
REFL, TRANS, BACK = 0, 1, 2
FEWER = 3


def split(x):
    hi = x.astype(BF16)
    lo = (x - hi.astype(F32)).astype(BF16)
    return hi, lo


def whole(pair):
    return pair[0].astype(F32) + pair[1].astype(F32)


def expand(h):
    m = h.shape[0]
    return jnp.concatenate([h, jnp.concatenate([-h[:, m:], h[:, :m]], axis=1)], axis=0)


def right(pair):
    return expand(pair[0]), expand(pair[1])


def dot(a, b):
    return jnp.dot(a, b, preferred_element_type=F32)


def deep(left):
    return jnp.concatenate([left[0], left[1], left[0]], axis=1)


def tall(weights):
    return jnp.concatenate([weights[0], weights[0], weights[1]], axis=0)


def mul(left, weights):
    return dot(deep(left), tall(weights))


def get(ref, *at):
    return ref[(*at, 0)], ref[(*at, 1)]


def keep(ref, pair, *at):
    ref[(*at, 0)], ref[(*at, 1)] = pair


def unit(m):
    row = lax.broadcasted_iota(jnp.int32, (m, 2 * m), 0)
    col = lax.broadcasted_iota(jnp.int32, (m, 2 * m), 1)
    return jnp.where(row == col, 1.0, 0.0).astype(F32)


def merge(former, latter):
    r1, t1, b1 = former
    r2, t2, b2 = latter
    m = t1[0].shape[0]
    t1w = tall(right(t1))
    both = dot(deep(b1), jnp.concatenate([tall(right(r2)), tall(right(b2))], axis=1))
    trans = dot(deep(t2), t1w)
    refl = whole(r1) + dot(deep(split(both[:, : 2 * m])), t1w)
    return split(refl), split(trans), split(both[:, 2 * m :])


def triple(ref, *at):
    return tuple(get(ref, *at, kind) for kind in range(3))


def keep_triple(ref, values, *at):
    for kind in range(3):
        keep(ref, values[kind], *at, kind)


def trans_leaf(lib_ref, col_ref, code):
    q, s = code >> SHIFT, code & LOW
    re, im = lib_ref[s, TRANS, 0], lib_ref[s, TRANS, 1]
    cr, ci = col_ref[q, 0], col_ref[q, 1]
    return split(jnp.concatenate([cr * re - ci * im, cr * im + ci * re], axis=1))


def back_leaf(lib_ref, row_ref, code):
    q, s = code >> SHIFT, code & LOW
    re, im = lib_ref[s, BACK, 0], lib_ref[s, BACK, 1]
    rr, ri = row_ref[q, 0][:1], row_ref[q, 1][:1]
    return split(jnp.concatenate([re * rr - im * ri, re * ri + im * rr], axis=1))


def refl_leaf(lib_ref, code):
    s = code & LOW
    return split(jnp.concatenate([lib_ref[s, REFL, 0], lib_ref[s, REFL, 1]], axis=1))


def leaf(lib_ref, row_ref, col_ref, code):
    return (
        refl_leaf(lib_ref, code),
        trans_leaf(lib_ref, col_ref, code),
        back_leaf(lib_ref, row_ref, code),
    )


def pass_kernel(code_ref, sent_ref):
    sent_ref[...] = code_ref[...]


def own_kernel(code_ref, lib_ref, loss_ref, phase_ref, nodes_ref, own_ref, row_ref, col_ref):
    profiles, m = loss_ref.shape
    amp, angle = loss_ref[...], phase_ref[...]
    for part, values in enumerate((amp * jnp.cos(angle), amp * jnp.sin(angle))):
        for q in range(profiles):
            wide = jnp.broadcast_to(values[q : q + 1], (m, m))
            row_ref[q, part] = wide[:8]
            col_ref[q, part] = wide.T
    cells = code_ref.shape[1]

    def cell(i):
        return leaf(lib_ref, row_ref, col_ref, code_ref[0, i])

    pairs = []
    for j in range(cells // 2):
        pairs.append(merge(cell(2 * j), cell(2 * j + 1)))
        keep_triple(nodes_ref, pairs[j], j)
    fours = []
    for j in range(cells // 4):
        fours.append(merge(pairs[2 * j], pairs[2 * j + 1]))
        keep_triple(nodes_ref, fours[j], cells // 2 + j)
    top = merge(*fours)
    for kind in range(3):
        own_ref[kind] = whole(top[kind])


def scan_kernel(
    code_ref, lib_ref, row_ref, col_ref, nodes_ref, own_ref,
    grown_ref, back_ref, trans_ref,
):
    m = own_ref.shape[1]

    def cell(i):
        return leaf(lib_ref, row_ref, col_ref, code_ref[0, i])

    def store(ref, i, pair):
        ref[0, i], ref[1, i] = pair

    def put(i, values):
        store(trans_ref, i, values[TRANS])
        store(back_ref, i, values[BACK])
        return values

    def grow(i, refl, before):
        store(grown_ref, i, split(whole(before) + mul(refl, right(before))))

    def trans_of(i):
        return trans_leaf(lib_ref, col_ref, code_ref[0, i])

    suffix4 = put(4, triple(nodes_ref, 5))
    before2 = get(nodes_ref, 0, TRANS)
    before4 = get(nodes_ref, 4, TRANS)
    suffix2 = put(2, merge(triple(nodes_ref, 1), suffix4))
    suffix3 = put(3, merge(cell(3), suffix4))
    before3 = split(mul(trans_of(2), right(before2)))
    grow(3, suffix3[REFL], before3)
    grow(2, suffix2[REFL], before2)
    grow(4, suffix4[REFL], before4)
    suffix1 = put(1, merge(cell(1), suffix2))
    before6 = split(mul(get(nodes_ref, 2, TRANS), right(before4)))
    suffix6 = put(6, triple(nodes_ref, 3))
    suffix5 = put(5, merge(cell(5), suffix6))
    grow(6, suffix6[REFL], before6)
    before5 = split(mul(trans_of(4), right(before4)))
    before7 = split(mul(trans_of(6), right(before6)))
    grow(5, suffix5[REFL], before5)
    suffix7 = put(7, cell(7))
    grow(7, suffix7[REFL], before7)
    grow(1, suffix1[REFL], trans_of(0))
    store(grown_ref, 0, split(unit(m) + own_ref[REFL]))
    store(trans_ref, 0, split(own_ref[TRANS]))
    store(back_ref, 0, split(own_ref[BACK]))


def far_core(chip, block, chips):
    if block < 2 * chip:
        return int(block >= chip)
    return int(block >= 2 * chip + 2 + chips - 1 - chip)


def routes(chips):
    blocks = 2 * chips
    wanted = [
        {2 * chip + far_core(chip, block, chips) for chip in range(chips) if chip != block // 2}
        for block in range(blocks)
    ]
    found = []
    for _ in range(chips - 1):
        source = [None] * blocks

        def place(block, seen):
            for device in sorted(wanted[block] - seen):
                seen.add(device)
                if source[device] is None or place(source[device], seen):
                    source[device] = block
                    return True
            return False

        for block in range(blocks):
            place(block, set())
        for device, block in enumerate(source):
            wanted[block].discard(device)
        found.append(source)
    return found[::-1]


def far_kernel(*refs):
    me_ref, *got_refs = refs[:-9]
    lib_ref, row_ref, col_ref, own_ref, out_ref, code_ref, pairs_ref, fours_ref, acc_ref = refs[-9:]
    blocks, cells = code_ref.shape
    chips = blocks // 2
    m = own_ref.shape[1]
    for ref, source in zip(got_refs, routes(chips)):
        k = source[0]
        for device in range(1, blocks):
            k = jnp.where(me_ref[0] == device, source[device], k)
        for i in range(cells):
            code_ref[k, i] = ref[0, i]
    chip = me_ref[0] >> 1
    core = me_ref[0] & 1
    right_count = chips - 1 - chip
    right_end = 2 * chip + 2 + (core + 1) * right_count
    left_end = (core + 1) * chip
    out_ref[0:3] = own_ref[...]
    eye = split(unit(m))
    none = (jnp.zeros_like(eye[0]), jnp.zeros_like(eye[0]))
    for side in range(2):
        keep_triple(acc_ref, (none, eye, eye), side)

    def place(i):
        on_right = i < right_count
        return jnp.where(on_right, right_end - 1 - i, left_end - 1 - (i - right_count))

    def pair_step(i, _):
        k = place(i)

        def cell(j):
            return leaf(lib_ref, row_ref, col_ref, code_ref[k, j])

        for j in range(cells // 2):
            keep_triple(
                pairs_ref,
                merge(cell(2 * j), cell(2 * j + 1)),
                i,
                j,
            )
        return 0

    if chips <= 4:
        for i in range(chips - 1):
            pair_step(i, 0)
    else:
        lax.fori_loop(0, chips - 1, pair_step, 0)
    for i in range(chips - 1):
        for j in range(cells // 4):
            keep_triple(
                fours_ref, merge(triple(pairs_ref, i, 2 * j), triple(pairs_ref, i, 2 * j + 1)), i, j
            )
    for i in range(chips - 1):
        keep_triple(pairs_ref, merge(triple(fours_ref, i, 0), triple(fours_ref, i, 1)), i, 0)
    for i in range(chips - 1):
        side = jnp.where(i < right_count, 1, 0)
        first = (i == 0) | (i == right_count)

        @pl.when(first)
        def _():
            acc_ref[side] = pairs_ref[i, 0]

        @pl.when(jnp.logical_not(first))
        def _():
            keep_triple(acc_ref, merge(triple(pairs_ref, i, 0), triple(acc_ref, side)), side)

    for side in range(2):
        for kind in range(3):
            out_ref[3 + 3 * side + kind] = whole(get(acc_ref, side, kind))


OWN, LEFT, RIGHT = 0, 3, 6


def sides(me_ref, mine_ref, theirs_ref):
    on_first = (me_ref[0] & 1) == 0

    def first(index):
        return jnp.where(on_first, mine_ref[index], theirs_ref[index])

    def second(index):
        return jnp.where(on_first, theirs_ref[index], mine_ref[index])

    return on_first, first, second


def chain_kernel(me_ref, target_ref, mine_ref, theirs_ref, x_ref, part_ref):
    m = target_ref.shape[1]
    on_first, first, second = sides(me_ref, mine_ref, theirs_ref)
    own0_t = split(first(OWN + TRANS))
    own1_t = split(second(OWN + TRANS))
    own1_tw = right(own1_t)
    far0_tw = right(split(first(RIGHT + TRANS)))
    p_far = mul(split(second(LEFT + TRANS)), right(split(first(LEFT + TRANS))))
    q_far = mul(split(second(RIGHT + TRANS)), far0_tw)
    p_fars, q_fars = split(p_far), split(q_far)
    z = mul(split(first(RIGHT + BACK)), right(split(second(RIGHT + REFL))))
    p_here = mul(own0_t, right(p_fars))
    q_here = mul(q_fars, own1_tw)
    s_far = first(RIGHT + REFL) + mul(split(z), far0_tw)
    total = mul(split(q_here), right(split(p_here)))
    z = mul(split(second(OWN + BACK)), right(split(s_far)))
    miss = jnp.concatenate(
        [(total[:, :m] - target_ref[0]).T, (total[:, m:] - target_ref[1]).T], axis=1
    )
    s_here = second(OWN + REFL) + mul(split(z), own1_tw)
    part_ref[0] = s_here
    part_ref[1] = p_far
    p = split(jnp.where(on_first, p_far, p_here))
    q = split(jnp.where(on_first, q_here, q_far))
    s = split(jnp.where(on_first, s_here, s_far))
    ahead = mul(split(miss), right(q))
    s_block = mul(s, right(split(mine_ref[OWN + TRANS])))
    x1 = right(split(mul(p, right(split(ahead)))))
    x_ref[0, 0], x_ref[0, 1] = x1
    x_ref[1, 0], x_ref[1, 1] = right(split(mul(split(s_block), x1)))


def reflect_kernel(me_ref, mine_ref, theirs_ref, part_ref, out_ref, left_ref):
    rows, m = out_ref.shape[1:]
    _, first, second = sides(me_ref, mine_ref, theirs_ref)
    left_ref[0] = first(LEFT + REFL)
    left_ref[1] = first(LEFT + BACK)
    at = pl.ds(pl.multiple_of(me_ref[0] * rows, rows), rows)
    back = split(left_ref[1, at, :])
    z = mul(split(first(OWN + BACK)), right(split(part_ref[0])))
    refl = first(OWN + REFL) + mul(split(z), right(split(first(OWN + TRANS))))
    z = mul(back, right(split(second(LEFT + REFL))))
    left = left_ref[0, at, :] + mul(split(z), right(split(first(LEFT + TRANS))))
    back = mul(back, right(split(second(LEFT + BACK))))
    z = mul(split(back), right(split(refl)))
    mine = left + mul(split(z), right(split(part_ref[1])))
    out_ref[0] = mine[:, :m]
    out_ref[1] = mine[:, m:]


def coupling_kernel(start, group, x_ref, grown_ref, back_ref, trans_ref, out_ref):
    m = grown_ref.shape[2]
    h = m // 2
    cells = slice(start, start + group)

    def stack(ref):
        return tuple(ref[part, cells].reshape(group * m, 2 * m) for part in range(2))

    row = lax.broadcasted_iota(jnp.int32, (h, m), 0)
    lane = lax.broadcasted_iota(jnp.int32, (h, m), 1)
    use_top = (lane >= h) | (row > lane)
    eye = lax.broadcasted_iota(jnp.int32, (m, m), 0) == lax.broadcasted_iota(jnp.int32, (m, m), 1)
    all_y = mul(stack(grown_ref), (x_ref[0, 0], x_ref[0, 1]))
    all_y = all_y + mul(stack(back_ref), (x_ref[1, 0], x_ref[1, 1]))
    out_ref[group * h :] = jnp.zeros_like(out_ref[group * h :])
    for j in range(group):
        y = all_y[j * m : (j + 1) * m]
        ys = split(jnp.concatenate([y[:, :m], -y[:, m:]], axis=1))
        t = [trans_ref[part, start + j] for part in range(2)]
        c = mul(ys, [jnp.concatenate([a[:, :m], a[:, m:]], axis=0) for a in t])
        both = c + c.T
        low = pltpu.roll(both[h:], h, 1)
        out_ref[j * h : (j + 1) * h] = jnp.where(use_top, both[:h], low)
        out_ref[group * h + j : group * h + j + 1] = jnp.sum(
            jnp.where(eye, c, 0.0), axis=0, keepdims=True
        )


def field_kernel(field_ref, hi_ref, lo_ref):
    for q in range(field_ref.shape[0]):
        hi_ref[q], lo_ref[q] = split(field_ref[q])


def project_kernel(start, group, prof_ref, hi_ref, lo_ref, mine_ref, theirs_ref, *rest):
    out_ref = rest[-1]
    m = hi_ref.shape[1]
    h = m // 2
    if start:
        out_ref[:start] = rest[0][...]
    row = lax.broadcasted_iota(jnp.int32, (h, m), 0)
    lane = lax.broadcasted_iota(jnp.int32, (h, m), 1)
    eye = lax.broadcasted_iota(jnp.int32, (m, m), 0) == lax.broadcasted_iota(jnp.int32, (m, m), 1)
    for j in range(group):
        at = slice(j * h, (j + 1) * h)
        packed = mine_ref[at] + theirs_ref[at]
        at = slice(group * h + j, group * h + j + 1)
        diag = mine_ref[at] + theirs_ref[at]
        top = jnp.where((lane >= h) | (row > lane), packed, 0.0)
        low = pltpu.roll(jnp.where((lane < h) & (row < lane), packed, 0.0), h, 1)
        c = jnp.concatenate([top, low], axis=0) + jnp.where(eye, diag, 0.0)
        ch, cl = split(c)
        q = prof_ref[start + j]
        fh, fl = hi_ref[q], lo_ref[q]
        w = dot(jnp.concatenate([ch, cl], axis=1), jnp.concatenate([fh, fh], axis=0))
        w = w + dot(ch, fl)
        i = start + j
        out_ref[i : i + 1] = jnp.sum(
            (fh.astype(F32) + fl.astype(F32)) * w, axis=0, keepdims=True
        )


def call(kernel, name, kinds, outs, scratch, limit, products, *args):
    def spec(kind):
        return pl.BlockSpec(memory_space=pltpu.SMEM if kind == "s" else pltpu.VMEM)

    several = isinstance(outs, list)
    return pl.pallas_call(
        kernel,
        out_shape=outs,
        in_specs=[spec(kind) for kind in kinds],
        out_specs=[spec("v")] * len(outs) if several else spec("v"),
        scratch_shapes=scratch,
        compiler_params=pltpu.CompilerParams(vmem_limit_bytes=limit * MIB),
        cost_estimate=pl.CostEstimate(
            flops=products * 6 * 8 * 128**3, bytes_accessed=4 * MIB, transcendentals=0
        ),
        name=name,
    )(*args)


def body(interfaces, cell_profile, cell_section, mode_loss, phase, mode_field, target):
    cells = cell_profile.shape[0]
    profiles, m = mode_loss.shape
    blocks = lax.axis_size("cell")
    waves = lax.axis_size("wl")
    pixels = mode_field.shape[2]
    chips = blocks // 2
    wanted = target.reshape(2, m, m)
    me = lax.axis_index("cell").astype(jnp.int32).reshape(1)

    def pairs(*lead):
        return (*lead, 2, m, 2 * m)

    def f32(*shape):
        return jax.ShapeDtypeStruct(shape, F32)

    def bf16(*shape):
        return jax.ShapeDtypeStruct(shape, BF16)

    codes = ((cell_profile << SHIFT) | cell_section).reshape(1, cells)
    codes = call(
        pass_kernel, "codes", "v", jax.ShapeDtypeStruct((1, cells), jnp.int32), [], 12, 60, codes
    )
    got = [
        lax.ppermute(codes, "cell", [(block, device) for device, block in enumerate(source)])
        for source in routes(chips)
    ]
    nodes, own, row_table, col_table = call(
        own_kernel, "own_tree", "svvv",
        [
            bf16(*pairs(6, 3)), f32(3, m, 2 * m),
            f32(profiles, 2, 8, m), f32(profiles, 2, m, m),
        ],
        [], 12, 28,
        codes, interfaces, mode_loss, phase.reshape(profiles, m),
    )
    mine = call(
        far_kernel, "far_trees", "s" * chips + "vvvv", f32(9, m, 2 * m),
        [
            pltpu.SMEM((blocks, cells), jnp.int32),
            pltpu.VMEM(pairs(chips - 1, cells // 2, 3), BF16),
            pltpu.VMEM(pairs(chips - 1, cells // 4, 3), BF16),
            pltpu.VMEM(pairs(2, 3), BF16),
        ],
        8 + 3 * blocks // 2, 32 * (chips - 1),
        me, *got, interfaces, row_table, col_table, own,
    )
    theirs = lax.ppermute(mine, "cell", [(i, i ^ 1) for i in range(blocks)])
    parts_shape = bf16(2, cells, m, 2 * m)
    grown, back, trans = call(
        scan_kernel, "own_scan", "svvvvv", [parts_shape] * 3, [], 16, 27,
        codes, interfaces, row_table, col_table, nodes, own,
    )
    def packed_shape(group):
        return f32(group * (m // 2) + 8, m)

    more = cells - FEWER
    x, part = call(
        chain_kernel, "chain", "svvv", [bf16(2, 2, 2 * m, 2 * m), f32(2, m, 2 * m)], [], 12, 20,
        me, wanted, mine, theirs,
    )
    groups = [
        call(
            functools.partial(coupling_kernel, start, group), "couplings", "vvvv",
            packed_shape(group), [], 12, 10,
            x, grown, back, trans,
        )
        for start, group in ((0, more), (more, FEWER))
    ]
    reflection = call(
        reflect_kernel, "reflection", "svvv", f32(2, m // blocks, m),
        [pltpu.VMEM((2, m, 2 * m), F32)], 12, 10,
        me, mine, theirs, part,
    )

    steps = []
    bit = 1
    while bit < waves:
        steps.append(bit)
        bit *= 2
    orders = (steps, steps[::-1])

    def exchange(part, number):
        pairs_of = [
            (w * blocks + c, (w ^ orders[c & 1][number]) * blocks + c)
            for w in range(waves)
            for c in range(blocks)
        ]
        return lax.ppermute(part, ("wl", "cell"), pairs_of)

    field = bf16(profiles, m, pixels)
    fields = call(field_kernel, "field_parts", "v", [field, field], [], 12, 1, mode_field)
    gradient = []
    start = 0
    for group, packed in zip((more, FEWER), groups):
        other = jnp.zeros_like(packed)
        for number in range(len(steps)):
            if number:
                packed = packed + other
            other = exchange(packed, number)
        gradient = [
            call(
                functools.partial(project_kernel, start, group), "project",
                "svvvv" + "v" * len(gradient), f32(start + group, pixels), [], 12, 4,
                cell_profile, *fields, packed, other, *gradient,
            )
        ]
        start += group
    return reflection[None], gradient[0]


def solution(mesh):
    in_specs = (
        P(),
        P("cell"),
        P("cell"),
        P(),
        P(None, "wl", None),
        P(None, None, "wl"),
        P("wl", None, None, None),
    )
    out_specs = (P("wl", None, "cell", None), P("cell", "wl"))
    return jax.shard_map(body, mesh=mesh, in_specs=in_specs, out_specs=out_specs, check_vma=False)
```
